32 devices in a mesh: tile: 16 (over z, y, core), dir: 2 (over x).
Axes of the slice: x: 2, y: 2, z: 4, core: 2. Of those that a mesh axis runs over, the one named last changes fastest.
Arguments:
- coherency: bfloat16 [32, 48, 12, 8, 256], P('tile', 'dir'), may hold values from -0.59765625 to 0.59765625
- observed: bfloat16 [32, 12, 8, 256], P('tile'), may hold values from -12 to 12
- flags: int32 [32, 3], P('tile'), may hold values 0 or 1
- tile_map: int32 [32, 2], P('tile'), may hold values from 0 to 31, as said below
- jones: float32 [48, 8, 512], P('dir', None, 'tile'), may hold values from -6 to 6
Outputs:
- residual: float32 [32, 12, 8, 256], P('tile', None, None, 'dir')
- gradient: float32 [48, 8, 512], P('dir', None, 'tile')
- curvature: float32 [48, 2, 512], P('dir', None, 'tile')
The draws below stay inside these ranges and needn't reach their ends.
Inputs may be any that keep to these rules, and one draw needn't show every extreme that they name: `tile_map`: each row names a station block pair (row block, column block) with row block <= column block; no pair appears twice.
All inputs are finite; a program needn't handle non-finite values. No bound on the sum of `flags` on one device may be relied on, other than what follows from the above.
Results may differ from the reference program's by a relative error of at most 0.00035.
Values sent between devices are 32-bit elements; how exact they have to be, the bound alone decides.
No kernel may reach another device: no remote copies, remote signals or barrier semaphores. Data moves between devices by JAX's collectives and lax.ppermute only.
A program may use at most 64 MiB of HBM per device.

```python
import jax
import jax.numpy as jnp
from jax import lax

STATIONS = 512
K = 48
SB = 16
FREQ_CHANNELS = 4
TIMES = 3
SAMPLES = 12
TILES = 32


def draw_tile_map(key, part):
    key = jax.random.fold_in(key, 11)
    blocks = STATIONS // SB
    pairs = blocks * (blocks + 1) // 2
    order = jax.random.permutation(jax.random.fold_in(key, 1), pairs).astype(jnp.int32)
    target = blocks - 1
    found = jnp.argmax(order == target).astype(jnp.int32)
    place = jax.random.randint(jax.random.fold_in(key, 2), (), 0, TILES).astype(jnp.int32)
    selected_entry = order.at[found].set(order[place]).at[place].set(target)[:TILES]
    indices = jnp.arange(blocks, dtype=jnp.int32)
    starts = indices * blocks - indices * (indices - 1) // 2
    row_block = jnp.sum((selected_entry[:, None] >= starts[None, 1:]).astype(jnp.int32), axis=1)
    col_block = row_block + selected_entry - starts[row_block]
    return jnp.stack([row_block, col_block], axis=1).astype(jnp.int32)


def set_ends(drawn, stream_key, low, largest):
    index_at = [jax.random.randint(jax.random.fold_in(stream_key, axis), (), 0, length) for axis, length in enumerate(drawn.shape)]
    widest = drawn.shape.index(max(drawn.shape))
    neighbour = index_at[:widest] + [(index_at[widest] + 1) % drawn.shape[widest]] + index_at[widest + 1:]
    return drawn.at[tuple(index_at)].set(low).at[tuple(neighbour)].set(largest)


def block_levels(own_key, shape, shards, smallest, largest):
    level = 1.0
    for position, blocks in shards:
        draws = jax.random.uniform(jax.random.fold_in(jax.random.fold_in(own_key, 6), position), (blocks,), jnp.float32, smallest / len(shards), largest / len(shards))
        level = level * jnp.repeat(jnp.exp(draws), shape[position] // blocks).reshape((-1,) + (1,) * (len(shape) - 1 - position))
    return level


def normal_values(own_key, extent, spread, limit, split=(), kind=jnp.bfloat16):
    entries = spread * jax.random.normal(own_key, extent, jnp.float32)
    if split:
        entries = entries * block_levels(own_key, extent, split, -0.22, 0.18)
    return jnp.clip(entries, -limit, limit).astype(kind)


def setup_inputs(seed: int = 0) -> dict:
    splits = jax.random.split(jax.random.key(seed), 6)
    coherency = normal_values(splits[0], (TILES, K, SAMPLES, 8, SB * SB), 0.1, 0.59765625, ((0, 16), (1, 2)))
    observed = normal_values(splits[1], (TILES, SAMPLES, 8, SB * SB), 2.0, 12.0, ((0, 16),))
    flags = set_ends((jax.random.randint(splits[2], (TILES, TIMES), 0, 8) < 1).astype(jnp.int32), jax.random.fold_in(splits[2], 1), 0, 1)
    tile_map = draw_tile_map(jax.random.fold_in(splits[5], 71), 0)
    jones = normal_values(splits[4], (K, 8, STATIONS), 1.0, 6.0, ((0, 2), (2, 16)), jnp.float32)
    return {"coherency": coherency, "observed": observed, "flags": flags, "tile_map": tile_map, "jones": jones}


def split_parts(values):
    shape = values.shape[:-2] + (2, 2, values.shape[-1])
    return values[..., 0:4, :].reshape(shape), values[..., 4:8, :].reshape(shape)


def join_parts(re_part, im_part):
    shape = re_part.shape[:-3] + (4, re_part.shape[-1])
    return jnp.concatenate([re_part.reshape(shape), im_part.reshape(shape)], axis=-2)


def complex_product(left_re, left_im, right_re, right_im):
    lre = left_re[..., :, :, None, :]
    lim = left_im[..., :, :, None, :]
    rre = right_re[..., None, :, :, :]
    rim = right_im[..., None, :, :, :]
    return jnp.sum(lre * rre - lim * rim, axis=-3), jnp.sum(lre * rim + lim * rre, axis=-3)


def adjoint(re_part, im_part):
    return jnp.swapaxes(re_part, -3, -2), -jnp.swapaxes(im_part, -3, -2)


def weights(row_flag_mask, block_pair):
    valid_samples = jnp.repeat((1 - row_flag_mask).astype(jnp.float32), FREQ_CHANNELS)
    baseline = jnp.arange(SB * SB, dtype=jnp.int32)
    inner_row = baseline // SB
    inner_col = baseline % SB
    upper_triangle_pairs = jnp.where((block_pair[0] < block_pair[1]) | (inner_row < inner_col), 1.0, 0.0).astype(jnp.float32)
    return valid_samples[:, None, None] * upper_triangle_pairs[None, None, :]


def tile_terms(coher, jones_all, block_pair):
    row_gain_matrix = lax.dynamic_slice_in_dim(jones_all, (block_pair[0] * SB).astype(jnp.int32), SB, 2)
    col_jones = lax.dynamic_slice_in_dim(jones_all, (block_pair[1] * SB).astype(jnp.int32), SB, 2)
    first_antenna = jnp.repeat(row_gain_matrix, SB, axis=2)[:, None]
    station_q = jnp.tile(col_jones, (1, 1, SB))[:, None]
    coh_re, coh_im = split_parts(coher)
    p_re, p_im = split_parts(first_antenna)
    q_re, q_im = split_parts(station_q)
    qh_re, qh_im = adjoint(q_re, q_im)
    m_re, m_im = complex_product(coh_re, coh_im, qh_re, qh_im)
    n_re, n_im = complex_product(p_re, p_im, coh_re, coh_im)
    v_re, v_im = complex_product(p_re, p_im, m_re, m_im)
    predicted = jnp.sum(join_parts(v_re, v_im), axis=0)
    return predicted, (m_re, m_im, n_re, n_im)


def station_terms(residual, weight, products):
    m_re, m_im, n_re, n_im = products
    r_re, r_im = split_parts(residual)
    mh_re, mh_im = adjoint(m_re, m_im)
    g_re, g_im = complex_product(r_re, r_im, mh_re, mh_im)
    row_side = jnp.sum(join_parts(g_re, g_im), axis=1)
    rh_re, rh_im = adjoint(r_re, r_im)
    f_re, f_im = complex_product(rh_re, rh_im, n_re, n_im)
    col_side = jnp.sum(join_parts(f_re, f_im), axis=1)
    row_curv = jnp.sum(jnp.sum(m_re * m_re + m_im * m_im, axis=-2) * weight[None], axis=1)
    column_curvature = jnp.sum(jnp.sum(n_re * n_re + n_im * n_im, axis=-3) * weight[None], axis=1)
    lead = row_side.shape[0]
    grad_row = jnp.sum(row_side.reshape(lead, 8, SB, SB), axis=3)
    grad_col = jnp.sum(col_side.reshape(lead, 8, SB, SB), axis=2)
    curv_row = jnp.sum(row_curv.reshape(lead, 2, SB, SB), axis=3)
    curv_col = jnp.sum(column_curvature.reshape(lead, 2, SB, SB), axis=2)
    return grad_row, grad_col, curv_row, curv_col


def add_block(total, piece, block):
    offset = (block * SB).astype(jnp.int32)
    current = lax.dynamic_slice_in_dim(total, offset, SB, 2)
    return lax.dynamic_update_slice_in_dim(total, current + piece, offset, 2)


def reference(coherency, observed, flags, tile_map, jones):
    def one_tile(carry, inputs):
        grad_total, curv_total = carry
        coher, seen, row_flag_mask, block_pair = inputs
        predicted, products = tile_terms(coher.astype(jnp.float32), jones, block_pair)
        weight = weights(row_flag_mask, block_pair)
        residual = weight * (seen.astype(jnp.float32) - predicted)
        grad_row, grad_col, curv_row, curv_col = station_terms(residual, weight, products)
        grad_total = add_block(add_block(grad_total, grad_row, block_pair[0]), grad_col, block_pair[1])
        curv_total = add_block(add_block(curv_total, curv_row, block_pair[0]), curv_col, block_pair[1])
        return (grad_total, curv_total), residual

    start = (jnp.zeros((K, 8, STATIONS), jnp.float32), jnp.zeros((K, 2, STATIONS), jnp.float32))
    (grad_total, curv_total), residual = lax.scan(one_tile, start, (coherency, observed, flags, tile_map))
    normalizer = 1.0 / (SAMPLES * SB)
    return residual, grad_total * normalizer, curv_total * normalizer
```

```python
import functools

import jax
import jax.numpy as jnp
from jax import lax
from jax.experimental import pallas as pl
from jax.experimental.pallas import tpu as pltpu
from jax.sharding import PartitionSpec as P

SB = 16
FREQ_CHANNELS = 4
LANES = 128
BASELINES = SB * SB
CHUNK = 3


def split_parts(values):
    shape = values.shape[:-2] + (2, 2, values.shape[-1])
    return (values[..., 0:4, :].reshape(shape), values[..., 4:8, :].reshape(shape))


def join_parts(re_part, im_part):
    shape = re_part.shape[:-3] + (4, re_part.shape[-1])
    return jnp.concatenate([re_part.reshape(shape), im_part.reshape(shape)], axis=-2)


def complex_product(left_re, left_im, right_re, right_im):
    lre = left_re[..., :, :, None, :]
    lim = left_im[..., :, :, None, :]
    rre = right_re[..., None, :, :, :]
    rim = right_im[..., None, :, :, :]
    return (jnp.sum(lre * rre - lim * rim, axis=-3), jnp.sum(lre * rim + lim * rre, axis=-3))


def adjoint(re_part, im_part):
    return (jnp.swapaxes(re_part, -3, -2), -jnp.swapaxes(im_part, -3, -2))


def weights(row_flag_mask, block_pair):
    valid_samples = jnp.repeat((1 - row_flag_mask).astype(jnp.float32), FREQ_CHANNELS)
    baseline = jnp.arange(SB * SB, dtype=jnp.int32)
    inner_row = baseline // SB
    inner_col = baseline % SB
    upper_triangle_pairs = jnp.where(
        (block_pair[0] < block_pair[1]) | (inner_row < inner_col), 1.0, 0.0
    ).astype(jnp.float32)
    return valid_samples[:, None, None] * upper_triangle_pairs[None, None, :]


def tile_terms(coher, jones_all, block_pair):
    row_gain_matrix = lax.dynamic_slice_in_dim(jones_all, block_pair[0] * SB, SB, 2)
    col_jones = lax.dynamic_slice_in_dim(jones_all, block_pair[1] * SB, SB, 2)
    first_antenna = jnp.repeat(row_gain_matrix, SB, axis=2)[:, None]
    station_q = jnp.tile(col_jones, (1, 1, SB))[:, None]
    coh_re, coh_im = split_parts(coher)
    p_re, p_im = split_parts(first_antenna)
    q_re, q_im = split_parts(station_q)
    qh_re, qh_im = adjoint(q_re, q_im)
    m_re, m_im = complex_product(coh_re, coh_im, qh_re, qh_im)
    n_re, n_im = complex_product(p_re, p_im, coh_re, coh_im)
    v_re, v_im = complex_product(p_re, p_im, m_re, m_im)
    predicted = jnp.sum(join_parts(v_re, v_im), axis=0)
    return (predicted, (m_re, m_im, n_re, n_im))


def station_terms(residual, weight, products):
    m_re, m_im, n_re, n_im = products
    r_re, r_im = split_parts(residual)
    mh_re, mh_im = adjoint(m_re, m_im)
    g_re, g_im = complex_product(r_re, r_im, mh_re, mh_im)
    row_side = jnp.sum(join_parts(g_re, g_im), axis=1)
    rh_re, rh_im = adjoint(r_re, r_im)
    f_re, f_im = complex_product(rh_re, rh_im, n_re, n_im)
    col_side = jnp.sum(join_parts(f_re, f_im), axis=1)
    row_curv = jnp.sum(jnp.sum(m_re * m_re + m_im * m_im, axis=-2) * weight[None], axis=1)
    column_curvature = jnp.sum(jnp.sum(n_re * n_re + n_im * n_im, axis=-3) * weight[None], axis=1)
    lead = row_side.shape[0]
    grad_row = jnp.sum(row_side.reshape(lead, 8, SB, SB), axis=3)
    grad_col = jnp.sum(col_side.reshape(lead, 8, SB, SB), axis=2)
    curv_row = jnp.sum(row_curv.reshape(lead, 2, SB, SB), axis=3)
    curv_col = jnp.sum(column_curvature.reshape(lead, 2, SB, SB), axis=2)
    return (grad_row, grad_col, curv_row, curv_col)


def add_block(total, piece, block):
    offset = block * SB
    current = lax.dynamic_slice_in_dim(total, offset, SB, 2)
    return lax.dynamic_update_slice_in_dim(total, current + piece, offset, 2)


def component(value):
    return lax.broadcasted_iota(jnp.int32, value.shape, value.ndim - 2)


def turn(value, ahead):
    return pltpu.roll(value, (8 - ahead) % 8, value.ndim - 2)


def flip(value, mask):
    if mask == 4:
        return turn(value, 4)
    return jnp.where(component(value) & mask == 0, turn(value, mask), turn(value, 8 - mask))


def transpose_matrix(value):
    place = component(value) & 3
    return jnp.where(place == 1, turn(value, 1), jnp.where(place == 2, turn(value, 7), value))


def fold(values):
    values = [values[x] + flip(values[x + 1], 1) for x in range(0, 4, 2)]
    return values[0] + flip(values[1], 2)


def pair_parts(first, second):
    low = component(first) < 4
    return jnp.where(low, first, turn(second, 4)), jnp.where(low, turn(first, 4), second)


def halves(value):
    high = value.astype(jnp.bfloat16)
    return high, (value - high.astype(jnp.float32)).astype(jnp.bfloat16)


def station_of(baseline, row_side):
    return baseline // SB if row_side else baseline % SB


def one_hot(row_side, transposed):
    shape = (BASELINES, LANES) if transposed else (LANES, BASELINES)
    lane = lax.broadcasted_iota(jnp.int32, shape, 1 if transposed else 0)
    baseline = lax.broadcasted_iota(jnp.int32, shape, 0 if transposed else 1)
    return (lane == station_of(baseline, row_side)).astype(jnp.bfloat16)


def expand(blocks, row_side):
    made = []
    for packed in blocks:
        made.extend([packed] + [pltpu.roll(packed, LANES - 2 * SB * g, 1) for g in range(1, 4)])
    high, low = halves(jnp.concatenate(made, axis=0))
    both = jnp.concatenate([high, low], axis=1)
    chosen = jnp.concatenate([one_hot(row_side, False)] * 2, axis=0)
    wide = jnp.dot(both, chosen, preferred_element_type=jnp.float32)
    ends = [0]
    for packed in blocks:
        ends.append(ends[-1] + 4 * packed.shape[0])
    return [wide[start:end] for start, end in zip(ends, ends[1:])]


def station_sums(values, row_side):
    high, low = halves(values)
    both = jnp.concatenate([high, low], axis=0)
    total = jnp.dot(both, one_hot(row_side, True), preferred_element_type=jnp.float32)
    count = high.shape[0]
    return total[:count] + total[count:]


def to_lanes(parts, half):
    moved = [pltpu.roll(part, 2 * SB * g + SB * half, 1) for g, part in enumerate(parts)]
    return sum(moved[1:], moved[0])


def arranged(ref, tile, half, k, mask):
    row = lambda c: ref[tile, half, pl.ds(8 * k + c, 8, stride=0), :]
    first = lax.broadcasted_iota(jnp.int32, (8, LANES), 0) & mask == 0
    pick = lambda c, d: jnp.where(first, row(c), row(d))
    return (pick(0, 3), pick(2, 1)), (pick(4, 7), pick(6, 5))


def half_lanes(index):
    return pl.ds(pl.multiple_of(index * LANES, LANES), LANES)


def upper_mask(meta, tile):
    shape = (8, BASELINES)
    baseline = lax.broadcasted_iota(jnp.int32, shape, 1)
    above = entry(meta, tile, 2, shape) < entry(meta, tile, 3, shape)
    return jnp.where((baseline // SB < baseline % SB) | above, 1.0, 0.0).astype(jnp.float32)


def pack_kernel(jones_in_hbm, slots, jones, packed, in_semaphore, semaphores):
    copy = pltpu.make_async_copy(jones_in_hbm, jones, in_semaphore)
    copy.start()
    copy.wait()
    each = jones.shape[0] // 4
    rows = packed.shape[0]
    packed[...] = jnp.concatenate(
        [jones[g * each : (g + 1) * each].reshape(rows, 2 * SB) for g in range(4)], axis=1
    )
    copies = [
        pltpu.make_async_copy(packed, slots.at[n], semaphores.at[n]) for n in range(slots.shape[0])
    ]
    for copy in copies:
        copy.start()
    for copy in copies:
        copy.wait()


def entry(meta, row, column, shape=(8, LANES)):
    return jnp.broadcast_to(meta[row : row + 1, column : column + 1], shape)


def station_block(meta, near, far, tile, side):
    block = entry(meta, tile, 2 + side)
    owner = block >> 1
    own_core = (owner ^ entry(meta, 0, 0)) & 1 == 0
    chips, rows = near.shape[:2]
    found = None
    for chip in range(chips):
        packed = jnp.where(own_core, near[chip].reshape(-1, 8, LANES), far[chip].reshape(-1, 8, LANES))
        found = packed if found is None else jnp.where(owner >> 1 == chip, packed, found)
    shifted = pltpu.roll(found.reshape(rows, LANES), LANES - SB, 1).reshape(found.shape)
    return jnp.where(block & 1 == 0, found, shifted).reshape(rows, LANES)


PIECES = 6


def block_of(meta, tile, side):
    return meta[tile, 2 + side]


def valid_of(flags, tile, sample):
    return (1 - flags[tile, sample // FREQ_CHANNELS]).astype(jnp.float32)


def sides(meta, tiles):
    return [[block_of(meta, tile, side) for tile in range(tiles)] for side in range(2)]


def pieces(source, target, semaphores):
    each = source.shape[0] // PIECES
    parts = [pl.ds(n * each, each) for n in range(PIECES)]
    return [
        pltpu.make_async_copy(source.at[part], target.at[part], semaphores.at[n])
        for n, part in enumerate(parts)
    ]


def moment_kernel(
    flags_in_hbm, source, moments_out, pairs,
    flags, coherency, moments, semaphores, flag_semaphore, out_semaphores,
):
    tiles, directions, samples = source.shape[:3]
    each = directions // PIECES
    flag_copy = pltpu.make_async_copy(flags_in_hbm, flags, flag_semaphore)
    flag_copy.start()
    copies = [pieces(source.at[t], coherency.at[t], semaphores.at[t]) for t in range(tiles)]
    for copy in sum(copies, []):
        copy.start()
    flag_copy.wait()
    sent = []
    for tile in range(tiles):

        def add_direction(k, _):
            rows = pl.ds(pl.multiple_of(8 * k, 8), 8)
            for half in range(2):
                lanes = slice(half * LANES, (half + 1) * LANES)
                sums = [jnp.zeros((8, LANES), jnp.float32)] * 4
                for s in range(samples):
                    c = coherency[tile, k, s, :, lanes].astype(jnp.float32)
                    weighted = valid_of(flags, tile, s) * c
                    sums = [v + weighted * (turn(c, n) if n else c) for n, v in enumerate(sums)]
                    if s % 2 == 1:
                        both = jnp.concatenate(pair_parts(before, c), axis=0)
                        pairs[tile, k, s // 2, :, lanes] = both.astype(pairs.dtype)
                    before = c
                for n in range(4):
                    moments[tile, n, rows, lanes] = sums[n]
            return 0

        for n, copy in enumerate(copies[tile]):
            copy.wait()
            lax.fori_loop(n * each, (n + 1) * each, add_direction, 0)
            rows = pl.ds(8 * n * each, 8 * each)
            sent.append(
                pltpu.make_async_copy(
                    moments.at[tile, :, rows],
                    moments_out.at[tile, :, rows],
                    out_semaphores.at[tile, n],
                )
            )
            sent[-1].start()
    for copy in sent:
        copy.wait()


def station_products(packed):
    e = packed.reshape(-1, 8, LANES)
    bits = component(e)
    part = bits >= 4
    second = bits & 1 != 0
    spread = lambda v: (lambda u: u + flip(u, 2))(v + flip(v, 4))
    across = flip(e, 1)
    squares = spread(e * e)
    cross_re = 2.0 * spread(e * across)
    sign = jnp.where(part == second, 1.0, -1.0)
    cross_im = 2.0 * spread(sign * (e * flip(across, 4)))
    made = jnp.where(bits & 2 == 0, squares, jnp.where(second, cross_im, cross_re))
    low = component(made[0]) < 4
    joined = [jnp.where(low, made[n], made[n + 1]) for n in range(0, made.shape[0], 2)]
    return jnp.concatenate(joined, axis=0)


def first_model_kernel(meta, near, far, narrow, model, row_jones, col_jones, paired, weight):
    tiles = narrow.shape[0]
    for side, jones in enumerate((row_jones, col_jones)):
        found = [station_block(meta, near, far, tile, side) for tile in range(tiles)]
        for tile, made in enumerate(expand(found, side == 0)):
            jones[tile, 0], jones[tile, 1] = made[:, :LANES], made[:, LANES:]
    models(0, narrow, row_jones, col_jones, model, paired, weight)


def next_model_kernel(tile, narrow, row_jones, col_jones, model, paired, weight):
    models(tile, narrow, row_jones, col_jones, model, paired, weight)


def models(tile, narrow, row_jones, col_jones, model, paired, weight):
    directions, pairs = paired.shape[:2]

    def weigh(k, _):
        for half in range(2):
            lanes = slice(half * LANES, (half + 1) * LANES)
            p_re, p_im = arranged(row_jones, tile, half, k, 2)
            q_re, q_im = arranged(col_jones, tile, half, k, 1)
            for x in range(4):
                a, b = x // 2, x % 2
                z_re = p_re[a] * q_re[b] + p_im[a] * q_im[b]
                z_im = p_im[a] * q_re[b] - p_re[a] * q_im[b]
                weight[k, 3 * x, :, lanes] = z_re
                weight[k, 3 * x + 1, :, lanes] = z_im - z_re
                weight[k, 3 * x + 2, :, lanes] = z_re + z_im
        return 0

    lax.fori_loop(0, directions, weigh, 0, unroll=2)

    def add_samples(step, _):
        lanes = half_lanes(step % 2)
        first = step // 2 * CHUNK
        zero = jnp.zeros((8, LANES), jnp.float32)
        low = component(zero) < 4
        sums = [[zero] * CHUNK for n in range(12)]
        for k in range(directions):
            parts = []
            for i in range(CHUNK):
                both = narrow[tile, k, first + i, :, lanes].astype(jnp.float32)
                real, imag = both[:8], both[8:]
                paired[k, first + i, 0, :, lanes] = real
                paired[k, first + i, 1, :, lanes] = imag
                parts.append((real + imag, real, imag))
            for n in range(12):
                w = weight[k, n, :, lanes]
                sums[n] = [sums[n][i] + w * parts[i][n % 3] for i in range(CHUNK)]
        for i in range(CHUNK):
            one, two, three = ([sums[3 * x + m][i] for x in range(4)] for m in range(3))
            real = fold([one[x] - three[x] for x in range(4)])
            imag = fold([one[x] + two[x] for x in range(4)])
            place = 2 * (first + i)
            model[place, :, lanes] = jnp.where(low, real, turn(imag, 4))
            model[place + 1, :, lanes] = jnp.where(low, turn(real, 4), imag)
        return 0

    lax.fori_loop(0, 2 * pairs // CHUNK, add_samples, 0)


def curvature_kernel(meta, near, far, moments, terms, masks, products):
    tiles = moments.shape[0]
    directions = moments.shape[2] // 8
    for tile in range(tiles):
        masks[tile, 0] = upper_mask(meta, tile)
        for time in range(masks.shape[1] - 1):
            valid = (1 - entry(meta, tile, 4 + time, (8, BASELINES))).astype(jnp.float32)
            masks[tile, 1 + time] = valid * masks[tile, 0]
    for side in range(2):
        found = [station_block(meta, near, far, tile, side) for tile in range(tiles)]
        made = expand([station_products(packed) for packed in found], side == 0)
        for tile in range(tiles):
            for half in range(2):
                products[tile, side, half] = made[tile][:, half * LANES : (half + 1) * LANES]

    def combine(step, _):
        tile, group = step // (directions // 4), step % (directions // 4)
        mask = masks[tile, 0]
        bits = component(mask[:, :LANES])
        odd = bits & 1 != 0
        upper = bits & 2 != 0
        sign = jnp.where(bits < 4, -1.0, 1.0)
        member = (bits >> 2) * 2 + (bits & 1)
        for half in range(2):
            lanes = slice(half * LANES, (half + 1) * LANES)
            found = [None, None]
            for i in range(4):
                k = 4 * group + i
                rows = pl.ds(pl.multiple_of(8 * k, 8), 8)
                m = [moments[tile, n, rows, lanes] for n in range(4)]
                row = lambda side, n: products[tile, side, half, pl.ds(4 * k + n, 8, stride=0), :]
                h = [row(1, n) for n in range(4)]
                row_sum = m[0] * jnp.where(odd, h[1], h[0])
                row_sum = row_sum + jnp.where(odd, sign * (m[3] * h[3]), m[1] * h[2])
                h = [row(0, n) for n in range(4)]
                col_sum = m[0] * jnp.where(upper, h[1], h[0])
                col_sum = col_sum + m[2] * jnp.where(upper, -sign * h[3], h[2])
                row_sum = row_sum + turn(row_sum, 4)
                row_sum = row_sum + flip(row_sum, 1)
                col_sum = transpose_matrix(col_sum)
                col_sum = col_sum + turn(col_sum, 4)
                col_sum = col_sum + flip(col_sum, 1)
                for side, v in enumerate((row_sum, col_sum)):
                    found[side] = v if i == 0 else jnp.where(member == i, v, found[side])
            for side in range(2):
                place = pl.ds(pl.multiple_of(8 * group, 8), 8)
                terms[side, tile, place, lanes] = mask[:, lanes] * found[side]
        return 0

    lax.fori_loop(0, tiles * directions // 4, combine, 0)


def add_to_owner(meta, near, far, block, part):
    owner = block // 2
    own_core = jnp.where(owner % 2 == meta[0, 0] % 2, 1.0, 0.0)
    near[owner // 2] = near[owner // 2] + own_core * part
    far[owner // 2] = far[owner // 2] + (1.0 - own_core) * part


def add_gradient_terms(
    tile, meta, masks, observed, mine, other, row_jones, col_jones, paired,
    residual_out, terms, residual, turned, semaphore,
):
    directions, pairs = paired.shape[:2]
    first_half = entry(meta, 0, 1) == 0
    for i in range(pairs):
        both = []
        for s in (2 * i, 2 * i + 1):
            summed = mine[s] + other[s]
            weight = masks[tile, 1 + s // FREQ_CHANNELS]
            r = weight * (observed[tile, s].astype(jnp.float32) - summed)
            residual[s] = jnp.where(first_half, r[:, :LANES], r[:, LANES:])
            both.append(r)
        made = [pair_parts(*both)]
        for x in range(1, 4):
            bit = x & -x
            made.append(tuple(flip(v, bit) for v in made[x - bit]))
        for x, (real, imag) in enumerate(made):
            turned[i, 3 * x] = real
            turned[i, 3 * x + 1] = real + imag
            turned[i, 3 * x + 2] = real - imag
    sent = pltpu.make_async_copy(residual, residual_out.at[tile], semaphore)
    sent.start()

    def add_directions(step, _):
        half, lanes = step % 2, half_lanes(step % 2)
        first = step // 2 * CHUNK
        zero = jnp.zeros((8, LANES), jnp.float32)
        sums = [[zero] * CHUNK for n in range(12)]
        for p in range(pairs):
            parts = []
            for i in range(CHUNK):
                real = paired[first + i, p, 0, :, lanes]
                imag = paired[first + i, p, 1, :, lanes]
                parts.append((real + imag, real, imag))
            for n in range(12):
                r = turned[p, n, :, lanes]
                sums[n] = [sums[n][i] + r * parts[i][n % 3] for i in range(CHUNK)]
        bits = component(zero)
        real = bits < 4
        equal = (bits >> 1) & 1 == bits & 1
        for i in range(CHUNK):
            k = first + i
            p_re, p_im = arranged(row_jones, tile, half, k, 2)
            q_re, q_im = arranged(col_jones, tile, half, k, 1)
            row_sum = [zero, zero]
            col_sum = [zero, zero]
            for x in range(4):
                a, b = x // 2, x % 2
                y_re = sums[3 * x][i] - sums[3 * x + 2][i]
                y_im = sums[3 * x + 1][i] - sums[3 * x][i]
                y_re = y_re + turn(y_re, 4)
                y_im = y_im + turn(y_im, 4)
                one, two = jnp.where(real, y_re, y_im), jnp.where(real, -y_im, y_re)
                row_sum[a] = row_sum[a] + (q_re[b] * one + q_im[b] * two)
                col_sum[b] = col_sum[b] + (p_re[a] * one - p_im[a] * two)
            rows = pl.ds(pl.multiple_of(8 * k, 8), 8)
            g, h = row_sum
            g = jnp.where(equal, g, h) + flip(jnp.where(equal, h, g), 1)
            terms[0, rows, lanes] = g
            g, h = col_sum
            g = jnp.where(equal, g, h) + flip(jnp.where(equal, h, g), 2)
            terms[1, rows, lanes] = g
        return 0

    lax.fori_loop(0, 2 * directions // CHUNK, add_directions, 0)
    return sent


def first_gradient_kernel(
    meta, masks, observed, mine, other, row_jones, col_jones, paired,
    residual_out, terms, residual, turned, semaphore,
):
    sent = add_gradient_terms(
        0, meta, masks, observed, mine, other, row_jones, col_jones, paired,
        residual_out, terms, residual, turned, semaphore,
    )
    sent.wait()


def last_gradient_kernel(
    tiles, meta_in_vmem, first_terms, curvature_terms,
    masks, observed, mine, other, row_jones, col_jones, paired,
    residual_before, residual_out, near, far, terms, residual, turned, semaphore,
    meta, meta_semaphore,
):
    del residual_before
    meta_copy = pltpu.make_async_copy(meta_in_vmem, meta, meta_semaphore)
    meta_copy.start()
    sent = add_gradient_terms(
        tiles - 1, meta_in_vmem, masks, observed, mine, other, row_jones, col_jones, paired,
        residual_out, terms, residual, turned, semaphore,
    )
    near[...] = jnp.zeros_like(near)
    far[...] = jnp.zeros_like(far)
    meta_copy.wait()
    directions = paired.shape[0]
    rows, few = 8 * directions, 2 * directions
    for side, blocks in enumerate(sides(meta, tiles)):
        stack = [first_terms[side], terms[side]]
        stack.extend(curvature_terms[side, tile] for tile in range(tiles))
        sums = station_sums(jnp.concatenate(stack, axis=0), side == 0)
        for tile, block in enumerate(blocks):
            half = block % 2
            part = to_lanes(jnp.split(sums[tile * rows : (tile + 1) * rows], 4, axis=0), half)
            part = part.reshape(-1, 8, LANES)
            if side == 0:
                part = transpose_matrix(part)
            else:
                part = jnp.where(component(part) < 4, part, -part)
            start = tiles * rows + tile * few
            groups = jnp.split(sums[start : start + few], directions // 4, axis=0)
            chosen = [groups[n : n + 4] for n in range(0, len(groups), 4)]
            made = [part.reshape(-1, LANES), *(to_lanes(parts, half) for parts in chosen)]
            add_to_owner(meta, near, far, block, jnp.concatenate(made, axis=0))
    sent.wait()


def finish_kernel(normalizer, parts, gradient, curvature):
    total = sum((parts[x] for x in range(1, parts.shape[0])), parts[0]) * normalizer
    directions = gradient.shape[0]
    rows, each = 2 * directions, directions // 4
    grad = total[:rows].reshape(each, 8, LANES)
    for g in range(4):
        gradient[g * each : (g + 1) * each] = grad[:, :, 2 * SB * g : 2 * SB * (g + 1)]
    for k in range(directions):
        group, member = k // 4, k % 4
        start = rows + group // 4 * 8 + member // 2 * 4 + member % 2
        lane = group % 4 * 2 * SB
        for c in range(2):
            row = total[start + 2 * c : start + 2 * c + 1]
            curvature[k, c : c + 1] = row[:, lane : lane + 2 * SB]


def call(kernel, scalars, arrays, in_hbm, results, scratch=(), to_hbm=(), aliases=None, cost=None):
    place = lambda space: pl.BlockSpec(memory_space=space)
    spaces = [pltpu.SMEM] * len(scalars) + [pltpu.VMEM] * len(arrays) + [pltpu.HBM] * len(in_hbm)
    return pl.pallas_call(
        kernel,
        in_specs=[place(space) for space in spaces],
        out_specs=[place(pltpu.HBM)] * len(to_hbm) + [place(pltpu.VMEM)] * len(results),
        out_shape=[
            *(pltpu.HBM(shape, jnp.float32) for shape in to_hbm),
            *(pltpu.VMEM(getattr(v, "shape", v), getattr(v, "dtype", jnp.float32)) for v in results),
        ],
        scratch_shapes=list(scratch),
        input_output_aliases=aliases or {},
        cost_estimate=cost,
        compiler_params=pltpu.CompilerParams(vmem_limit_bytes=32 * 1024 * 1024),
    )(*scalars, *arrays, *(pltpu.with_memory_space_constraint(v, pltpu.HBM) for v in in_hbm))


def swap_with(value, axis, mask):
    size = lax.axis_size(axis)
    return lax.ppermute(value, axis, [(place, place ^ mask) for place in range(size)])


def trade(slots):
    size = lax.axis_size("tile")
    groups = [list(range(core, size, 2)) for core in range(2)]
    return lax.all_to_all(slots, "tile", 0, 0, axis_index_groups=groups, tiled=True)


def body_kernels(coherency, observed, flags, tile_map, jones):
    tiles, directions, samples = coherency.shape[:3]
    chips = lax.axis_size("tile") // 2
    rows = 2 * directions
    extra = -(-directions // 16) * 8
    place = [
        jnp.full((tiles, 1), lax.axis_index(axis), jnp.int32) for axis in ("tile", "dir")
    ]
    meta = jnp.concatenate([*place, tile_map, flags], axis=1)

    def memory(*shape, kind=jnp.float32):
        return pltpu.VMEM(shape, kind)

    (packed,) = call(
        pack_kernel,
        [],
        [],
        [jones],
        [],
        [
            memory(*jones.shape),
            memory(rows, LANES),
            pltpu.SemaphoreType.DMA,
            pltpu.SemaphoreType.DMA((chips,)),
        ],
        [(chips, rows, LANES)],
    )
    near = trade(packed)
    narrow = (tiles, directions, samples // 2, 16, BASELINES)
    moments, narrow = call(
        moment_kernel,
        [],
        [],
        [flags, coherency],
        [jax.ShapeDtypeStruct(narrow, coherency.dtype)],
        [
            pltpu.SMEM(flags.shape, flags.dtype),
            memory(*coherency.shape, kind=coherency.dtype),
            memory(tiles, 4, 4 * rows, BASELINES),
            pltpu.SemaphoreType.DMA((tiles, PIECES)),
            pltpu.SemaphoreType.DMA,
            pltpu.SemaphoreType.DMA((tiles, PIECES)),
        ],
        [(tiles, 4, 4 * rows, BASELINES)],
        cost=pl.CostEstimate(
            flops=10 * coherency.size, bytes_accessed=4 * coherency.size, transcendentals=0
        ),
    )
    far = swap_with(near, "tile", 1)

    expanded = (tiles, 2, 4 * rows, LANES)
    of_tile = [(samples, 8, BASELINES), (directions, samples // 2, 2, 8, BASELINES)]
    narrow = pltpu.with_memory_space_constraint(narrow, pltpu.VMEM)
    weight = memory(directions, 12, 8, BASELINES)
    model, row_jones, col_jones, paired = call(
        first_model_kernel,
        [],
        [meta, near, far, narrow],
        [],
        [
            of_tile[0],
            expanded,
            expanded,
            of_tile[1],
        ],
        [weight],
    )
    first = [model, swap_with(model, "dir", 1), row_jones, col_jones, paired]
    model, paired = call(
        functools.partial(next_model_kernel, 1),
        [],
        [narrow, row_jones, col_jones],
        [],
        of_tile,
        [weight],
    )
    last = [model, swap_with(model, "dir", 1), row_jones, col_jones, paired]

    residual_shape = (tiles, samples, 8, LANES)
    terms = (2, 4 * rows, BASELINES)
    scratch = [
        memory(samples, 8, LANES),
        memory(samples // 2, 12, 8, BASELINES),
        pltpu.SemaphoreType.DMA,
    ]
    curvature_terms, masks = call(
        curvature_kernel,
        [],
        [meta, near, far, moments],
        [],
        [(2, tiles, 2 * directions, BASELINES), (tiles, 1 + flags.shape[1], 8, BASELINES)],
        [memory(tiles, 2, 2, 4 * directions, LANES)],
        cost=pl.CostEstimate(
            flops=coherency.size, bytes_accessed=coherency.size, transcendentals=0
        ),
    )
    residual, first_terms = call(
        first_gradient_kernel,
        [],
        [meta, masks, observed, *first],
        [],
        [terms],
        scratch,
        [residual_shape],
    )
    slots = (chips, rows + extra, LANES)
    residual, near, far = call(
        functools.partial(last_gradient_kernel, tiles),
        [],
        [meta, first_terms, curvature_terms, masks, observed, *last],
        [residual],
        [slots, slots],
        [
            memory(*terms),
            *scratch,
            pltpu.SMEM(meta.shape, meta.dtype),
            pltpu.SemaphoreType.DMA,
        ],
        [residual_shape],
        {10: 0},
    )
    parts = trade(near + swap_with(far, "tile", 1))
    directions, _, owned = jones.shape
    in_vmem = pl.BlockSpec(memory_space=pltpu.VMEM)
    gradient, curvature = pl.pallas_call(
        functools.partial(finish_kernel, 1.0 / (samples * SB)),
        in_specs=[in_vmem],
        out_specs=[in_vmem] * 2,
        out_shape=[
            jax.ShapeDtypeStruct(jones.shape, jnp.float32),
            jax.ShapeDtypeStruct((directions, 2, owned), jnp.float32),
        ],
        compiler_params=pltpu.CompilerParams(vmem_limit_bytes=32 * 1024 * 1024),
    )(parts)
    return residual, gradient, curvature


def body(coherency, observed, flags, tile_map, jones):
    jones_all = lax.all_gather(jones, "tile", axis=2, tiled=True)
    how_many = coherency.shape[0]
    predictions = []
    products_list = []
    weight_list = []
    for number in range(how_many):
        predicted, products = tile_terms(
            coherency[number].astype(jnp.float32), jones_all, tile_map[number]
        )
        predictions.append(predicted)
        products_list.append(products)
        weight_list.append(weights(flags[number], tile_map[number]))
    partial_value = jnp.stack(predictions)
    weight = jnp.stack(weight_list)
    columns = observed.shape[3]
    portion = columns // lax.axis_size("dir")
    offset = lax.axis_index("dir") * portion
    summed = lax.psum(partial_value, "dir")
    residual = weight * (observed.astype(jnp.float32) - summed)
    residual_mine = lax.dynamic_slice_in_dim(residual, offset, portion, 3)
    grad_total = jnp.zeros((jones_all.shape[0], 8, jones_all.shape[2]), jnp.float32)
    curv_total = jnp.zeros((jones_all.shape[0], 2, jones_all.shape[2]), jnp.float32)
    for number in range(how_many):
        grad_row, grad_col, curv_row, curv_col = station_terms(
            residual[number], weight[number], products_list[number]
        )
        block_pair = tile_map[number]
        grad_total = add_block(
            add_block(grad_total, grad_row, block_pair[0]), grad_col, block_pair[1]
        )
        curv_total = add_block(
            add_block(curv_total, curv_row, block_pair[0]), curv_col, block_pair[1]
        )
    grad_owned, curv_owned = (
        lax.psum_scatter(grad_total, "tile", scatter_dimension=2, tiled=True),
        lax.psum_scatter(curv_total, "tile", scatter_dimension=2, tiled=True),
    )
    normalizer = 1.0 / (observed.shape[1] * SB)
    return (residual_mine, grad_owned * normalizer, curv_owned * normalizer)


def solution(mesh):
    specs = dict(
        mesh=mesh,
        in_specs=(
            P("tile", "dir", None, None, None),
            P("tile", None, None, None),
            P("tile", None),
            P("tile", None),
            P("dir", None, "tile"),
        ),
        out_specs=(P("tile", None, None, "dir"), P("dir", None, "tile"), P("dir", None, "tile")),
        check_vma=False,
    )

    def run(coherency, observed, flags, tile_map, jones):
        owned = jones.shape[2] // mesh.shape["tile"]
        directions = jones.shape[0] // mesh.shape["dir"]
        fits = owned == 2 * SB and directions % 12 == 0
        paired = mesh.shape["dir"] == 2 and mesh.shape["tile"] == 16
        paired = paired and coherency.shape[0] == 2 * mesh.shape["tile"]
        chosen = body_kernels if fits and paired else body
        return jax.shard_map(chosen, **specs)(coherency, observed, flags, tile_map, jones)

    return run
```

```python
import functools

import jax
import jax.numpy as jnp
from jax import lax
from jax.experimental import pallas as pl
from jax.experimental.pallas import tpu as pltpu
from jax.sharding import PartitionSpec as P

SB = 16
FREQ_CHANNELS = 4
LANES = 128
BASELINES = SB * SB
CHUNK = 3


def split_parts(values):
    shape = values.shape[:-2] + (2, 2, values.shape[-1])
    return (values[..., 0:4, :].reshape(shape), values[..., 4:8, :].reshape(shape))


def join_parts(re_part, im_part):
    shape = re_part.shape[:-3] + (4, re_part.shape[-1])
    return jnp.concatenate([re_part.reshape(shape), im_part.reshape(shape)], axis=-2)


def complex_product(left_re, left_im, right_re, right_im):
    lre = left_re[..., :, :, None, :]
    lim = left_im[..., :, :, None, :]
    rre = right_re[..., None, :, :, :]
    rim = right_im[..., None, :, :, :]
    return (jnp.sum(lre * rre - lim * rim, axis=-3), jnp.sum(lre * rim + lim * rre, axis=-3))


def adjoint(re_part, im_part):
    return (jnp.swapaxes(re_part, -3, -2), -jnp.swapaxes(im_part, -3, -2))


def weights(row_flag_mask, block_pair):
    valid_samples = jnp.repeat((1 - row_flag_mask).astype(jnp.float32), FREQ_CHANNELS)
    baseline = jnp.arange(SB * SB, dtype=jnp.int32)
    inner_row = baseline // SB
    inner_col = baseline % SB
    upper_triangle_pairs = jnp.where(
        (block_pair[0] < block_pair[1]) | (inner_row < inner_col), 1.0, 0.0
    ).astype(jnp.float32)
    return valid_samples[:, None, None] * upper_triangle_pairs[None, None, :]


def tile_terms(coher, jones_all, block_pair):
    row_gain_matrix = lax.dynamic_slice_in_dim(jones_all, block_pair[0] * SB, SB, 2)
    col_jones = lax.dynamic_slice_in_dim(jones_all, block_pair[1] * SB, SB, 2)
    first_antenna = jnp.repeat(row_gain_matrix, SB, axis=2)[:, None]
    station_q = jnp.tile(col_jones, (1, 1, SB))[:, None]
    coh_re, coh_im = split_parts(coher)
    p_re, p_im = split_parts(first_antenna)
    q_re, q_im = split_parts(station_q)
    qh_re, qh_im = adjoint(q_re, q_im)
    m_re, m_im = complex_product(coh_re, coh_im, qh_re, qh_im)
    n_re, n_im = complex_product(p_re, p_im, coh_re, coh_im)
    v_re, v_im = complex_product(p_re, p_im, m_re, m_im)
    predicted = jnp.sum(join_parts(v_re, v_im), axis=0)
    return (predicted, (m_re, m_im, n_re, n_im))


def station_terms(residual, weight, products):
    m_re, m_im, n_re, n_im = products
    r_re, r_im = split_parts(residual)
    mh_re, mh_im = adjoint(m_re, m_im)
    g_re, g_im = complex_product(r_re, r_im, mh_re, mh_im)
    row_side = jnp.sum(join_parts(g_re, g_im), axis=1)
    rh_re, rh_im = adjoint(r_re, r_im)
    f_re, f_im = complex_product(rh_re, rh_im, n_re, n_im)
    col_side = jnp.sum(join_parts(f_re, f_im), axis=1)
    row_curv = jnp.sum(jnp.sum(m_re * m_re + m_im * m_im, axis=-2) * weight[None], axis=1)
    column_curvature = jnp.sum(jnp.sum(n_re * n_re + n_im * n_im, axis=-3) * weight[None], axis=1)
    lead = row_side.shape[0]
    grad_row = jnp.sum(row_side.reshape(lead, 8, SB, SB), axis=3)
    grad_col = jnp.sum(col_side.reshape(lead, 8, SB, SB), axis=2)
    curv_row = jnp.sum(row_curv.reshape(lead, 2, SB, SB), axis=3)
    curv_col = jnp.sum(column_curvature.reshape(lead, 2, SB, SB), axis=2)
    return (grad_row, grad_col, curv_row, curv_col)


def add_block(total, piece, block):
    offset = block * SB
    current = lax.dynamic_slice_in_dim(total, offset, SB, 2)
    return lax.dynamic_update_slice_in_dim(total, current + piece, offset, 2)


def component(value):
    return lax.broadcasted_iota(jnp.int32, value.shape, value.ndim - 2)


def turn(value, ahead):
    return pltpu.roll(value, (8 - ahead) % 8, value.ndim - 2)


def flip(value, mask):
    if mask == 4:
        return turn(value, 4)
    return jnp.where(component(value) & mask == 0, turn(value, mask), turn(value, 8 - mask))


def transpose_matrix(value):
    place = component(value) & 3
    return jnp.where(place == 1, turn(value, 1), jnp.where(place == 2, turn(value, 7), value))


def fold(values):
    values = [values[x] + flip(values[x + 1], 1) for x in range(0, 4, 2)]
    return values[0] + flip(values[1], 2)


def pair_parts(first, second):
    low = component(first) < 4
    return jnp.where(low, first, turn(second, 4)), jnp.where(low, turn(first, 4), second)


def add_all(sums, values):
    if sums is None:
        return values
    return [v if total is None else total + v for total, v in zip(sums, values)]


def halves(value):
    high = value.astype(jnp.bfloat16)
    return high, (value - high.astype(jnp.float32)).astype(jnp.bfloat16)


def station_of(baseline, row_side):
    return baseline // SB if row_side else baseline % SB


def one_hot(row_side, transposed):
    shape = (BASELINES, LANES) if transposed else (LANES, BASELINES)
    lane = lax.broadcasted_iota(jnp.int32, shape, 1 if transposed else 0)
    baseline = lax.broadcasted_iota(jnp.int32, shape, 0 if transposed else 1)
    return (lane == station_of(baseline, row_side)).astype(jnp.bfloat16)


def expand(blocks, row_side):
    made = []
    for packed in blocks:
        made.extend([packed] + [pltpu.roll(packed, LANES - 2 * SB * g, 1) for g in range(1, 4)])
    high, low = halves(jnp.concatenate(made, axis=0))
    both = jnp.concatenate([high, low], axis=1)
    chosen = jnp.concatenate([one_hot(row_side, False)] * 2, axis=0)
    wide = jnp.dot(both, chosen, preferred_element_type=jnp.float32)
    ends = [0]
    for packed in blocks:
        ends.append(ends[-1] + 4 * packed.shape[0])
    return [wide[start:end] for start, end in zip(ends, ends[1:])]


def station_sums(values, row_side):
    high, low = halves(values)
    both = jnp.concatenate([high, low], axis=0)
    total = jnp.dot(both, one_hot(row_side, True), preferred_element_type=jnp.float32)
    count = high.shape[0]
    return total[:count] + total[count:]


def to_lanes(parts):
    return sum((pltpu.roll(part, 2 * SB * g, 1) for g, part in enumerate(parts) if g), parts[0])


def arranged(ref, tile, half, k, mask):
    row = lambda c: ref[tile, half, pl.ds(8 * k + c, 8, stride=0), :]
    first = lax.broadcasted_iota(jnp.int32, (8, LANES), 0) & mask == 0
    pick = lambda c, d: jnp.where(first, row(c), row(d))
    return (pick(0, 3), pick(2, 1)), (pick(4, 7), pick(6, 5))


def half_lanes(index):
    return pl.ds(pl.multiple_of(index * LANES, LANES), LANES)


def upper_mask(meta, tile):
    shape = (8, BASELINES)
    baseline = lax.broadcasted_iota(jnp.int32, shape, 1)
    above = entry(meta, tile, 2, shape) < entry(meta, tile, 3, shape)
    return jnp.where((baseline // SB < baseline % SB) | above, 1.0, 0.0).astype(jnp.float32)


def pack_kernel(jones_in_hbm, packed, jones, semaphore):
    copy = pltpu.make_async_copy(jones_in_hbm, jones, semaphore)
    copy.start()
    copy.wait()
    each = jones.shape[0] // 4
    rows = packed.shape[1]
    made = jnp.concatenate(
        [jones[g * each : (g + 1) * each].reshape(rows, 2 * SB) for g in range(4)], axis=1
    )
    for copy in range(packed.shape[0]):
        packed[copy] = made


def entry(meta, row, column, shape=(8, LANES)):
    return jnp.broadcast_to(meta[row : row + 1, column : column + 1], shape)


def station_block(meta, near, far, tile, side):
    block = entry(meta, tile, 2 + side)
    owner = block >> 1
    own_core = (owner ^ entry(meta, 0, 0)) & 1 == 0
    chips, rows = near.shape[:2]
    found = None
    for chip in range(chips):
        packed = jnp.where(own_core, near[chip].reshape(-1, 8, LANES), far[chip].reshape(-1, 8, LANES))
        found = packed if found is None else jnp.where(owner >> 1 == chip, packed, found)
    shifted = pltpu.roll(found.reshape(rows, LANES), LANES - SB, 1).reshape(found.shape)
    return jnp.where(block & 1 == 0, found, shifted).reshape(rows, LANES)


PIECES = 6
SPARE_ROWS = 8
BLOCK_NUMBERS = 64


def block_of(meta, tile, side):
    return meta[tile, 2 + side]


def valid_of(flags, tile, sample):
    return (1 - flags[tile, sample // FREQ_CHANNELS]).astype(jnp.float32)


def sides(meta, tiles):
    return [[block_of(meta, tile, side) for tile in range(tiles)] for side in range(2)]


def pieces(source, target, semaphores):
    each = source.shape[0] // PIECES
    parts = [pl.ds(n * each, each) for n in range(PIECES)]
    return [
        pltpu.make_async_copy(source.at[part], target.at[part], semaphores.at[n])
        for n, part in enumerate(parts)
    ]


def moment_kernel(
    flags_in_hbm, source, moments_out, pairs,
    flags, coherency, moments, semaphores, flag_semaphore, out_semaphores,
):
    tiles, directions, samples = source.shape[:3]
    each = directions // PIECES
    flag_copy = pltpu.make_async_copy(flags_in_hbm, flags, flag_semaphore)
    flag_copy.start()
    copies = [pieces(source.at[t], coherency.at[t], semaphores.at[t]) for t in range(tiles)]
    for copy in sum(copies, []):
        copy.start()
    flag_copy.wait()
    sent = []
    for tile in range(tiles):

        def add_direction(k, _):
            rows = pl.ds(pl.multiple_of(8 * k, 8), 8)
            for half in range(2):
                lanes = slice(half * LANES, (half + 1) * LANES)
                sums = [jnp.zeros((8, LANES), jnp.float32)] * 4
                for s in range(samples):
                    c = coherency[tile, k, s, :, lanes].astype(jnp.float32)
                    weighted = valid_of(flags, tile, s) * c
                    sums = [v + weighted * (turn(c, n) if n else c) for n, v in enumerate(sums)]
                    if s % 2 == 1:
                        both = jnp.concatenate(pair_parts(before, c), axis=0)
                        pairs[tile, k, s // 2, :, lanes] = both.astype(pairs.dtype)
                    before = c
                for n in range(4):
                    moments[tile, n, rows, lanes] = sums[n]
            return 0

        for n, copy in enumerate(copies[tile]):
            copy.wait()
            lax.fori_loop(n * each, (n + 1) * each, add_direction, 0)
            rows = pl.ds(8 * n * each, 8 * each)
            sent.append(
                pltpu.make_async_copy(
                    moments.at[tile, :, rows],
                    moments_out.at[tile, :, rows],
                    out_semaphores.at[tile, n],
                )
            )
            sent[-1].start()
    for copy in sent:
        copy.wait()


def station_products(packed):
    e = packed.reshape(-1, 8, LANES)
    bits = component(e)
    part = bits >= 4
    second = bits & 1 != 0
    spread = lambda v: (lambda u: u + flip(u, 2))(v + flip(v, 4))
    across = flip(e, 1)
    squares = spread(e * e)
    cross_re = 2.0 * spread(e * across)
    sign = jnp.where(part == second, 1.0, -1.0)
    cross_im = 2.0 * spread(sign * (e * flip(across, 4)))
    made = jnp.where(bits & 2 == 0, squares, jnp.where(second, cross_im, cross_re))
    low = component(made[0]) < 4
    joined = [jnp.where(low, made[n], made[n + 1]) for n in range(0, made.shape[0], 2)]
    return jnp.concatenate(joined, axis=0)


def first_model_kernel(meta, near, far, narrow, model, row_jones, col_jones, paired, weight):
    tiles = narrow.shape[0]
    for side, jones in enumerate((row_jones, col_jones)):
        found = [station_block(meta, near, far, tile, side) for tile in range(tiles)]
        for tile, made in enumerate(expand(found, side == 0)):
            for half in range(2):
                lanes = slice(half * LANES, (half + 1) * LANES)
                jones[tile, half, : made.shape[0]] = made[:, lanes]
    models(0, narrow, row_jones, col_jones, model, paired, weight)


def next_model_kernel(tile, narrow, row_jones, col_jones, model, paired, weight):
    models(tile, narrow, row_jones, col_jones, model, paired, weight)


def models(tile, narrow, row_jones, col_jones, model, paired, weight):
    directions, pairs = paired.shape[:2]

    def weigh(k, _):
        for half in range(2):
            lanes = slice(half * LANES, (half + 1) * LANES)
            p_re, p_im = arranged(row_jones, tile, half, k, 2)
            q_re, q_im = arranged(col_jones, tile, half, k, 1)
            for x in range(4):
                a, b = x // 2, x % 2
                z_re = p_re[a] * q_re[b] + p_im[a] * q_im[b]
                z_im = p_im[a] * q_re[b] - p_re[a] * q_im[b]
                weight[k, 3 * x, :, lanes] = z_re
                weight[k, 3 * x + 1, :, lanes] = z_im - z_re
                weight[k, 3 * x + 2, :, lanes] = z_re + z_im
        return 0

    lax.fori_loop(0, directions, weigh, 0, unroll=2)

    def add_samples(step, _):
        lanes = half_lanes(step % 2)
        first = step // 2 * CHUNK
        zero = jnp.zeros((8, LANES), jnp.float32)
        low = component(zero) < 4
        sums = [None] * 12
        for k in range(directions):
            parts = []
            for i in range(CHUNK):
                both = narrow[tile, k, first + i, :, lanes].astype(jnp.float32)
                real, imag = both[:8], both[8:]
                paired[k, first + i, 0, :, lanes] = real
                paired[k, first + i, 1, :, lanes] = imag
                parts.append((real + imag, real, imag))
            for n in range(12):
                w = weight[k, n, :, lanes]
                sums[n] = add_all(sums[n], [w * parts[i][n % 3] for i in range(CHUNK)])
        for i in range(CHUNK):
            one, two, three = ([sums[3 * x + m][i] for x in range(4)] for m in range(3))
            real = fold([one[x] - three[x] for x in range(4)])
            imag = fold([one[x] + two[x] for x in range(4)])
            place = 2 * (first + i)
            model[place, :, lanes] = jnp.where(low, real, turn(imag, 4))
            model[place + 1, :, lanes] = jnp.where(low, turn(real, 4), imag)
        return 0

    lax.fori_loop(0, 2 * pairs // CHUNK, add_samples, 0)


def curvature_kernel(meta, near, far, moments, terms, masks, products):
    tiles = moments.shape[0]
    directions = moments.shape[2] // 8
    for tile in range(tiles):
        masks[tile, 0] = upper_mask(meta, tile)
        for time in range(masks.shape[1] - 1):
            valid = (1 - entry(meta, tile, 4 + time, (8, BASELINES))).astype(jnp.float32)
            masks[tile, 1 + time] = valid * masks[tile, 0]
    for side in range(2):
        found = [station_block(meta, near, far, tile, side) for tile in range(tiles)]
        made = expand([station_products(packed) for packed in found], side == 0)
        for tile in range(tiles):
            for half in range(2):
                lanes = slice(half * LANES, (half + 1) * LANES)
                products[tile, side, half, : made[tile].shape[0]] = made[tile][:, lanes]

    def combine(step, _):
        tile, group = step // (directions // 4), step % (directions // 4)
        mask = masks[tile, 0]
        bits = component(mask[:, :LANES])
        odd = bits & 1 != 0
        upper = bits & 2 != 0
        sign = jnp.where(bits < 4, -1.0, 1.0)
        member = (bits >> 2) * 2 + (bits & 1)
        for half in range(2):
            lanes = slice(half * LANES, (half + 1) * LANES)
            found = [None, None]
            for i in range(4):
                k = 4 * group + i
                rows = pl.ds(pl.multiple_of(8 * k, 8), 8)
                m = [moments[tile, n, rows, lanes] for n in range(4)]
                row = lambda side, n: products[tile, side, half, pl.ds(4 * k + n, 8, stride=0), :]
                h = [row(1, n) for n in range(4)]
                row_sum = m[0] * jnp.where(odd, h[1], h[0])
                row_sum = row_sum + jnp.where(odd, sign * (m[3] * h[3]), m[1] * h[2])
                h = [row(0, n) for n in range(4)]
                col_sum = m[0] * jnp.where(upper, h[1], h[0])
                col_sum = col_sum + m[2] * jnp.where(upper, -sign * h[3], h[2])
                row_sum = row_sum + turn(row_sum, 4)
                row_sum = row_sum + flip(row_sum, 1)
                col_sum = transpose_matrix(col_sum)
                col_sum = col_sum + turn(col_sum, 4)
                col_sum = col_sum + flip(col_sum, 1)
                for side, v in enumerate((row_sum, col_sum)):
                    found[side] = v if i == 0 else jnp.where(member == i, v, found[side])
            for side in range(2):
                place = pl.ds(pl.multiple_of(8 * group, 8), 8)
                terms[side, tile, place, lanes] = mask[:, lanes] * found[side]
        return 0

    lax.fori_loop(0, tiles * directions // 4, combine, 0)


def add_to_owner(meta, near, block, part):
    owner = block // 2
    own_core = jnp.where(owner % 2 == meta[0, 0] % 2, 1.0, 0.0)
    near[owner // 2] = near[owner // 2] + own_core * pltpu.roll(part, SB * (block % 2), 1)


def add_gradient_terms(
    tile, meta, masks, observed, mine, other, row_jones, col_jones, paired,
    residual_out, terms, residual, turned, semaphore,
):
    directions, pairs = paired.shape[:2]
    first_half = entry(meta, 0, 1) == 0
    for i in range(pairs):
        both = []
        for s in (2 * i, 2 * i + 1):
            summed = mine[s] + other[s]
            weight = masks[tile, 1 + s // FREQ_CHANNELS]
            r = weight * (observed[tile, s].astype(jnp.float32) - summed)
            residual[s] = jnp.where(first_half, r[:, :LANES], r[:, LANES:])
            both.append(r)
        made = [pair_parts(*both)]
        for x in range(1, 4):
            bit = x & -x
            made.append(tuple(flip(v, bit) for v in made[x - bit]))
        for x, (real, imag) in enumerate(made):
            turned[i, 3 * x] = real
            turned[i, 3 * x + 1] = real + imag
            turned[i, 3 * x + 2] = real - imag
    sent = pltpu.make_async_copy(residual, residual_out.at[tile], semaphore)
    sent.start()

    def add_directions(step, _):
        half, lanes = step % 2, half_lanes(step % 2)
        first = step // 2 * CHUNK
        zero = jnp.zeros((8, LANES), jnp.float32)
        sums = [None] * 12
        for p in range(pairs):
            parts = []
            for i in range(CHUNK):
                real = paired[first + i, p, 0, :, lanes]
                imag = paired[first + i, p, 1, :, lanes]
                parts.append((real + imag, real, imag))
            for n in range(12):
                r = turned[p, n, :, lanes]
                sums[n] = add_all(sums[n], [r * parts[i][n % 3] for i in range(CHUNK)])
        bits = component(zero)
        real = bits < 4
        equal = (bits >> 1) & 1 == bits & 1
        for i in range(CHUNK):
            k = first + i
            p_re, p_im = arranged(row_jones, tile, half, k, 2)
            q_re, q_im = arranged(col_jones, tile, half, k, 1)
            row_sum = [None, None]
            col_sum = [None, None]
            for x in range(4):
                a, b = x // 2, x % 2
                y_re = sums[3 * x][i] - sums[3 * x + 2][i]
                y_im = sums[3 * x + 1][i] - sums[3 * x][i]
                y_re = y_re + turn(y_re, 4)
                y_im = y_im + turn(y_im, 4)
                one, two = jnp.where(real, y_re, y_im), jnp.where(real, -y_im, y_re)
                (row_sum[a],) = add_all(row_sum[a : a + 1], [q_re[b] * one + q_im[b] * two])
                (col_sum[b],) = add_all(col_sum[b : b + 1], [p_re[a] * one - p_im[a] * two])
            rows = pl.ds(pl.multiple_of(8 * k, 8), 8)
            g, h = row_sum
            g = jnp.where(equal, g, h) + flip(jnp.where(equal, h, g), 1)
            terms[0, rows, lanes] = g
            g, h = col_sum
            g = jnp.where(equal, g, h) + flip(jnp.where(equal, h, g), 2)
            terms[1, rows, lanes] = g
        return 0

    lax.fori_loop(0, 2 * directions // CHUNK, add_directions, 0)
    return sent


def first_gradient_kernel(
    meta, masks, observed, mine, other, row_jones, col_jones, paired,
    residual_out, terms, residual, turned, semaphore,
):
    sent = add_gradient_terms(
        0, meta, masks, observed, mine, other, row_jones, col_jones, paired,
        residual_out, terms, residual, turned, semaphore,
    )
    sent.wait()


def last_gradient_kernel(
    tiles, meta_in_vmem, first_terms, curvature_terms,
    masks, observed, mine, other, row_jones, col_jones, paired,
    residual_before, residual_out, near, compact, terms, residual, turned, semaphore,
    meta, meta_semaphore,
):
    del residual_before
    meta_copy = pltpu.make_async_copy(meta_in_vmem, meta, meta_semaphore)
    meta_copy.start()
    sent = add_gradient_terms(
        tiles - 1, meta_in_vmem, masks, observed, mine, other, row_jones, col_jones, paired,
        residual_out, terms, residual, turned, semaphore,
    )
    near[...] = jnp.zeros_like(near)
    meta_copy.wait()
    directions = paired.shape[0]
    rows, few = 8 * directions, 2 * directions
    both_sides = sides(meta, tiles)
    for side, blocks in enumerate(both_sides):
        stack = [first_terms[side], terms[side]]
        stack.extend(curvature_terms[side, tile] for tile in range(tiles))
        sums = station_sums(jnp.concatenate(stack, axis=0), side == 0)
        for tile, block in enumerate(blocks):
            part = to_lanes(jnp.split(sums[tile * rows : (tile + 1) * rows], 4, axis=0))
            part = part.reshape(-1, 8, LANES)
            if side == 0:
                part = transpose_matrix(part)
            else:
                part = jnp.where(component(part) < 4, part, -part)
            start = tiles * rows + tile * few
            groups = jnp.split(sums[start : start + few], directions // 4, axis=0)
            chosen = [groups[n : n + 4] for n in range(0, len(groups), 4)]
            made = [part.reshape(-1, LANES), *(to_lanes(parts) for parts in chosen)]
            part = jnp.concatenate(made, axis=0)
            add_to_owner(meta, near, block, part)
            compact[tile] = part if side == 0 else compact[tile] + pltpu.roll(part, SB, 1)
    lane = lax.broadcasted_iota(jnp.int32, (8, LANES), 1)
    for tile in range(tiles):
        numbers = [blocks[tile].astype(jnp.float32) for blocks in both_sides]
        number = jnp.where(lane < BLOCK_NUMBERS + 2 * SB, *numbers)
        compact[tile, -8:] = jnp.where(lane < BLOCK_NUMBERS, compact[tile, -8:], number)
    sent.wait()


def merge_kernel(meta, near, compact, total):
    slots, rows = near.shape[:2]
    lane = lax.broadcasted_iota(jnp.int32, (8, LANES), 1)
    found = []
    for tile in range(compact.shape[0]):
        value = compact[tile]
        for side in range(2):
            start = BLOCK_NUMBERS + 2 * SB * side
            number = jnp.broadcast_to(value[-8:, start : start + 1], (8, LANES))
            block = number.astype(jnp.int32)
            owner = block >> 1
            slot = jnp.where((owner ^ entry(meta, 0, 0)) & 1 == 0, owner >> 1, -1)
            shifted = pltpu.roll(value, SB if side == 0 else LANES - SB, 1)
            stays = block & 1 == side
            part = jnp.where(stays, value.reshape(-1, 8, LANES), shifted.reshape(-1, 8, LANES))
            part = jnp.where((lane // SB) & 1 == block & 1, part, 0.0)
            found.append((slot, part))
    for n in range(slots):
        out = near[n].reshape(-1, 8, LANES)
        for slot, part in found:
            out = out + jnp.where(slot == n, part, 0.0)
        total[n] = out.reshape(rows, LANES)


def finish_kernel(normalizer, parts, gradient, curvature):
    total = sum((parts[x] for x in range(1, parts.shape[0])), parts[0]) * normalizer
    directions = gradient.shape[0]
    rows, each = 2 * directions, directions // 4
    grad = total[:rows].reshape(each, 8, LANES)
    for g in range(4):
        gradient[g * each : (g + 1) * each] = grad[:, :, 2 * SB * g : 2 * SB * (g + 1)]
    for k in range(directions):
        group, member = k // 4, k % 4
        start = rows + group // 4 * 8 + member // 2 * 4 + member % 2
        lane = group % 4 * 2 * SB
        for c in range(2):
            row = total[start + 2 * c : start + 2 * c + 1]
            curvature[k, c : c + 1] = row[:, lane : lane + 2 * SB]


def call(kernel, scalars, arrays, in_hbm, results, scratch=(), to_hbm=(), aliases=None, cost=None):
    place = lambda space: pl.BlockSpec(memory_space=space)
    spaces = [pltpu.SMEM] * len(scalars) + [pltpu.VMEM] * len(arrays) + [pltpu.HBM] * len(in_hbm)
    return pl.pallas_call(
        kernel,
        in_specs=[place(space) for space in spaces],
        out_specs=[place(pltpu.HBM)] * len(to_hbm) + [place(pltpu.VMEM)] * len(results),
        out_shape=[
            *(pltpu.HBM(shape, jnp.float32) for shape in to_hbm),
            *(pltpu.VMEM(getattr(v, "shape", v), getattr(v, "dtype", jnp.float32)) for v in results),
        ],
        scratch_shapes=list(scratch),
        input_output_aliases=aliases or {},
        cost_estimate=cost,
        compiler_params=pltpu.CompilerParams(vmem_limit_bytes=32 * 1024 * 1024),
    )(*scalars, *arrays, *(pltpu.with_memory_space_constraint(v, pltpu.HBM) for v in in_hbm))


def swap_with(value, axis, mask):
    size = lax.axis_size(axis)
    return lax.ppermute(value, axis, [(place, place ^ mask) for place in range(size)])


def trade(slots):
    size = lax.axis_size("tile")
    groups = [list(range(core, size, 2)) for core in range(2)]
    return lax.all_to_all(slots, "tile", 0, 0, axis_index_groups=groups, tiled=True)


def body_kernels(coherency, observed, flags, tile_map, jones):
    tiles, directions, samples = coherency.shape[:3]
    chips = lax.axis_size("tile") // 2
    rows = 2 * directions
    extra = -(-directions // 16) * 8
    place = [
        jnp.full((tiles, 1), lax.axis_index(axis), jnp.int32) for axis in ("tile", "dir")
    ]
    meta = jnp.concatenate([*place, tile_map, flags], axis=1)

    def memory(*shape, kind=jnp.float32):
        return pltpu.VMEM(shape, kind)

    (packed,) = call(
        pack_kernel,
        [],
        [],
        [jones],
        [(chips, rows, LANES)],
        [memory(*jones.shape), pltpu.SemaphoreType.DMA],
    )
    near = trade(packed)
    narrow = (tiles, directions, samples // 2, 16, BASELINES)
    moments, narrow = call(
        moment_kernel,
        [],
        [],
        [flags, coherency],
        [jax.ShapeDtypeStruct(narrow, coherency.dtype)],
        [
            pltpu.SMEM(flags.shape, flags.dtype),
            memory(*coherency.shape, kind=coherency.dtype),
            memory(tiles, 4, 4 * rows, BASELINES),
            pltpu.SemaphoreType.DMA((tiles, PIECES)),
            pltpu.SemaphoreType.DMA,
            pltpu.SemaphoreType.DMA((tiles, PIECES)),
        ],
        [(tiles, 4, 4 * rows, BASELINES)],
        cost=pl.CostEstimate(
            flops=10 * coherency.size, bytes_accessed=4 * coherency.size, transcendentals=0
        ),
    )
    far = swap_with(near, "tile", 1)

    expanded = (tiles, 2, 4 * rows + SPARE_ROWS, LANES)
    of_tile = [(samples, 8, BASELINES), (directions, samples // 2, 2, 8, BASELINES)]
    narrow = pltpu.with_memory_space_constraint(narrow, pltpu.VMEM)
    weight = memory(directions, 12, 8, BASELINES)
    model, row_jones, col_jones, paired = call(
        first_model_kernel,
        [],
        [meta, near, far, narrow],
        [],
        [
            of_tile[0],
            expanded,
            expanded,
            of_tile[1],
        ],
        [weight],
    )
    first = [model, swap_with(model, "dir", 1), row_jones, col_jones, paired]
    model, paired = call(
        functools.partial(next_model_kernel, 1),
        [],
        [narrow, row_jones, col_jones],
        [],
        of_tile,
        [weight],
    )
    last = [model, swap_with(model, "dir", 1), row_jones, col_jones, paired]

    residual_shape = (tiles, samples, 8, LANES)
    terms = (2, 4 * rows, BASELINES)
    scratch = [
        memory(samples, 8, LANES),
        memory(samples // 2, 12, 8, BASELINES),
        pltpu.SemaphoreType.DMA,
    ]
    curvature_terms, masks = call(
        curvature_kernel,
        [],
        [meta, near, far, moments],
        [],
        [(2, tiles, 2 * directions, BASELINES), (tiles, 1 + flags.shape[1], 8, BASELINES)],
        [memory(tiles, 2, 2, 4 * directions + SPARE_ROWS, LANES)],
        cost=pl.CostEstimate(
            flops=coherency.size, bytes_accessed=coherency.size, transcendentals=0
        ),
    )
    residual, first_terms = call(
        first_gradient_kernel,
        [],
        [meta, masks, observed, *first],
        [],
        [terms],
        scratch,
        [residual_shape],
    )
    slots = (chips, rows + extra, LANES)
    residual, near, compact = call(
        functools.partial(last_gradient_kernel, tiles),
        [],
        [meta, first_terms, curvature_terms, masks, observed, *last],
        [residual],
        [slots, (tiles,) + slots[1:]],
        [
            memory(*terms),
            *scratch,
            pltpu.SMEM(meta.shape, meta.dtype),
            pltpu.SemaphoreType.DMA,
        ],
        [residual_shape],
        {10: 0},
    )
    theirs = swap_with(compact, "tile", 1)
    (total,) = call(merge_kernel, [], [meta, near, theirs], [], [slots])
    parts = trade(total)
    directions, _, owned = jones.shape
    in_vmem = pl.BlockSpec(memory_space=pltpu.VMEM)
    gradient, curvature = pl.pallas_call(
        functools.partial(finish_kernel, 1.0 / (samples * SB)),
        in_specs=[in_vmem],
        out_specs=[in_vmem] * 2,
        out_shape=[
            jax.ShapeDtypeStruct(jones.shape, jnp.float32),
            jax.ShapeDtypeStruct((directions, 2, owned), jnp.float32),
        ],
        compiler_params=pltpu.CompilerParams(vmem_limit_bytes=32 * 1024 * 1024),
    )(parts)
    return residual, gradient, curvature


def body(coherency, observed, flags, tile_map, jones):
    jones_all = lax.all_gather(jones, "tile", axis=2, tiled=True)
    how_many = coherency.shape[0]
    predictions = []
    products_list = []
    weight_list = []
    for number in range(how_many):
        predicted, products = tile_terms(
            coherency[number].astype(jnp.float32), jones_all, tile_map[number]
        )
        predictions.append(predicted)
        products_list.append(products)
        weight_list.append(weights(flags[number], tile_map[number]))
    partial_value = jnp.stack(predictions)
    weight = jnp.stack(weight_list)
    columns = observed.shape[3]
    portion = columns // lax.axis_size("dir")
    offset = lax.axis_index("dir") * portion
    summed = lax.psum(partial_value, "dir")
    residual = weight * (observed.astype(jnp.float32) - summed)
    residual_mine = lax.dynamic_slice_in_dim(residual, offset, portion, 3)
    grad_total = jnp.zeros((jones_all.shape[0], 8, jones_all.shape[2]), jnp.float32)
    curv_total = jnp.zeros((jones_all.shape[0], 2, jones_all.shape[2]), jnp.float32)
    for number in range(how_many):
        grad_row, grad_col, curv_row, curv_col = station_terms(
            residual[number], weight[number], products_list[number]
        )
        block_pair = tile_map[number]
        grad_total = add_block(
            add_block(grad_total, grad_row, block_pair[0]), grad_col, block_pair[1]
        )
        curv_total = add_block(
            add_block(curv_total, curv_row, block_pair[0]), curv_col, block_pair[1]
        )
    grad_owned, curv_owned = (
        lax.psum_scatter(grad_total, "tile", scatter_dimension=2, tiled=True),
        lax.psum_scatter(curv_total, "tile", scatter_dimension=2, tiled=True),
    )
    normalizer = 1.0 / (observed.shape[1] * SB)
    return (residual_mine, grad_owned * normalizer, curv_owned * normalizer)


def solution(mesh):
    specs = dict(
        mesh=mesh,
        in_specs=(
            P("tile", "dir", None, None, None),
            P("tile", None, None, None),
            P("tile", None),
            P("tile", None),
            P("dir", None, "tile"),
        ),
        out_specs=(P("tile", None, None, "dir"), P("dir", None, "tile"), P("dir", None, "tile")),
        check_vma=False,
    )

    def run(coherency, observed, flags, tile_map, jones):
        owned = jones.shape[2] // mesh.shape["tile"]
        directions = jones.shape[0] // mesh.shape["dir"]
        fits = owned == 2 * SB and directions == 24
        paired = mesh.shape["dir"] == 2 and mesh.shape["tile"] == 16
        paired = paired and coherency.shape[0] == 2 * mesh.shape["tile"]
        chosen = body_kernels if fits and paired else body
        return jax.shard_map(chosen, **specs)(coherency, observed, flags, tile_map, jones)

    return run
```

```python
import functools

import jax
import jax.numpy as jnp
from jax import lax
from jax.experimental import pallas as pl
from jax.experimental.pallas import tpu as pltpu
from jax.sharding import PartitionSpec as P

SB = 16
FREQ_CHANNELS = 4
LANES = 128
BASELINES = SB * SB
CHUNK = 3


def split_parts(values):
    shape = values.shape[:-2] + (2, 2, values.shape[-1])
    return (values[..., 0:4, :].reshape(shape), values[..., 4:8, :].reshape(shape))


def join_parts(re_part, im_part):
    shape = re_part.shape[:-3] + (4, re_part.shape[-1])
    return jnp.concatenate([re_part.reshape(shape), im_part.reshape(shape)], axis=-2)


def complex_product(left_re, left_im, right_re, right_im):
    lre = left_re[..., :, :, None, :]
    lim = left_im[..., :, :, None, :]
    rre = right_re[..., None, :, :, :]
    rim = right_im[..., None, :, :, :]
    return (jnp.sum(lre * rre - lim * rim, axis=-3), jnp.sum(lre * rim + lim * rre, axis=-3))


def adjoint(re_part, im_part):
    return (jnp.swapaxes(re_part, -3, -2), -jnp.swapaxes(im_part, -3, -2))


def weights(row_flag_mask, block_pair):
    valid_samples = jnp.repeat((1 - row_flag_mask).astype(jnp.float32), FREQ_CHANNELS)
    baseline = jnp.arange(SB * SB, dtype=jnp.int32)
    inner_row = baseline // SB
    inner_col = baseline % SB
    upper_triangle_pairs = jnp.where(
        (block_pair[0] < block_pair[1]) | (inner_row < inner_col), 1.0, 0.0
    ).astype(jnp.float32)
    return valid_samples[:, None, None] * upper_triangle_pairs[None, None, :]


def tile_terms(coher, jones_all, block_pair):
    row_gain_matrix = lax.dynamic_slice_in_dim(jones_all, block_pair[0] * SB, SB, 2)
    col_jones = lax.dynamic_slice_in_dim(jones_all, block_pair[1] * SB, SB, 2)
    first_antenna = jnp.repeat(row_gain_matrix, SB, axis=2)[:, None]
    station_q = jnp.tile(col_jones, (1, 1, SB))[:, None]
    coh_re, coh_im = split_parts(coher)
    p_re, p_im = split_parts(first_antenna)
    q_re, q_im = split_parts(station_q)
    qh_re, qh_im = adjoint(q_re, q_im)
    m_re, m_im = complex_product(coh_re, coh_im, qh_re, qh_im)
    n_re, n_im = complex_product(p_re, p_im, coh_re, coh_im)
    v_re, v_im = complex_product(p_re, p_im, m_re, m_im)
    predicted = jnp.sum(join_parts(v_re, v_im), axis=0)
    return (predicted, (m_re, m_im, n_re, n_im))


def station_terms(residual, weight, products):
    m_re, m_im, n_re, n_im = products
    r_re, r_im = split_parts(residual)
    mh_re, mh_im = adjoint(m_re, m_im)
    g_re, g_im = complex_product(r_re, r_im, mh_re, mh_im)
    row_side = jnp.sum(join_parts(g_re, g_im), axis=1)
    rh_re, rh_im = adjoint(r_re, r_im)
    f_re, f_im = complex_product(rh_re, rh_im, n_re, n_im)
    col_side = jnp.sum(join_parts(f_re, f_im), axis=1)
    row_curv = jnp.sum(jnp.sum(m_re * m_re + m_im * m_im, axis=-2) * weight[None], axis=1)
    column_curvature = jnp.sum(jnp.sum(n_re * n_re + n_im * n_im, axis=-3) * weight[None], axis=1)
    lead = row_side.shape[0]
    grad_row = jnp.sum(row_side.reshape(lead, 8, SB, SB), axis=3)
    grad_col = jnp.sum(col_side.reshape(lead, 8, SB, SB), axis=2)
    curv_row = jnp.sum(row_curv.reshape(lead, 2, SB, SB), axis=3)
    curv_col = jnp.sum(column_curvature.reshape(lead, 2, SB, SB), axis=2)
    return (grad_row, grad_col, curv_row, curv_col)


def add_block(total, piece, block):
    offset = block * SB
    current = lax.dynamic_slice_in_dim(total, offset, SB, 2)
    return lax.dynamic_update_slice_in_dim(total, current + piece, offset, 2)


def component(value):
    return lax.broadcasted_iota(jnp.int32, value.shape, value.ndim - 2)


def turn(value, ahead):
    return pltpu.roll(value, (8 - ahead) % 8, value.ndim - 2)


def flip(value, mask):
    if mask == 4:
        return turn(value, 4)
    return jnp.where(component(value) & mask == 0, turn(value, mask), turn(value, 8 - mask))


def transpose_matrix(value):
    place = component(value) & 3
    return jnp.where(place == 1, turn(value, 1), jnp.where(place == 2, turn(value, 7), value))


def fold(values):
    values = [values[x] + flip(values[x + 1], 1) for x in range(0, 4, 2)]
    return values[0] + flip(values[1], 2)


def pair_parts(first, second):
    low = component(first) < 4
    return jnp.where(low, first, turn(second, 4)), jnp.where(low, turn(first, 4), second)


def add_all(sums, values):
    if sums is None:
        return values
    return [v if total is None else total + v for total, v in zip(sums, values)]


def halves(value):
    high = value.astype(jnp.bfloat16)
    return high, (value - high.astype(jnp.float32)).astype(jnp.bfloat16)


def station_of(baseline, row_side):
    return baseline // SB if row_side else baseline % SB


def one_hot(row_side, transposed):
    shape = (BASELINES, LANES) if transposed else (LANES, BASELINES)
    lane = lax.broadcasted_iota(jnp.int32, shape, 1 if transposed else 0)
    baseline = lax.broadcasted_iota(jnp.int32, shape, 0 if transposed else 1)
    return (lane == station_of(baseline, row_side)).astype(jnp.bfloat16)


def expand(blocks, row_side):
    made = []
    for packed in blocks:
        made.extend([packed] + [pltpu.roll(packed, LANES - 2 * SB * g, 1) for g in range(1, 4)])
    high, low = halves(jnp.concatenate(made, axis=0))
    both = jnp.concatenate([high, low], axis=1)
    chosen = jnp.concatenate([one_hot(row_side, False)] * 2, axis=0)
    wide = jnp.dot(both, chosen, preferred_element_type=jnp.float32)
    ends = [0]
    for packed in blocks:
        ends.append(ends[-1] + 4 * packed.shape[0])
    return [wide[start:end] for start, end in zip(ends, ends[1:])]


def station_sums(values, row_side):
    high, low = halves(values)
    both = jnp.concatenate([high, low], axis=0)
    total = jnp.dot(both, one_hot(row_side, True), preferred_element_type=jnp.float32)
    count = high.shape[0]
    return total[:count] + total[count:]


def to_lanes(parts, half):
    moved = [pltpu.roll(part, 2 * SB * g + SB * half, 1) for g, part in enumerate(parts)]
    return sum(moved[1:], moved[0])


def arranged(ref, tile, half, k, mask):
    row = lambda c: ref[tile, half, pl.ds(8 * k + c, 8, stride=0), :]
    first = lax.broadcasted_iota(jnp.int32, (8, LANES), 0) & mask == 0
    pick = lambda c, d: jnp.where(first, row(c), row(d))
    return (pick(0, 3), pick(2, 1)), (pick(4, 7), pick(6, 5))


def half_lanes(index):
    return pl.ds(pl.multiple_of(index * LANES, LANES), LANES)


def upper_mask(meta, tile):
    shape = (8, BASELINES)
    baseline = lax.broadcasted_iota(jnp.int32, shape, 1)
    above = entry(meta, tile, 2, shape) < entry(meta, tile, 3, shape)
    return jnp.where((baseline // SB < baseline % SB) | above, 1.0, 0.0).astype(jnp.float32)


def pack_kernel(jones_in_hbm, slots, jones, packed, in_semaphore, semaphores):
    copy = pltpu.make_async_copy(jones_in_hbm, jones, in_semaphore)
    copy.start()
    copy.wait()
    each = jones.shape[0] // 4
    rows = packed.shape[0]
    packed[...] = jnp.concatenate(
        [jones[g * each : (g + 1) * each].reshape(rows, 2 * SB) for g in range(4)], axis=1
    )
    copies = [
        pltpu.make_async_copy(packed, slots.at[n], semaphores.at[n]) for n in range(slots.shape[0])
    ]
    for copy in copies:
        copy.start()
    for copy in copies:
        copy.wait()


def entry(meta, row, column, shape=(8, LANES)):
    return jnp.broadcast_to(meta[row : row + 1, column : column + 1], shape)


def station_block(meta, near, far, tile, side):
    block = entry(meta, tile, 2 + side)
    owner = block >> 1
    own_core = (owner ^ entry(meta, 0, 0)) & 1 == 0
    chips, rows = near.shape[:2]
    found = None
    for chip in range(chips):
        packed = jnp.where(own_core, near[chip].reshape(-1, 8, LANES), far[chip].reshape(-1, 8, LANES))
        found = packed if found is None else jnp.where(owner >> 1 == chip, packed, found)
    shifted = pltpu.roll(found.reshape(rows, LANES), LANES - SB, 1).reshape(found.shape)
    return jnp.where(block & 1 == 0, found, shifted).reshape(rows, LANES)


PIECES = 6
SPARE_ROWS = 8


def block_of(meta, tile, side):
    return meta[tile, 2 + side]


def valid_of(flags, tile, sample):
    return (1 - flags[tile, sample // FREQ_CHANNELS]).astype(jnp.float32)


def sides(meta, tiles):
    return [[block_of(meta, tile, side) for tile in range(tiles)] for side in range(2)]


def pieces(source, target, semaphores):
    each = source.shape[0] // PIECES
    parts = [pl.ds(n * each, each) for n in range(PIECES)]
    return [
        pltpu.make_async_copy(source.at[part], target.at[part], semaphores.at[n])
        for n, part in enumerate(parts)
    ]


def moment_kernel(
    flags_in_hbm, source, moments_out, pairs,
    flags, coherency, moments, semaphores, flag_semaphore, out_semaphores,
):
    tiles, directions, samples = source.shape[:3]
    each = directions // PIECES
    flag_copy = pltpu.make_async_copy(flags_in_hbm, flags, flag_semaphore)
    flag_copy.start()
    copies = [pieces(source.at[t], coherency.at[t], semaphores.at[t]) for t in range(tiles)]
    for copy in sum(copies, []):
        copy.start()
    flag_copy.wait()
    sent = []
    for tile in range(tiles):

        def add_direction(k, _):
            rows = pl.ds(pl.multiple_of(8 * k, 8), 8)
            for half in range(2):
                lanes = slice(half * LANES, (half + 1) * LANES)
                sums = [jnp.zeros((8, LANES), jnp.float32)] * 4
                for s in range(samples):
                    c = coherency[tile, k, s, :, lanes].astype(jnp.float32)
                    weighted = valid_of(flags, tile, s) * c
                    sums = [v + weighted * (turn(c, n) if n else c) for n, v in enumerate(sums)]
                    if s % 2 == 1:
                        both = jnp.concatenate(pair_parts(before, c), axis=0)
                        pairs[tile, k, s // 2, :, lanes] = both.astype(pairs.dtype)
                    before = c
                for n in range(4):
                    moments[tile, n, rows, lanes] = sums[n]
            return 0

        for n, copy in enumerate(copies[tile]):
            copy.wait()
            lax.fori_loop(n * each, (n + 1) * each, add_direction, 0)
            rows = pl.ds(8 * n * each, 8 * each)
            sent.append(
                pltpu.make_async_copy(
                    moments.at[tile, :, rows],
                    moments_out.at[tile, :, rows],
                    out_semaphores.at[tile, n],
                )
            )
            sent[-1].start()
    for copy in sent:
        copy.wait()


def station_products(packed):
    e = packed.reshape(-1, 8, LANES)
    bits = component(e)
    part = bits >= 4
    second = bits & 1 != 0
    spread = lambda v: (lambda u: u + flip(u, 2))(v + flip(v, 4))
    across = flip(e, 1)
    squares = spread(e * e)
    cross_re = 2.0 * spread(e * across)
    sign = jnp.where(part == second, 1.0, -1.0)
    cross_im = 2.0 * spread(sign * (e * flip(across, 4)))
    made = jnp.where(bits & 2 == 0, squares, jnp.where(second, cross_im, cross_re))
    low = component(made[0]) < 4
    joined = [jnp.where(low, made[n], made[n + 1]) for n in range(0, made.shape[0], 2)]
    return jnp.concatenate(joined, axis=0)


def first_model_kernel(meta, near, far, narrow, model, row_jones, col_jones, paired, weight):
    tiles = narrow.shape[0]
    for side, jones in enumerate((row_jones, col_jones)):
        found = [station_block(meta, near, far, tile, side) for tile in range(tiles)]
        for tile, made in enumerate(expand(found, side == 0)):
            for half in range(2):
                lanes = slice(half * LANES, (half + 1) * LANES)
                jones[tile, half, : made.shape[0]] = made[:, lanes]
    models(0, narrow, row_jones, col_jones, model, paired, weight)


def next_model_kernel(tile, narrow, row_jones, col_jones, model, paired, weight):
    models(tile, narrow, row_jones, col_jones, model, paired, weight)


def models(tile, narrow, row_jones, col_jones, model, paired, weight):
    directions, pairs = paired.shape[:2]

    def weigh(k, _):
        for half in range(2):
            lanes = slice(half * LANES, (half + 1) * LANES)
            p_re, p_im = arranged(row_jones, tile, half, k, 2)
            q_re, q_im = arranged(col_jones, tile, half, k, 1)
            for x in range(4):
                a, b = x // 2, x % 2
                z_re = p_re[a] * q_re[b] + p_im[a] * q_im[b]
                z_im = p_im[a] * q_re[b] - p_re[a] * q_im[b]
                weight[k, 3 * x, :, lanes] = z_re
                weight[k, 3 * x + 1, :, lanes] = z_im - z_re
                weight[k, 3 * x + 2, :, lanes] = z_re + z_im
        return 0

    lax.fori_loop(0, directions, weigh, 0, unroll=8)

    def add_samples(step, _):
        lanes = half_lanes(step % 2)
        first = step // 2 * CHUNK
        zero = jnp.zeros((8, LANES), jnp.float32)
        low = component(zero) < 4
        sums = [None] * 12
        for k in range(directions):
            parts = []
            for i in range(CHUNK):
                both = narrow[tile, k, first + i, :, lanes].astype(jnp.float32)
                real, imag = both[:8], both[8:]
                paired[k, first + i, 0, :, lanes] = real
                paired[k, first + i, 1, :, lanes] = imag
                parts.append((real + imag, real, imag))
            for n in range(12):
                w = weight[k, n, :, lanes]
                sums[n] = add_all(sums[n], [w * parts[i][n % 3] for i in range(CHUNK)])
        for i in range(CHUNK):
            one, two, three = ([sums[3 * x + m][i] for x in range(4)] for m in range(3))
            real = fold([one[x] - three[x] for x in range(4)])
            imag = fold([one[x] + two[x] for x in range(4)])
            place = 2 * (first + i)
            model[place, :, lanes] = jnp.where(low, real, turn(imag, 4))
            model[place + 1, :, lanes] = jnp.where(low, turn(real, 4), imag)
        return 0

    lax.fori_loop(0, 2 * pairs // CHUNK, add_samples, 0, unroll=4)


def curvature_kernel(meta, near, far, moments, terms, masks, products):
    tiles = moments.shape[0]
    directions = moments.shape[2] // 8
    for tile in range(tiles):
        masks[tile, 0] = upper_mask(meta, tile)
        for time in range(masks.shape[1] - 1):
            valid = (1 - entry(meta, tile, 4 + time, (8, BASELINES))).astype(jnp.float32)
            masks[tile, 1 + time] = valid * masks[tile, 0]
    for side in range(2):
        found = [station_block(meta, near, far, tile, side) for tile in range(tiles)]
        made = expand([station_products(packed) for packed in found], side == 0)
        for tile in range(tiles):
            for half in range(2):
                lanes = slice(half * LANES, (half + 1) * LANES)
                products[tile, side, half, : made[tile].shape[0]] = made[tile][:, lanes]

    def combine(step, _):
        tile, group = step // (directions // 4), step % (directions // 4)
        mask = masks[tile, 0]
        bits = component(mask[:, :LANES])
        odd = bits & 1 != 0
        upper = bits & 2 != 0
        sign = jnp.where(bits < 4, -1.0, 1.0)
        member = (bits >> 2) * 2 + (bits & 1)
        for half in range(2):
            lanes = slice(half * LANES, (half + 1) * LANES)
            found = [None, None]
            for i in range(4):
                k = 4 * group + i
                rows = pl.ds(pl.multiple_of(8 * k, 8), 8)
                m = [moments[tile, n, rows, lanes] for n in range(4)]
                row = lambda side, n: products[tile, side, half, pl.ds(4 * k + n, 8, stride=0), :]
                h = [row(1, n) for n in range(4)]
                row_sum = m[0] * jnp.where(odd, h[1], h[0])
                row_sum = row_sum + jnp.where(odd, sign * (m[3] * h[3]), m[1] * h[2])
                h = [row(0, n) for n in range(4)]
                col_sum = m[0] * jnp.where(upper, h[1], h[0])
                col_sum = col_sum + m[2] * jnp.where(upper, -sign * h[3], h[2])
                row_sum = row_sum + turn(row_sum, 4)
                row_sum = row_sum + flip(row_sum, 1)
                col_sum = transpose_matrix(col_sum)
                col_sum = col_sum + turn(col_sum, 4)
                col_sum = col_sum + flip(col_sum, 1)
                for side, v in enumerate((row_sum, col_sum)):
                    found[side] = v if i == 0 else jnp.where(member == i, v, found[side])
            for side in range(2):
                place = pl.ds(pl.multiple_of(8 * group, 8), 8)
                terms[side, tile, place, lanes] = mask[:, lanes] * found[side]
        return 0

    lax.fori_loop(0, tiles * directions // 4, combine, 0)


def add_to_owner(meta, near, far, block, part):
    owner = block // 2
    own_core = jnp.where(owner % 2 == meta[0, 0] % 2, 1.0, 0.0)
    near[owner // 2] = near[owner // 2] + own_core * part
    far[owner // 2] = far[owner // 2] + (1.0 - own_core) * part


def add_gradient_terms(
    tile, meta, masks, observed, mine, other, row_jones, col_jones, paired,
    residual_out, terms, residual, turned, semaphore,
):
    directions, pairs = paired.shape[:2]
    first_half = entry(meta, 0, 1) == 0
    for i in range(pairs):
        both = []
        for s in (2 * i, 2 * i + 1):
            summed = mine[s] + other[s]
            weight = masks[tile, 1 + s // FREQ_CHANNELS]
            r = weight * (observed[tile, s].astype(jnp.float32) - summed)
            residual[s] = jnp.where(first_half, r[:, :LANES], r[:, LANES:])
            both.append(r)
        made = [pair_parts(*both)]
        for x in range(1, 4):
            bit = x & -x
            made.append(tuple(flip(v, bit) for v in made[x - bit]))
        for x, (real, imag) in enumerate(made):
            turned[i, 3 * x] = real
            turned[i, 3 * x + 1] = real + imag
            turned[i, 3 * x + 2] = real - imag
    sent = pltpu.make_async_copy(residual, residual_out.at[tile], semaphore)
    sent.start()

    def add_directions(step, _):
        half, lanes = step % 2, half_lanes(step % 2)
        first = step // 2 * CHUNK
        zero = jnp.zeros((8, LANES), jnp.float32)
        sums = [None] * 12
        for p in range(pairs):
            parts = []
            for i in range(CHUNK):
                real = paired[first + i, p, 0, :, lanes]
                imag = paired[first + i, p, 1, :, lanes]
                parts.append((real + imag, real, imag))
            for n in range(12):
                r = turned[p, n, :, lanes]
                sums[n] = add_all(sums[n], [r * parts[i][n % 3] for i in range(CHUNK)])
        bits = component(zero)
        real = bits < 4
        equal = (bits >> 1) & 1 == bits & 1
        for i in range(CHUNK):
            k = first + i
            p_re, p_im = arranged(row_jones, tile, half, k, 2)
            q_re, q_im = arranged(col_jones, tile, half, k, 1)
            row_sum = [None, None]
            col_sum = [None, None]
            for x in range(4):
                a, b = x // 2, x % 2
                y_re = sums[3 * x][i] - sums[3 * x + 2][i]
                y_im = sums[3 * x + 1][i] - sums[3 * x][i]
                y_re = y_re + turn(y_re, 4)
                y_im = y_im + turn(y_im, 4)
                one, two = jnp.where(real, y_re, y_im), jnp.where(real, -y_im, y_re)
                (row_sum[a],) = add_all(row_sum[a : a + 1], [q_re[b] * one + q_im[b] * two])
                (col_sum[b],) = add_all(col_sum[b : b + 1], [p_re[a] * one - p_im[a] * two])
            rows = pl.ds(pl.multiple_of(8 * k, 8), 8)
            g, h = row_sum
            g = jnp.where(equal, g, h) + flip(jnp.where(equal, h, g), 1)
            terms[0, rows, lanes] = g
            g, h = col_sum
            g = jnp.where(equal, g, h) + flip(jnp.where(equal, h, g), 2)
            terms[1, rows, lanes] = g
        return 0

    lax.fori_loop(0, 2 * directions // CHUNK, add_directions, 0, unroll=4)
    return sent


def first_gradient_kernel(
    meta, masks, observed, mine, other, row_jones, col_jones, paired,
    residual_out, terms, residual, turned, semaphore,
):
    sent = add_gradient_terms(
        0, meta, masks, observed, mine, other, row_jones, col_jones, paired,
        residual_out, terms, residual, turned, semaphore,
    )
    sent.wait()


def last_gradient_kernel(
    tiles, meta_in_vmem, first_terms, curvature_terms,
    masks, observed, mine, other, row_jones, col_jones, paired,
    residual_before, residual_out, near, far, terms, residual, turned, semaphore,
    meta, meta_semaphore,
):
    del residual_before
    meta_copy = pltpu.make_async_copy(meta_in_vmem, meta, meta_semaphore)
    meta_copy.start()
    sent = add_gradient_terms(
        tiles - 1, meta_in_vmem, masks, observed, mine, other, row_jones, col_jones, paired,
        residual_out, terms, residual, turned, semaphore,
    )
    near[...] = jnp.zeros_like(near)
    far[...] = jnp.zeros_like(far)
    meta_copy.wait()
    directions = paired.shape[0]
    rows, few = 8 * directions, 2 * directions
    for side, blocks in enumerate(sides(meta, tiles)):
        stack = [first_terms[side], terms[side]]
        stack.extend(curvature_terms[side, tile] for tile in range(tiles))
        sums = station_sums(jnp.concatenate(stack, axis=0), side == 0)
        for tile, block in enumerate(blocks):
            half = block % 2
            part = to_lanes(jnp.split(sums[tile * rows : (tile + 1) * rows], 4, axis=0), half)
            part = part.reshape(-1, 8, LANES)
            if side == 0:
                part = transpose_matrix(part)
            else:
                part = jnp.where(component(part) < 4, part, -part)
            start = tiles * rows + tile * few
            groups = jnp.split(sums[start : start + few], directions // 4, axis=0)
            chosen = [groups[n : n + 4] for n in range(0, len(groups), 4)]
            made = [part.reshape(-1, LANES), *(to_lanes(parts, half) for parts in chosen)]
            add_to_owner(meta, near, far, block, jnp.concatenate(made, axis=0))
    sent.wait()


def finish_kernel(normalizer, parts, gradient, curvature):
    total = sum((parts[x] for x in range(1, parts.shape[0])), parts[0]) * normalizer
    directions = gradient.shape[0]
    rows, each = 2 * directions, directions // 4
    grad = total[:rows].reshape(each, 8, LANES)
    for g in range(4):
        gradient[g * each : (g + 1) * each] = grad[:, :, 2 * SB * g : 2 * SB * (g + 1)]
    for k in range(directions):
        group, member = k // 4, k % 4
        start = rows + group // 4 * 8 + member // 2 * 4 + member % 2
        lane = group % 4 * 2 * SB
        for c in range(2):
            row = total[start + 2 * c : start + 2 * c + 1]
            curvature[k, c : c + 1] = row[:, lane : lane + 2 * SB]


def call(kernel, scalars, arrays, in_hbm, results, scratch=(), to_hbm=(), aliases=None, cost=None):
    place = lambda space: pl.BlockSpec(memory_space=space)
    spaces = [pltpu.SMEM] * len(scalars) + [pltpu.VMEM] * len(arrays) + [pltpu.HBM] * len(in_hbm)
    return pl.pallas_call(
        kernel,
        in_specs=[place(space) for space in spaces],
        out_specs=[place(pltpu.HBM)] * len(to_hbm) + [place(pltpu.VMEM)] * len(results),
        out_shape=[
            *(pltpu.HBM(shape, jnp.float32) for shape in to_hbm),
            *(pltpu.VMEM(getattr(v, "shape", v), getattr(v, "dtype", jnp.float32)) for v in results),
        ],
        scratch_shapes=list(scratch),
        input_output_aliases=aliases or {},
        cost_estimate=cost,
        compiler_params=pltpu.CompilerParams(vmem_limit_bytes=32 * 1024 * 1024),
    )(*scalars, *arrays, *(pltpu.with_memory_space_constraint(v, pltpu.HBM) for v in in_hbm))


def swap_with(value, axis, mask):
    size = lax.axis_size(axis)
    return lax.ppermute(value, axis, [(place, place ^ mask) for place in range(size)])


def trade(slots):
    size = lax.axis_size("tile")
    groups = [list(range(core, size, 2)) for core in range(2)]
    return lax.all_to_all(slots, "tile", 0, 0, axis_index_groups=groups, tiled=True)


def body_kernels(coherency, observed, flags, tile_map, jones):
    tiles, directions, samples = coherency.shape[:3]
    chips = lax.axis_size("tile") // 2
    rows = 2 * directions
    extra = -(-directions // 16) * 8
    place = [
        jnp.full((tiles, 1), lax.axis_index(axis), jnp.int32) for axis in ("tile", "dir")
    ]
    meta = jnp.concatenate([*place, tile_map, flags], axis=1)

    def memory(*shape, kind=jnp.float32):
        return pltpu.VMEM(shape, kind)

    (packed,) = call(
        pack_kernel,
        [],
        [],
        [jones],
        [],
        [
            memory(*jones.shape),
            memory(rows, LANES),
            pltpu.SemaphoreType.DMA,
            pltpu.SemaphoreType.DMA((chips,)),
        ],
        [(chips, rows, LANES)],
    )
    near = trade(packed)
    narrow = (tiles, directions, samples // 2, 16, BASELINES)
    moments, narrow = call(
        moment_kernel,
        [],
        [],
        [flags, coherency],
        [jax.ShapeDtypeStruct(narrow, coherency.dtype)],
        [
            pltpu.SMEM(flags.shape, flags.dtype),
            memory(*coherency.shape, kind=coherency.dtype),
            memory(tiles, 4, 4 * rows, BASELINES),
            pltpu.SemaphoreType.DMA((tiles, PIECES)),
            pltpu.SemaphoreType.DMA,
            pltpu.SemaphoreType.DMA((tiles, PIECES)),
        ],
        [(tiles, 4, 4 * rows, BASELINES)],
        cost=pl.CostEstimate(
            flops=10 * coherency.size, bytes_accessed=4 * coherency.size, transcendentals=0
        ),
    )
    far = swap_with(near, "tile", 1)

    expanded = (tiles, 2, 4 * rows + SPARE_ROWS, LANES)
    of_tile = [(samples, 8, BASELINES), (directions, samples // 2, 2, 8, BASELINES)]
    narrow = pltpu.with_memory_space_constraint(narrow, pltpu.VMEM)
    weight = memory(directions, 12, 8, BASELINES)
    model, row_jones, col_jones, paired = call(
        first_model_kernel,
        [],
        [meta, near, far, narrow],
        [],
        [
            of_tile[0],
            expanded,
            expanded,
            of_tile[1],
        ],
        [weight],
    )
    first = [model, swap_with(model, "dir", 1), row_jones, col_jones, paired]
    model, paired = call(
        functools.partial(next_model_kernel, 1),
        [],
        [narrow, row_jones, col_jones],
        [],
        of_tile,
        [weight],
    )
    last = [model, swap_with(model, "dir", 1), row_jones, col_jones, paired]

    residual_shape = (tiles, samples, 8, LANES)
    terms = (2, 4 * rows, BASELINES)
    scratch = [
        memory(samples, 8, LANES),
        memory(samples // 2, 12, 8, BASELINES),
        pltpu.SemaphoreType.DMA,
    ]
    curvature_terms, masks = call(
        curvature_kernel,
        [],
        [meta, near, far, moments],
        [],
        [(2, tiles, 2 * directions, BASELINES), (tiles, 1 + flags.shape[1], 8, BASELINES)],
        [memory(tiles, 2, 2, 4 * directions + SPARE_ROWS, LANES)],
        cost=pl.CostEstimate(
            flops=coherency.size, bytes_accessed=coherency.size, transcendentals=0
        ),
    )
    residual, first_terms = call(
        first_gradient_kernel,
        [],
        [meta, masks, observed, *first],
        [],
        [terms],
        scratch,
        [residual_shape],
    )
    slots = (chips, rows + extra, LANES)
    residual, near, far = call(
        functools.partial(last_gradient_kernel, tiles),
        [],
        [meta, first_terms, curvature_terms, masks, observed, *last],
        [residual],
        [slots, slots],
        [
            memory(*terms),
            *scratch,
            pltpu.SMEM(meta.shape, meta.dtype),
            pltpu.SemaphoreType.DMA,
        ],
        [residual_shape],
        {10: 0},
    )
    parts = trade(near + swap_with(far, "tile", 1))
    directions, _, owned = jones.shape
    in_vmem = pl.BlockSpec(memory_space=pltpu.VMEM)
    gradient, curvature = pl.pallas_call(
        functools.partial(finish_kernel, 1.0 / (samples * SB)),
        in_specs=[in_vmem],
        out_specs=[in_vmem] * 2,
        out_shape=[
            jax.ShapeDtypeStruct(jones.shape, jnp.float32),
            jax.ShapeDtypeStruct((directions, 2, owned), jnp.float32),
        ],
        compiler_params=pltpu.CompilerParams(vmem_limit_bytes=32 * 1024 * 1024),
    )(parts)
    return residual, gradient, curvature


def body(coherency, observed, flags, tile_map, jones):
    jones_all = lax.all_gather(jones, "tile", axis=2, tiled=True)
    how_many = coherency.shape[0]
    predictions = []
    products_list = []
    weight_list = []
    for number in range(how_many):
        predicted, products = tile_terms(
            coherency[number].astype(jnp.float32), jones_all, tile_map[number]
        )
        predictions.append(predicted)
        products_list.append(products)
        weight_list.append(weights(flags[number], tile_map[number]))
    partial_value = jnp.stack(predictions)
    weight = jnp.stack(weight_list)
    columns = observed.shape[3]
    portion = columns // lax.axis_size("dir")
    offset = lax.axis_index("dir") * portion
    summed = lax.psum(partial_value, "dir")
    residual = weight * (observed.astype(jnp.float32) - summed)
    residual_mine = lax.dynamic_slice_in_dim(residual, offset, portion, 3)
    grad_total = jnp.zeros((jones_all.shape[0], 8, jones_all.shape[2]), jnp.float32)
    curv_total = jnp.zeros((jones_all.shape[0], 2, jones_all.shape[2]), jnp.float32)
    for number in range(how_many):
        grad_row, grad_col, curv_row, curv_col = station_terms(
            residual[number], weight[number], products_list[number]
        )
        block_pair = tile_map[number]
        grad_total = add_block(
            add_block(grad_total, grad_row, block_pair[0]), grad_col, block_pair[1]
        )
        curv_total = add_block(
            add_block(curv_total, curv_row, block_pair[0]), curv_col, block_pair[1]
        )
    grad_owned, curv_owned = (
        lax.psum_scatter(grad_total, "tile", scatter_dimension=2, tiled=True),
        lax.psum_scatter(curv_total, "tile", scatter_dimension=2, tiled=True),
    )
    normalizer = 1.0 / (observed.shape[1] * SB)
    return (residual_mine, grad_owned * normalizer, curv_owned * normalizer)


def solution(mesh):
    specs = dict(
        mesh=mesh,
        in_specs=(
            P("tile", "dir", None, None, None),
            P("tile", None, None, None),
            P("tile", None),
            P("tile", None),
            P("dir", None, "tile"),
        ),
        out_specs=(P("tile", None, None, "dir"), P("dir", None, "tile"), P("dir", None, "tile")),
        check_vma=False,
    )

    def run(coherency, observed, flags, tile_map, jones):
        owned = jones.shape[2] // mesh.shape["tile"]
        directions = jones.shape[0] // mesh.shape["dir"]
        fits = owned == 2 * SB and directions == 24
        paired = mesh.shape["dir"] == 2 and mesh.shape["tile"] == 16
        paired = paired and coherency.shape[0] == 2 * mesh.shape["tile"]
        chosen = body_kernels if fits and paired else body
        return jax.shard_map(chosen, **specs)(coherency, observed, flags, tile_map, jones)

    return run
```

```python
import functools

import jax
import jax.numpy as jnp
from jax import lax
from jax.experimental import pallas as pl
from jax.experimental.pallas import tpu as pltpu
from jax.sharding import PartitionSpec as P

SB = 16
FREQ_CHANNELS = 4
LANES = 128
BASELINES = SB * SB
CHUNK = 3


def split_parts(values):
    shape = values.shape[:-2] + (2, 2, values.shape[-1])
    return (values[..., 0:4, :].reshape(shape), values[..., 4:8, :].reshape(shape))


def join_parts(re_part, im_part):
    shape = re_part.shape[:-3] + (4, re_part.shape[-1])
    return jnp.concatenate([re_part.reshape(shape), im_part.reshape(shape)], axis=-2)


def complex_product(left_re, left_im, right_re, right_im):
    lre = left_re[..., :, :, None, :]
    lim = left_im[..., :, :, None, :]
    rre = right_re[..., None, :, :, :]
    rim = right_im[..., None, :, :, :]
    return (jnp.sum(lre * rre - lim * rim, axis=-3), jnp.sum(lre * rim + lim * rre, axis=-3))


def adjoint(re_part, im_part):
    return (jnp.swapaxes(re_part, -3, -2), -jnp.swapaxes(im_part, -3, -2))


def weights(row_flag_mask, block_pair):
    valid_samples = jnp.repeat((1 - row_flag_mask).astype(jnp.float32), FREQ_CHANNELS)
    baseline = jnp.arange(SB * SB, dtype=jnp.int32)
    inner_row = baseline // SB
    inner_col = baseline % SB
    upper_triangle_pairs = jnp.where(
        (block_pair[0] < block_pair[1]) | (inner_row < inner_col), 1.0, 0.0
    ).astype(jnp.float32)
    return valid_samples[:, None, None] * upper_triangle_pairs[None, None, :]


def tile_terms(coher, jones_all, block_pair):
    row_gain_matrix = lax.dynamic_slice_in_dim(jones_all, block_pair[0] * SB, SB, 2)
    col_jones = lax.dynamic_slice_in_dim(jones_all, block_pair[1] * SB, SB, 2)
    first_antenna = jnp.repeat(row_gain_matrix, SB, axis=2)[:, None]
    station_q = jnp.tile(col_jones, (1, 1, SB))[:, None]
    coh_re, coh_im = split_parts(coher)
    p_re, p_im = split_parts(first_antenna)
    q_re, q_im = split_parts(station_q)
    qh_re, qh_im = adjoint(q_re, q_im)
    m_re, m_im = complex_product(coh_re, coh_im, qh_re, qh_im)
    n_re, n_im = complex_product(p_re, p_im, coh_re, coh_im)
    v_re, v_im = complex_product(p_re, p_im, m_re, m_im)
    predicted = jnp.sum(join_parts(v_re, v_im), axis=0)
    return (predicted, (m_re, m_im, n_re, n_im))


def station_terms(residual, weight, products):
    m_re, m_im, n_re, n_im = products
    r_re, r_im = split_parts(residual)
    mh_re, mh_im = adjoint(m_re, m_im)
    g_re, g_im = complex_product(r_re, r_im, mh_re, mh_im)
    row_side = jnp.sum(join_parts(g_re, g_im), axis=1)
    rh_re, rh_im = adjoint(r_re, r_im)
    f_re, f_im = complex_product(rh_re, rh_im, n_re, n_im)
    col_side = jnp.sum(join_parts(f_re, f_im), axis=1)
    row_curv = jnp.sum(jnp.sum(m_re * m_re + m_im * m_im, axis=-2) * weight[None], axis=1)
    column_curvature = jnp.sum(jnp.sum(n_re * n_re + n_im * n_im, axis=-3) * weight[None], axis=1)
    lead = row_side.shape[0]
    grad_row = jnp.sum(row_side.reshape(lead, 8, SB, SB), axis=3)
    grad_col = jnp.sum(col_side.reshape(lead, 8, SB, SB), axis=2)
    curv_row = jnp.sum(row_curv.reshape(lead, 2, SB, SB), axis=3)
    curv_col = jnp.sum(column_curvature.reshape(lead, 2, SB, SB), axis=2)
    return (grad_row, grad_col, curv_row, curv_col)


def add_block(total, piece, block):
    offset = block * SB
    current = lax.dynamic_slice_in_dim(total, offset, SB, 2)
    return lax.dynamic_update_slice_in_dim(total, current + piece, offset, 2)


def component(value):
    return lax.broadcasted_iota(jnp.int32, value.shape, value.ndim - 2)


def turn(value, ahead):
    return pltpu.roll(value, (8 - ahead) % 8, value.ndim - 2)


def flip(value, mask):
    if mask == 4:
        return turn(value, 4)
    return jnp.where(component(value) & mask == 0, turn(value, mask), turn(value, 8 - mask))


def transpose_matrix(value):
    place = component(value) & 3
    return jnp.where(place == 1, turn(value, 1), jnp.where(place == 2, turn(value, 7), value))


def fold(values):
    values = [values[x] + flip(values[x + 1], 1) for x in range(0, 4, 2)]
    return values[0] + flip(values[1], 2)


def pair_parts(first, second):
    low = component(first) < 4
    return jnp.where(low, first, turn(second, 4)), jnp.where(low, turn(first, 4), second)


def add_all(sums, values):
    if sums is None:
        return values
    return [v if total is None else total + v for total, v in zip(sums, values)]


def halves(value):
    high = value.astype(jnp.bfloat16)
    return high, (value - high.astype(jnp.float32)).astype(jnp.bfloat16)


def station_of(baseline, row_side):
    return baseline // SB if row_side else baseline % SB


def one_hot(row_side, transposed):
    shape = (BASELINES, LANES) if transposed else (LANES, BASELINES)
    lane = lax.broadcasted_iota(jnp.int32, shape, 1 if transposed else 0)
    baseline = lax.broadcasted_iota(jnp.int32, shape, 0 if transposed else 1)
    return (lane == station_of(baseline, row_side)).astype(jnp.bfloat16)


def expand(blocks, row_side):
    made = []
    for packed in blocks:
        made.extend([packed] + [pltpu.roll(packed, LANES - 2 * SB * g, 1) for g in range(1, 4)])
    high, low = halves(jnp.concatenate(made, axis=0))
    both = jnp.concatenate([high, low], axis=1)
    chosen = jnp.concatenate([one_hot(row_side, False)] * 2, axis=0)
    wide = jnp.dot(both, chosen, preferred_element_type=jnp.float32)
    ends = [0]
    for packed in blocks:
        ends.append(ends[-1] + 4 * packed.shape[0])
    return [wide[start:end] for start, end in zip(ends, ends[1:])]


def station_sums(values, row_side):
    high, low = halves(values)
    both = jnp.concatenate([high, low], axis=0)
    total = jnp.dot(both, one_hot(row_side, True), preferred_element_type=jnp.float32)
    count = high.shape[0]
    return total[:count] + total[count:]


def to_lanes(parts, half):
    moved = [pltpu.roll(part, 2 * SB * g + SB * half, 1) for g, part in enumerate(parts)]
    return sum(moved[1:], moved[0])


def arranged(ref, tile, half, k, mask):
    row = lambda c: ref[tile, half, pl.ds(8 * k + c, 8, stride=0), :]
    first = lax.broadcasted_iota(jnp.int32, (8, LANES), 0) & mask == 0
    pick = lambda c, d: jnp.where(first, row(c), row(d))
    return (pick(0, 3), pick(2, 1)), (pick(4, 7), pick(6, 5))


def half_lanes(index):
    return pl.ds(pl.multiple_of(index * LANES, LANES), LANES)


def upper_mask(meta, tile):
    shape = (8, BASELINES)
    baseline = lax.broadcasted_iota(jnp.int32, shape, 1)
    above = entry(meta, tile, 2, shape) < entry(meta, tile, 3, shape)
    return jnp.where((baseline // SB < baseline % SB) | above, 1.0, 0.0).astype(jnp.float32)


def pack_kernel(jones_in_hbm, packed, jones, semaphore):
    copy = pltpu.make_async_copy(jones_in_hbm, jones, semaphore)
    copy.start()
    copy.wait()
    each = jones.shape[0] // 4
    rows = packed.shape[1]
    made = jnp.concatenate(
        [jones[g * each : (g + 1) * each].reshape(rows, 2 * SB) for g in range(4)], axis=1
    )
    for copy in range(packed.shape[0]):
        packed[copy] = made


def entry(meta, row, column, shape=(8, LANES)):
    return jnp.broadcast_to(meta[row : row + 1, column : column + 1], shape)


def station_block(meta, near, far, tile, side):
    block = entry(meta, tile, 2 + side)
    owner = block >> 1
    own_core = (owner ^ entry(meta, 0, 0)) & 1 == 0
    chips, rows = near.shape[:2]
    found = None
    for chip in range(chips):
        packed = jnp.where(own_core, near[chip].reshape(-1, 8, LANES), far[chip].reshape(-1, 8, LANES))
        found = packed if found is None else jnp.where(owner >> 1 == chip, packed, found)
    shifted = pltpu.roll(found.reshape(rows, LANES), LANES - SB, 1).reshape(found.shape)
    return jnp.where(block & 1 == 0, found, shifted).reshape(rows, LANES)


PIECES = 6
SPARE_ROWS = 8


def block_of(meta, tile, side):
    return meta[tile, 2 + side]


def valid_of(flags, tile, sample):
    return (1 - flags[tile, sample // FREQ_CHANNELS]).astype(jnp.float32)


def sides(meta, tiles):
    return [[block_of(meta, tile, side) for tile in range(tiles)] for side in range(2)]


def pieces(source, target, semaphores):
    each = source.shape[0] // PIECES
    parts = [pl.ds(n * each, each) for n in range(PIECES)]
    return [
        pltpu.make_async_copy(source.at[part], target.at[part], semaphores.at[n])
        for n, part in enumerate(parts)
    ]


def moment_kernel(
    flags_in_hbm, source, moments_out, pairs,
    flags, coherency, moments, semaphores, flag_semaphore, out_semaphores,
):
    tiles, directions, samples = source.shape[:3]
    each = directions // PIECES
    flag_copy = pltpu.make_async_copy(flags_in_hbm, flags, flag_semaphore)
    flag_copy.start()
    copies = [pieces(source.at[t], coherency.at[t], semaphores.at[t]) for t in range(tiles)]
    for copy in sum(copies, []):
        copy.start()
    flag_copy.wait()
    sent = []
    for tile in range(tiles):

        def add_direction(k, _):
            rows = pl.ds(pl.multiple_of(8 * k, 8), 8)
            for half in range(2):
                lanes = slice(half * LANES, (half + 1) * LANES)
                sums = [jnp.zeros((8, LANES), jnp.float32)] * 4
                for s in range(samples):
                    c = coherency[tile, k, s, :, lanes].astype(jnp.float32)
                    weighted = valid_of(flags, tile, s) * c
                    sums = [v + weighted * (turn(c, n) if n else c) for n, v in enumerate(sums)]
                    if s % 2 == 1:
                        both = jnp.concatenate(pair_parts(before, c), axis=0)
                        pairs[tile, k, s // 2, :, lanes] = both.astype(pairs.dtype)
                    before = c
                for n in range(4):
                    moments[tile, n, rows, lanes] = sums[n]
            return 0

        for n, copy in enumerate(copies[tile]):
            copy.wait()
            lax.fori_loop(n * each, (n + 1) * each, add_direction, 0)
            rows = pl.ds(8 * n * each, 8 * each)
            sent.append(
                pltpu.make_async_copy(
                    moments.at[tile, :, rows],
                    moments_out.at[tile, :, rows],
                    out_semaphores.at[tile, n],
                )
            )
            sent[-1].start()
    for copy in sent:
        copy.wait()


def station_products(packed):
    e = packed.reshape(-1, 8, LANES)
    bits = component(e)
    part = bits >= 4
    second = bits & 1 != 0
    spread = lambda v: (lambda u: u + flip(u, 2))(v + flip(v, 4))
    across = flip(e, 1)
    squares = spread(e * e)
    cross_re = 2.0 * spread(e * across)
    sign = jnp.where(part == second, 1.0, -1.0)
    cross_im = 2.0 * spread(sign * (e * flip(across, 4)))
    made = jnp.where(bits & 2 == 0, squares, jnp.where(second, cross_im, cross_re))
    low = component(made[0]) < 4
    joined = [jnp.where(low, made[n], made[n + 1]) for n in range(0, made.shape[0], 2)]
    return jnp.concatenate(joined, axis=0)


def first_model_kernel(meta, near, far, narrow, model, row_jones, col_jones, paired, weight):
    tiles = narrow.shape[0]
    for side, jones in enumerate((row_jones, col_jones)):
        found = [station_block(meta, near, far, tile, side) for tile in range(tiles)]
        for tile, made in enumerate(expand(found, side == 0)):
            for half in range(2):
                lanes = slice(half * LANES, (half + 1) * LANES)
                jones[tile, half, : made.shape[0]] = made[:, lanes]
    models(0, narrow, row_jones, col_jones, model, paired, weight)


def next_model_kernel(tile, narrow, row_jones, col_jones, model, paired, weight):
    models(tile, narrow, row_jones, col_jones, model, paired, weight)


def models(tile, narrow, row_jones, col_jones, model, paired, weight):
    directions, pairs = paired.shape[:2]

    def weigh(k, _):
        for half in range(2):
            lanes = slice(half * LANES, (half + 1) * LANES)
            p_re, p_im = arranged(row_jones, tile, half, k, 2)
            q_re, q_im = arranged(col_jones, tile, half, k, 1)
            for x in range(4):
                a, b = x // 2, x % 2
                z_re = p_re[a] * q_re[b] + p_im[a] * q_im[b]
                z_im = p_im[a] * q_re[b] - p_re[a] * q_im[b]
                weight[k, 3 * x, :, lanes] = z_re
                weight[k, 3 * x + 1, :, lanes] = z_im - z_re
                weight[k, 3 * x + 2, :, lanes] = z_re + z_im
        return 0

    lax.fori_loop(0, directions, weigh, 0, unroll=8)

    def add_samples(step, _):
        lanes = half_lanes(step % 2)
        first = step // 2 * CHUNK
        zero = jnp.zeros((8, LANES), jnp.float32)
        low = component(zero) < 4
        sums = [None] * 12
        for k in range(directions):
            parts = []
            for i in range(CHUNK):
                both = narrow[tile, k, first + i, :, lanes].astype(jnp.float32)
                real, imag = both[:8], both[8:]
                paired[k, first + i, 0, :, lanes] = real
                paired[k, first + i, 1, :, lanes] = imag
                parts.append((real + imag, real, imag))
            for n in range(12):
                w = weight[k, n, :, lanes]
                sums[n] = add_all(sums[n], [w * parts[i][n % 3] for i in range(CHUNK)])
        for i in range(CHUNK):
            one, two, three = ([sums[3 * x + m][i] for x in range(4)] for m in range(3))
            real = fold([one[x] - three[x] for x in range(4)])
            imag = fold([one[x] + two[x] for x in range(4)])
            place = 2 * (first + i)
            model[place, :, lanes] = jnp.where(low, real, turn(imag, 4))
            model[place + 1, :, lanes] = jnp.where(low, turn(real, 4), imag)
        return 0

    lax.fori_loop(0, 2 * pairs // CHUNK, add_samples, 0, unroll=4)


def curvature_kernel(meta, near, far, moments, terms, masks, products):
    tiles = moments.shape[0]
    directions = moments.shape[2] // 8
    for tile in range(tiles):
        masks[tile, 0] = upper_mask(meta, tile)
        for time in range(masks.shape[1] - 1):
            valid = (1 - entry(meta, tile, 4 + time, (8, BASELINES))).astype(jnp.float32)
            masks[tile, 1 + time] = valid * masks[tile, 0]
    for side in range(2):
        found = [station_block(meta, near, far, tile, side) for tile in range(tiles)]
        made = expand([station_products(packed) for packed in found], side == 0)
        for tile in range(tiles):
            for half in range(2):
                lanes = slice(half * LANES, (half + 1) * LANES)
                products[tile, side, half, : made[tile].shape[0]] = made[tile][:, lanes]

    def combine(step, _):
        tile, group = step // (directions // 4), step % (directions // 4)
        mask = masks[tile, 0]
        bits = component(mask[:, :LANES])
        odd = bits & 1 != 0
        upper = bits & 2 != 0
        sign = jnp.where(bits < 4, -1.0, 1.0)
        member = (bits >> 2) * 2 + (bits & 1)
        for half in range(2):
            lanes = slice(half * LANES, (half + 1) * LANES)
            found = [None, None]
            for i in range(4):
                k = 4 * group + i
                rows = pl.ds(pl.multiple_of(8 * k, 8), 8)
                m = [moments[tile, n, rows, lanes] for n in range(4)]
                row = lambda side, n: products[tile, side, half, pl.ds(4 * k + n, 8, stride=0), :]
                h = [row(1, n) for n in range(4)]
                row_sum = m[0] * jnp.where(odd, h[1], h[0])
                row_sum = row_sum + jnp.where(odd, sign * (m[3] * h[3]), m[1] * h[2])
                h = [row(0, n) for n in range(4)]
                col_sum = m[0] * jnp.where(upper, h[1], h[0])
                col_sum = col_sum + m[2] * jnp.where(upper, -sign * h[3], h[2])
                row_sum = row_sum + turn(row_sum, 4)
                row_sum = row_sum + flip(row_sum, 1)
                col_sum = transpose_matrix(col_sum)
                col_sum = col_sum + turn(col_sum, 4)
                col_sum = col_sum + flip(col_sum, 1)
                for side, v in enumerate((row_sum, col_sum)):
                    found[side] = v if i == 0 else jnp.where(member == i, v, found[side])
            for side in range(2):
                place = pl.ds(pl.multiple_of(8 * group, 8), 8)
                terms[side, tile, place, lanes] = mask[:, lanes] * found[side]
        return 0

    lax.fori_loop(0, tiles * directions // 4, combine, 0, unroll=3)


def add_to_owner(meta, near, far, block, rows, part):
    owner = block // 2
    own_core = jnp.where(owner % 2 == meta[0, 0] % 2, 1.0, 0.0)
    near[owner // 2, rows] = near[owner // 2, rows] + own_core * part
    far[owner // 2, rows] = far[owner // 2, rows] + (1.0 - own_core) * part


def gradient_block(sums, half, side):
    part = to_lanes(jnp.split(sums, 4, axis=0), half).reshape(-1, 8, LANES)
    if side == 0:
        part = transpose_matrix(part)
    else:
        part = jnp.where(component(part) < 4, part, -part)
    return part.reshape(-1, LANES)


def add_gradient_terms(
    tile, meta, masks, observed, mine, other, row_jones, col_jones, paired,
    residual_out, terms, residual, turned, semaphore,
):
    directions, pairs = paired.shape[:2]
    first_half = entry(meta, 0, 1) == 0
    for i in range(pairs):
        both = []
        for s in (2 * i, 2 * i + 1):
            summed = mine[s] + other[s]
            weight = masks[tile, 1 + s // FREQ_CHANNELS]
            r = weight * (observed[tile, s].astype(jnp.float32) - summed)
            residual[s] = jnp.where(first_half, r[:, :LANES], r[:, LANES:])
            both.append(r)
        made = [pair_parts(*both)]
        for x in range(1, 4):
            bit = x & -x
            made.append(tuple(flip(v, bit) for v in made[x - bit]))
        for x, (real, imag) in enumerate(made):
            turned[i, 3 * x] = real
            turned[i, 3 * x + 1] = real + imag
            turned[i, 3 * x + 2] = real - imag
    sent = pltpu.make_async_copy(residual, residual_out.at[tile], semaphore)
    sent.start()

    def add_directions(step, _):
        half, lanes = step % 2, half_lanes(step % 2)
        first = step // 2 * CHUNK
        zero = jnp.zeros((8, LANES), jnp.float32)
        sums = [None] * 12
        for p in range(pairs):
            parts = []
            for i in range(CHUNK):
                real = paired[first + i, p, 0, :, lanes]
                imag = paired[first + i, p, 1, :, lanes]
                parts.append((real + imag, real, imag))
            for n in range(12):
                r = turned[p, n, :, lanes]
                sums[n] = add_all(sums[n], [r * parts[i][n % 3] for i in range(CHUNK)])
        bits = component(zero)
        real = bits < 4
        equal = (bits >> 1) & 1 == bits & 1
        for i in range(CHUNK):
            k = first + i
            p_re, p_im = arranged(row_jones, tile, half, k, 2)
            q_re, q_im = arranged(col_jones, tile, half, k, 1)
            row_sum = [None, None]
            col_sum = [None, None]
            for x in range(4):
                a, b = x // 2, x % 2
                y_re = sums[3 * x][i] - sums[3 * x + 2][i]
                y_im = sums[3 * x + 1][i] - sums[3 * x][i]
                y_re = y_re + turn(y_re, 4)
                y_im = y_im + turn(y_im, 4)
                one, two = jnp.where(real, y_re, y_im), jnp.where(real, -y_im, y_re)
                (row_sum[a],) = add_all(row_sum[a : a + 1], [q_re[b] * one + q_im[b] * two])
                (col_sum[b],) = add_all(col_sum[b : b + 1], [p_re[a] * one - p_im[a] * two])
            rows = pl.ds(pl.multiple_of(8 * k, 8), 8)
            g, h = row_sum
            g = jnp.where(equal, g, h) + flip(jnp.where(equal, h, g), 1)
            terms[0, rows, lanes] = g
            g, h = col_sum
            g = jnp.where(equal, g, h) + flip(jnp.where(equal, h, g), 2)
            terms[1, rows, lanes] = g
        return 0

    lax.fori_loop(0, 2 * directions // CHUNK, add_directions, 0, unroll=4)
    return sent


def first_gradient_kernel(
    meta_in_vmem, curvature_terms, masks, observed, mine, other, row_jones, col_jones, paired,
    residual_out, near, far, terms, residual, turned, semaphore, meta, meta_semaphore,
):
    meta_copy = pltpu.make_async_copy(meta_in_vmem, meta, meta_semaphore)
    meta_copy.start()
    sent = add_gradient_terms(
        0, meta_in_vmem, masks, observed, mine, other, row_jones, col_jones, paired,
        residual_out, terms, residual, turned, semaphore,
    )
    near[...] = jnp.zeros_like(near)
    far[...] = jnp.zeros_like(far)
    meta_copy.wait()
    tiles, directions = curvature_terms.shape[1], paired.shape[0]
    rows, few = 8 * directions, 2 * directions
    for side, blocks in enumerate(sides(meta, tiles)):
        stack = [terms[side], *(curvature_terms[side, tile] for tile in range(tiles))]
        sums = station_sums(jnp.concatenate(stack, axis=0), side == 0)
        part = gradient_block(sums[:rows], blocks[0] % 2, side)
        add_to_owner(meta, near, far, blocks[0], slice(0, few), part)
        for tile, block in enumerate(blocks):
            start = rows + tile * few
            groups = jnp.split(sums[start : start + few], directions // 4, axis=0)
            chosen = [groups[n : n + 4] for n in range(0, len(groups), 4)]
            made = [to_lanes(parts, block % 2) for parts in chosen]
            part = jnp.concatenate(made, axis=0)
            add_to_owner(meta, near, far, block, slice(few, None), part)
    sent.wait()


def last_gradient_kernel(
    tiles, meta_in_vmem, near_before, far_before,
    masks, observed, mine, other, row_jones, col_jones, paired,
    residual_before, residual_out, near, far, terms, residual, turned, semaphore,
    meta, meta_semaphore,
):
    del residual_before, near_before, far_before
    meta_copy = pltpu.make_async_copy(meta_in_vmem, meta, meta_semaphore)
    meta_copy.start()
    sent = add_gradient_terms(
        tiles - 1, meta_in_vmem, masks, observed, mine, other, row_jones, col_jones, paired,
        residual_out, terms, residual, turned, semaphore,
    )
    meta_copy.wait()
    for side in range(2):
        block = block_of(meta, tiles - 1, side)
        part = gradient_block(station_sums(terms[side], side == 0), block % 2, side)
        add_to_owner(meta, near, far, block, slice(0, part.shape[0]), part)
    sent.wait()


def finish_kernel(normalizer, parts, gradient, curvature):
    total = sum((parts[x] for x in range(1, parts.shape[0])), parts[0]) * normalizer
    directions = gradient.shape[0]
    rows, each = 2 * directions, directions // 4
    grad = total[:rows].reshape(each, 8, LANES)
    for g in range(4):
        gradient[g * each : (g + 1) * each] = grad[:, :, 2 * SB * g : 2 * SB * (g + 1)]
    for k in range(directions):
        group, member = k // 4, k % 4
        start = rows + group // 4 * 8 + member // 2 * 4 + member % 2
        lane = group % 4 * 2 * SB
        for c in range(2):
            row = total[start + 2 * c : start + 2 * c + 1]
            curvature[k, c : c + 1] = row[:, lane : lane + 2 * SB]


def call(kernel, scalars, arrays, in_hbm, results, scratch=(), to_hbm=(), aliases=None, cost=None):
    place = lambda space: pl.BlockSpec(memory_space=space)
    spaces = [pltpu.SMEM] * len(scalars) + [pltpu.VMEM] * len(arrays) + [pltpu.HBM] * len(in_hbm)
    return pl.pallas_call(
        kernel,
        in_specs=[place(space) for space in spaces],
        out_specs=[place(pltpu.HBM)] * len(to_hbm) + [place(pltpu.VMEM)] * len(results),
        out_shape=[
            *(pltpu.HBM(shape, jnp.float32) for shape in to_hbm),
            *(pltpu.VMEM(getattr(v, "shape", v), getattr(v, "dtype", jnp.float32)) for v in results),
        ],
        scratch_shapes=list(scratch),
        input_output_aliases=aliases or {},
        cost_estimate=cost,
        compiler_params=pltpu.CompilerParams(vmem_limit_bytes=32 * 1024 * 1024),
    )(*scalars, *arrays, *(pltpu.with_memory_space_constraint(v, pltpu.HBM) for v in in_hbm))


def swap_with(value, axis, mask):
    size = lax.axis_size(axis)
    return lax.ppermute(value, axis, [(place, place ^ mask) for place in range(size)])


def trade(slots):
    size = lax.axis_size("tile")
    groups = [list(range(core, size, 2)) for core in range(2)]
    return lax.all_to_all(slots, "tile", 0, 0, axis_index_groups=groups, tiled=True)


def body_kernels(coherency, observed, flags, tile_map, jones):
    tiles, directions, samples = coherency.shape[:3]
    chips = lax.axis_size("tile") // 2
    rows = 2 * directions
    extra = -(-directions // 16) * 8
    place = [
        jnp.full((tiles, 1), lax.axis_index(axis), jnp.int32) for axis in ("tile", "dir")
    ]
    meta = jnp.concatenate([*place, tile_map, flags], axis=1)

    def memory(*shape, kind=jnp.float32):
        return pltpu.VMEM(shape, kind)

    (packed,) = call(
        pack_kernel,
        [],
        [],
        [jones],
        [(chips, rows, LANES)],
        [memory(*jones.shape), pltpu.SemaphoreType.DMA],
    )
    near = trade(packed)
    narrow = (tiles, directions, samples // 2, 16, BASELINES)
    moments, narrow = call(
        moment_kernel,
        [],
        [],
        [flags, coherency],
        [jax.ShapeDtypeStruct(narrow, coherency.dtype)],
        [
            pltpu.SMEM(flags.shape, flags.dtype),
            memory(*coherency.shape, kind=coherency.dtype),
            memory(tiles, 4, 4 * rows, BASELINES),
            pltpu.SemaphoreType.DMA((tiles, PIECES)),
            pltpu.SemaphoreType.DMA,
            pltpu.SemaphoreType.DMA((tiles, PIECES)),
        ],
        [(tiles, 4, 4 * rows, BASELINES)],
        cost=pl.CostEstimate(
            flops=10 * coherency.size, bytes_accessed=4 * coherency.size, transcendentals=0
        ),
    )
    far = swap_with(near, "tile", 1)

    expanded = (tiles, 2, 4 * rows + SPARE_ROWS, LANES)
    of_tile = [(samples, 8, BASELINES), (directions, samples // 2, 2, 8, BASELINES)]
    narrow = pltpu.with_memory_space_constraint(narrow, pltpu.VMEM)
    weight = memory(directions, 12, 8, BASELINES)
    model, row_jones, col_jones, paired = call(
        first_model_kernel,
        [],
        [meta, near, far, narrow],
        [],
        [
            of_tile[0],
            expanded,
            expanded,
            of_tile[1],
        ],
        [weight],
    )
    first = [model, swap_with(model, "dir", 1), row_jones, col_jones, paired]
    model, paired = call(
        functools.partial(next_model_kernel, 1),
        [],
        [narrow, row_jones, col_jones],
        [],
        of_tile,
        [weight],
    )
    last = [model, swap_with(model, "dir", 1), row_jones, col_jones, paired]

    residual_shape = (tiles, samples, 8, LANES)
    terms = (2, 4 * rows, BASELINES)
    scratch = [
        memory(samples, 8, LANES),
        memory(samples // 2, 12, 8, BASELINES),
        pltpu.SemaphoreType.DMA,
    ]
    curvature_terms, masks = call(
        curvature_kernel,
        [],
        [meta, near, far, moments],
        [],
        [(2, tiles, 2 * directions, BASELINES), (tiles, 1 + flags.shape[1], 8, BASELINES)],
        [memory(tiles, 2, 2, 4 * directions + SPARE_ROWS, LANES)],
        cost=pl.CostEstimate(
            flops=coherency.size, bytes_accessed=coherency.size, transcendentals=0
        ),
    )
    scratch = [
        memory(*terms),
        *scratch,
        pltpu.SMEM(meta.shape, meta.dtype),
        pltpu.SemaphoreType.DMA,
    ]
    slots = (chips, rows + extra, LANES)
    residual, near, far = call(
        first_gradient_kernel,
        [],
        [meta, curvature_terms, masks, observed, *first],
        [],
        [slots, slots],
        scratch,
        [residual_shape],
    )
    residual, near, far = call(
        functools.partial(last_gradient_kernel, tiles),
        [],
        [meta, near, far, masks, observed, *last],
        [residual],
        [slots, slots],
        scratch,
        [residual_shape],
        {10: 0, 1: 1, 2: 2},
    )
    parts = trade(near + swap_with(far, "tile", 1))
    directions, _, owned = jones.shape
    in_vmem = pl.BlockSpec(memory_space=pltpu.VMEM)
    gradient, curvature = pl.pallas_call(
        functools.partial(finish_kernel, 1.0 / (samples * SB)),
        in_specs=[in_vmem],
        out_specs=[in_vmem] * 2,
        out_shape=[
            jax.ShapeDtypeStruct(jones.shape, jnp.float32),
            jax.ShapeDtypeStruct((directions, 2, owned), jnp.float32),
        ],
        compiler_params=pltpu.CompilerParams(vmem_limit_bytes=32 * 1024 * 1024),
    )(parts)
    return residual, gradient, curvature


def body(coherency, observed, flags, tile_map, jones):
    jones_all = lax.all_gather(jones, "tile", axis=2, tiled=True)
    how_many = coherency.shape[0]
    predictions = []
    products_list = []
    weight_list = []
    for number in range(how_many):
        predicted, products = tile_terms(
            coherency[number].astype(jnp.float32), jones_all, tile_map[number]
        )
        predictions.append(predicted)
        products_list.append(products)
        weight_list.append(weights(flags[number], tile_map[number]))
    partial_value = jnp.stack(predictions)
    weight = jnp.stack(weight_list)
    columns = observed.shape[3]
    portion = columns // lax.axis_size("dir")
    offset = lax.axis_index("dir") * portion
    summed = lax.psum(partial_value, "dir")
    residual = weight * (observed.astype(jnp.float32) - summed)
    residual_mine = lax.dynamic_slice_in_dim(residual, offset, portion, 3)
    grad_total = jnp.zeros((jones_all.shape[0], 8, jones_all.shape[2]), jnp.float32)
    curv_total = jnp.zeros((jones_all.shape[0], 2, jones_all.shape[2]), jnp.float32)
    for number in range(how_many):
        grad_row, grad_col, curv_row, curv_col = station_terms(
            residual[number], weight[number], products_list[number]
        )
        block_pair = tile_map[number]
        grad_total = add_block(
            add_block(grad_total, grad_row, block_pair[0]), grad_col, block_pair[1]
        )
        curv_total = add_block(
            add_block(curv_total, curv_row, block_pair[0]), curv_col, block_pair[1]
        )
    grad_owned, curv_owned = (
        lax.psum_scatter(grad_total, "tile", scatter_dimension=2, tiled=True),
        lax.psum_scatter(curv_total, "tile", scatter_dimension=2, tiled=True),
    )
    normalizer = 1.0 / (observed.shape[1] * SB)
    return (residual_mine, grad_owned * normalizer, curv_owned * normalizer)


def solution(mesh):
    specs = dict(
        mesh=mesh,
        in_specs=(
            P("tile", "dir", None, None, None),
            P("tile", None, None, None),
            P("tile", None),
            P("tile", None),
            P("dir", None, "tile"),
        ),
        out_specs=(P("tile", None, None, "dir"), P("dir", None, "tile"), P("dir", None, "tile")),
        check_vma=False,
    )

    def run(coherency, observed, flags, tile_map, jones):
        owned = jones.shape[2] // mesh.shape["tile"]
        directions = jones.shape[0] // mesh.shape["dir"]
        fits = owned == 2 * SB and directions == 24
        paired = mesh.shape["dir"] == 2 and mesh.shape["tile"] == 16
        paired = paired and coherency.shape[0] == 2 * mesh.shape["tile"]
        chosen = body_kernels if fits and paired else body
        return jax.shard_map(chosen, **specs)(coherency, observed, flags, tile_map, jones)

    return run
```

```python
import functools

import jax
import jax.numpy as jnp
from jax import lax
from jax.experimental import pallas as pl
from jax.experimental.pallas import tpu as pltpu
from jax.sharding import PartitionSpec as P

SB = 16
FREQ_CHANNELS = 4
LANES = 128
BASELINES = SB * SB
CHUNK = 3


def split_parts(values):
    shape = values.shape[:-2] + (2, 2, values.shape[-1])
    return (values[..., 0:4, :].reshape(shape), values[..., 4:8, :].reshape(shape))


def join_parts(re_part, im_part):
    shape = re_part.shape[:-3] + (4, re_part.shape[-1])
    return jnp.concatenate([re_part.reshape(shape), im_part.reshape(shape)], axis=-2)


def complex_product(left_re, left_im, right_re, right_im):
    lre = left_re[..., :, :, None, :]
    lim = left_im[..., :, :, None, :]
    rre = right_re[..., None, :, :, :]
    rim = right_im[..., None, :, :, :]
    return (jnp.sum(lre * rre - lim * rim, axis=-3), jnp.sum(lre * rim + lim * rre, axis=-3))


def adjoint(re_part, im_part):
    return (jnp.swapaxes(re_part, -3, -2), -jnp.swapaxes(im_part, -3, -2))


def weights(row_flag_mask, block_pair):
    valid_samples = jnp.repeat((1 - row_flag_mask).astype(jnp.float32), FREQ_CHANNELS)
    baseline = jnp.arange(SB * SB, dtype=jnp.int32)
    inner_row = baseline // SB
    inner_col = baseline % SB
    upper_triangle_pairs = jnp.where(
        (block_pair[0] < block_pair[1]) | (inner_row < inner_col), 1.0, 0.0
    ).astype(jnp.float32)
    return valid_samples[:, None, None] * upper_triangle_pairs[None, None, :]


def tile_terms(coher, jones_all, block_pair):
    row_gain_matrix = lax.dynamic_slice_in_dim(jones_all, block_pair[0] * SB, SB, 2)
    col_jones = lax.dynamic_slice_in_dim(jones_all, block_pair[1] * SB, SB, 2)
    first_antenna = jnp.repeat(row_gain_matrix, SB, axis=2)[:, None]
    station_q = jnp.tile(col_jones, (1, 1, SB))[:, None]
    coh_re, coh_im = split_parts(coher)
    p_re, p_im = split_parts(first_antenna)
    q_re, q_im = split_parts(station_q)
    qh_re, qh_im = adjoint(q_re, q_im)
    m_re, m_im = complex_product(coh_re, coh_im, qh_re, qh_im)
    n_re, n_im = complex_product(p_re, p_im, coh_re, coh_im)
    v_re, v_im = complex_product(p_re, p_im, m_re, m_im)
    predicted = jnp.sum(join_parts(v_re, v_im), axis=0)
    return (predicted, (m_re, m_im, n_re, n_im))


def station_terms(residual, weight, products):
    m_re, m_im, n_re, n_im = products
    r_re, r_im = split_parts(residual)
    mh_re, mh_im = adjoint(m_re, m_im)
    g_re, g_im = complex_product(r_re, r_im, mh_re, mh_im)
    row_side = jnp.sum(join_parts(g_re, g_im), axis=1)
    rh_re, rh_im = adjoint(r_re, r_im)
    f_re, f_im = complex_product(rh_re, rh_im, n_re, n_im)
    col_side = jnp.sum(join_parts(f_re, f_im), axis=1)
    row_curv = jnp.sum(jnp.sum(m_re * m_re + m_im * m_im, axis=-2) * weight[None], axis=1)
    column_curvature = jnp.sum(jnp.sum(n_re * n_re + n_im * n_im, axis=-3) * weight[None], axis=1)
    lead = row_side.shape[0]
    grad_row = jnp.sum(row_side.reshape(lead, 8, SB, SB), axis=3)
    grad_col = jnp.sum(col_side.reshape(lead, 8, SB, SB), axis=2)
    curv_row = jnp.sum(row_curv.reshape(lead, 2, SB, SB), axis=3)
    curv_col = jnp.sum(column_curvature.reshape(lead, 2, SB, SB), axis=2)
    return (grad_row, grad_col, curv_row, curv_col)


def add_block(total, piece, block):
    offset = block * SB
    current = lax.dynamic_slice_in_dim(total, offset, SB, 2)
    return lax.dynamic_update_slice_in_dim(total, current + piece, offset, 2)


def component(value):
    return lax.broadcasted_iota(jnp.int32, value.shape, value.ndim - 2)


def turn(value, ahead):
    return pltpu.roll(value, (8 - ahead) % 8, value.ndim - 2)


def flip(value, mask):
    if mask == 4:
        return turn(value, 4)
    return jnp.where(component(value) & mask == 0, turn(value, mask), turn(value, 8 - mask))


def transpose_matrix(value):
    place = component(value) & 3
    return jnp.where(place == 1, turn(value, 1), jnp.where(place == 2, turn(value, 7), value))


def fold(values):
    values = [values[x] + flip(values[x + 1], 1) for x in range(0, 4, 2)]
    return values[0] + flip(values[1], 2)


def pair_parts(first, second):
    low = component(first) < 4
    return jnp.where(low, first, turn(second, 4)), jnp.where(low, turn(first, 4), second)


def add_all(sums, values):
    if sums is None:
        return values
    return [v if total is None else total + v for total, v in zip(sums, values)]


def halves(value):
    high = value.astype(jnp.bfloat16)
    return high, (value - high.astype(jnp.float32)).astype(jnp.bfloat16)


def station_of(baseline, row_side):
    return baseline // SB if row_side else baseline % SB


def one_hot(row_side, transposed):
    shape = (BASELINES, LANES) if transposed else (LANES, BASELINES)
    lane = lax.broadcasted_iota(jnp.int32, shape, 1 if transposed else 0)
    baseline = lax.broadcasted_iota(jnp.int32, shape, 0 if transposed else 1)
    return (lane == station_of(baseline, row_side)).astype(jnp.bfloat16)


def expand(blocks, row_side):
    made = []
    for packed in blocks:
        made.extend([packed] + [pltpu.roll(packed, LANES - 2 * SB * g, 1) for g in range(1, 4)])
    high, low = halves(jnp.concatenate(made, axis=0))
    both = jnp.concatenate([high, low], axis=1)
    chosen = jnp.concatenate([one_hot(row_side, False)] * 2, axis=0)
    wide = jnp.dot(both, chosen, preferred_element_type=jnp.float32)
    ends = [0]
    for packed in blocks:
        ends.append(ends[-1] + 4 * packed.shape[0])
    return [wide[start:end] for start, end in zip(ends, ends[1:])]


def station_sums(values, row_side):
    high, low = halves(values)
    both = jnp.concatenate([high, low], axis=0)
    total = jnp.dot(both, one_hot(row_side, True), preferred_element_type=jnp.float32)
    count = high.shape[0]
    return total[:count] + total[count:]


def to_lanes(parts, half):
    moved = [pltpu.roll(part, 2 * SB * g + SB * half, 1) for g, part in enumerate(parts)]
    return sum(moved[1:], moved[0])


def arranged(ref, tile, half, k, mask):
    row = lambda c: ref[tile, half, pl.ds(8 * k + c, 8, stride=0), :]
    first = lax.broadcasted_iota(jnp.int32, (8, LANES), 0) & mask == 0
    pick = lambda c, d: jnp.where(first, row(c), row(d))
    return (pick(0, 3), pick(2, 1)), (pick(4, 7), pick(6, 5))


def half_lanes(index):
    return pl.ds(pl.multiple_of(index * LANES, LANES), LANES)


def upper_mask(meta, tile):
    shape = (8, BASELINES)
    baseline = lax.broadcasted_iota(jnp.int32, shape, 1)
    above = entry(meta, tile, 2, shape) < entry(meta, tile, 3, shape)
    return jnp.where((baseline // SB < baseline % SB) | above, 1.0, 0.0).astype(jnp.float32)


def pack_kernel(jones_in_hbm, packed, jones, semaphore):
    copy = pltpu.make_async_copy(jones_in_hbm, jones, semaphore)
    copy.start()
    copy.wait()
    each = jones.shape[0] // 4
    rows = packed.shape[1]
    made = jnp.concatenate(
        [jones[g * each : (g + 1) * each].reshape(rows, 2 * SB) for g in range(4)], axis=1
    )
    for copy in range(packed.shape[0]):
        packed[copy] = made


def entry(meta, row, column, shape=(8, LANES)):
    return jnp.broadcast_to(meta[row : row + 1, column : column + 1], shape)


def station_block(meta, near, far, tile, side):
    block = entry(meta, tile, 2 + side)
    owner = block >> 1
    own_core = (owner ^ entry(meta, 0, 0)) & 1 == 0
    chips, rows = near.shape[:2]
    found = None
    for chip in range(chips):
        packed = jnp.where(own_core, near[chip].reshape(-1, 8, LANES), far[chip].reshape(-1, 8, LANES))
        found = packed if found is None else jnp.where(owner >> 1 == chip, packed, found)
    shifted = pltpu.roll(found.reshape(rows, LANES), LANES - SB, 1).reshape(found.shape)
    return jnp.where(block & 1 == 0, found, shifted).reshape(rows, LANES)


PIECES = 6
SPARE_ROWS = 8


def block_of(meta, tile, side):
    return meta[tile, 2 + side]


def valid_of(flags, tile, sample):
    return (1 - flags[tile, sample // FREQ_CHANNELS]).astype(jnp.float32)


def sides(meta, tiles):
    return [[block_of(meta, tile, side) for tile in range(tiles)] for side in range(2)]


def pieces(source, target, semaphores):
    each = source.shape[0] // PIECES
    parts = [pl.ds(n * each, each) for n in range(PIECES)]
    return [
        pltpu.make_async_copy(source.at[part], target.at[part], semaphores.at[n])
        for n, part in enumerate(parts)
    ]


def moment_kernel(
    flags_in_hbm, source, moments_out, pairs,
    flags, coherency, moments, semaphores, flag_semaphore, out_semaphores,
):
    tiles, directions, samples = source.shape[:3]
    each = directions // PIECES
    flag_copy = pltpu.make_async_copy(flags_in_hbm, flags, flag_semaphore)
    flag_copy.start()
    copies = [pieces(source.at[t], coherency.at[t], semaphores.at[t]) for t in range(tiles)]
    for copy in sum(copies, []):
        copy.start()
    flag_copy.wait()
    sent = []
    for tile in range(tiles):

        def add_direction(k, _):
            rows = pl.ds(pl.multiple_of(8 * k, 8), 8)
            for half in range(2):
                lanes = slice(half * LANES, (half + 1) * LANES)
                sums = [jnp.zeros((8, LANES), jnp.float32)] * 4
                for s in range(samples):
                    c = coherency[tile, k, s, :, lanes].astype(jnp.float32)
                    weighted = valid_of(flags, tile, s) * c
                    sums = [v + weighted * (turn(c, n) if n else c) for n, v in enumerate(sums)]
                    if s % 2 == 1:
                        both = jnp.concatenate(pair_parts(before, c), axis=0)
                        pairs[tile, k, s // 2, :, lanes] = both.astype(pairs.dtype)
                    before = c
                for n in range(4):
                    moments[tile, n, rows, lanes] = sums[n]
            return 0

        for n, copy in enumerate(copies[tile]):
            copy.wait()
            lax.fori_loop(n * each, (n + 1) * each, add_direction, 0)
            rows = pl.ds(8 * n * each, 8 * each)
            sent.append(
                pltpu.make_async_copy(
                    moments.at[tile, :, rows],
                    moments_out.at[tile, :, rows],
                    out_semaphores.at[tile, n],
                )
            )
            sent[-1].start()
    for copy in sent:
        copy.wait()


def station_products(packed):
    e = packed.reshape(-1, 8, LANES)
    bits = component(e)
    part = bits >= 4
    second = bits & 1 != 0
    spread = lambda v: (lambda u: u + flip(u, 2))(v + flip(v, 4))
    across = flip(e, 1)
    squares = spread(e * e)
    cross_re = 2.0 * spread(e * across)
    sign = jnp.where(part == second, 1.0, -1.0)
    cross_im = 2.0 * spread(sign * (e * flip(across, 4)))
    made = jnp.where(bits & 2 == 0, squares, jnp.where(second, cross_im, cross_re))
    low = component(made[0]) < 4
    joined = [jnp.where(low, made[n], made[n + 1]) for n in range(0, made.shape[0], 2)]
    return jnp.concatenate(joined, axis=0)


def first_model_kernel(meta, near, far, narrow, model, row_jones, col_jones, paired, weight):
    tiles = narrow.shape[0]
    for side, jones in enumerate((row_jones, col_jones)):
        found = [station_block(meta, near, far, tile, side) for tile in range(tiles)]
        for tile, made in enumerate(expand(found, side == 0)):
            for half in range(2):
                lanes = slice(half * LANES, (half + 1) * LANES)
                jones[tile, half, : made.shape[0]] = made[:, lanes]
    models(0, narrow, row_jones, col_jones, model, paired, weight)


def next_model_kernel(tile, narrow, row_jones, col_jones, model, paired, weight):
    models(tile, narrow, row_jones, col_jones, model, paired, weight)


def models(tile, narrow, row_jones, col_jones, model, paired, weight):
    directions, pairs = paired.shape[:2]

    def weigh(k, _):
        for half in range(2):
            lanes = slice(half * LANES, (half + 1) * LANES)
            p_re, p_im = arranged(row_jones, tile, half, k, 2)
            q_re, q_im = arranged(col_jones, tile, half, k, 1)
            for x in range(4):
                a, b = x // 2, x % 2
                z_re = p_re[a] * q_re[b] + p_im[a] * q_im[b]
                z_im = p_im[a] * q_re[b] - p_re[a] * q_im[b]
                weight[k, 3 * x, :, lanes] = z_re
                weight[k, 3 * x + 1, :, lanes] = z_im - z_re
                weight[k, 3 * x + 2, :, lanes] = z_re + z_im
        return 0

    lax.fori_loop(0, directions, weigh, 0, unroll=8)

    def add_samples(step, _):
        lanes = half_lanes(step % 2)
        first = step // 2 * CHUNK
        zero = jnp.zeros((8, LANES), jnp.float32)
        low = component(zero) < 4
        sums = [None] * 12
        for k in range(directions):
            parts = []
            for i in range(CHUNK):
                both = narrow[tile, k, first + i, :, lanes].astype(jnp.float32)
                real, imag = both[:8], both[8:]
                paired[k, first + i, 0, :, lanes] = real
                paired[k, first + i, 1, :, lanes] = imag
                parts.append((real + imag, real, imag))
            for n in range(12):
                w = weight[k, n, :, lanes]
                sums[n] = add_all(sums[n], [w * parts[i][n % 3] for i in range(CHUNK)])
        for i in range(CHUNK):
            one, two, three = ([sums[3 * x + m][i] for x in range(4)] for m in range(3))
            real = fold([one[x] - three[x] for x in range(4)])
            imag = fold([one[x] + two[x] for x in range(4)])
            place = 2 * (first + i)
            model[place, :, lanes] = jnp.where(low, real, turn(imag, 4))
            model[place + 1, :, lanes] = jnp.where(low, turn(real, 4), imag)
        return 0

    lax.fori_loop(0, 2 * pairs // CHUNK, add_samples, 0, unroll=4)


def curvature_kernel(meta, near, far, moments, terms, masks, products):
    tiles = moments.shape[0]
    directions = moments.shape[2] // 8
    for tile in range(tiles):
        masks[tile, 0] = upper_mask(meta, tile)
        for time in range(masks.shape[1] - 1):
            valid = (1 - entry(meta, tile, 4 + time, (8, BASELINES))).astype(jnp.float32)
            masks[tile, 1 + time] = valid * masks[tile, 0]
    for side in range(2):
        found = [station_block(meta, near, far, tile, side) for tile in range(tiles)]
        made = expand([station_products(packed) for packed in found], side == 0)
        for tile in range(tiles):
            for half in range(2):
                lanes = slice(half * LANES, (half + 1) * LANES)
                products[tile, side, half, : made[tile].shape[0]] = made[tile][:, lanes]

    def combine(step, _):
        tile, group = step // (directions // 4), step % (directions // 4)
        mask = masks[tile, 0]
        bits = component(mask[:, :LANES])
        odd = bits & 1 != 0
        upper = bits & 2 != 0
        sign = jnp.where(bits < 4, -1.0, 1.0)
        member = (bits >> 2) * 2 + (bits & 1)
        for half in range(2):
            lanes = slice(half * LANES, (half + 1) * LANES)
            found = [None, None]
            for i in range(4):
                k = 4 * group + i
                rows = pl.ds(pl.multiple_of(8 * k, 8), 8)
                m = [moments[tile, n, rows, lanes] for n in range(4)]
                row = lambda side, n: products[tile, side, half, pl.ds(4 * k + n, 8, stride=0), :]
                h = [row(1, n) for n in range(4)]
                row_sum = m[0] * jnp.where(odd, h[1], h[0])
                row_sum = row_sum + jnp.where(odd, sign * (m[3] * h[3]), m[1] * h[2])
                h = [row(0, n) for n in range(4)]
                col_sum = m[0] * jnp.where(upper, h[1], h[0])
                col_sum = col_sum + m[2] * jnp.where(upper, -sign * h[3], h[2])
                row_sum = row_sum + turn(row_sum, 4)
                row_sum = row_sum + flip(row_sum, 1)
                col_sum = transpose_matrix(col_sum)
                col_sum = col_sum + turn(col_sum, 4)
                col_sum = col_sum + flip(col_sum, 1)
                for side, v in enumerate((row_sum, col_sum)):
                    found[side] = v if i == 0 else jnp.where(member == i, v, found[side])
            for side in range(2):
                place = pl.ds(pl.multiple_of(8 * group, 8), 8)
                terms[side, tile, place, lanes] = mask[:, lanes] * found[side]
        return 0

    lax.fori_loop(0, tiles * directions // 4, combine, 0, unroll=3)


def add_to_owner(meta, near, far, block, rows, part):
    owner = block // 2
    own_core = jnp.where(owner % 2 == meta[0, 0] % 2, 1.0, 0.0)
    near[owner // 2, rows] = near[owner // 2, rows] + own_core * part
    far[owner // 2, rows] = far[owner // 2, rows] + (1.0 - own_core) * part


def gradient_block(sums, half, side):
    part = to_lanes(jnp.split(sums, 4, axis=0), half).reshape(-1, 8, LANES)
    if side == 0:
        part = transpose_matrix(part)
    else:
        part = jnp.where(component(part) < 4, part, -part)
    return part.reshape(-1, LANES)


def add_gradient_terms(
    tile, meta, masks, observed, mine, other, row_jones, col_jones, paired,
    residual_out, terms, residual, turned, semaphore,
):
    directions, pairs = paired.shape[:2]
    first_half = entry(meta, 0, 1) == 0
    for i in range(pairs):
        both = []
        for s in (2 * i, 2 * i + 1):
            summed = mine[s] + other[s]
            weight = masks[tile, 1 + s // FREQ_CHANNELS]
            r = weight * (observed[tile, s].astype(jnp.float32) - summed)
            residual[s] = jnp.where(first_half, r[:, :LANES], r[:, LANES:])
            both.append(r)
        made = [pair_parts(*both)]
        for x in range(1, 4):
            bit = x & -x
            made.append(tuple(flip(v, bit) for v in made[x - bit]))
        for x, (real, imag) in enumerate(made):
            turned[i, 3 * x] = real
            turned[i, 3 * x + 1] = real + imag
            turned[i, 3 * x + 2] = real - imag
    sent = pltpu.make_async_copy(residual, residual_out.at[tile], semaphore)
    sent.start()

    def add_directions(step, _):
        half, lanes = step % 2, half_lanes(step % 2)
        first = step // 2 * CHUNK
        zero = jnp.zeros((8, LANES), jnp.float32)
        sums = [None] * 12
        for p in range(pairs):
            parts = []
            for i in range(CHUNK):
                real = paired[first + i, p, 0, :, lanes]
                imag = paired[first + i, p, 1, :, lanes]
                parts.append((real + imag, real, imag))
            for n in range(12):
                r = turned[p, n, :, lanes]
                sums[n] = add_all(sums[n], [r * parts[i][n % 3] for i in range(CHUNK)])
        bits = component(zero)
        real = bits < 4
        equal = (bits >> 1) & 1 == bits & 1
        for i in range(CHUNK):
            k = first + i
            p_re, p_im = arranged(row_jones, tile, half, k, 2)
            q_re, q_im = arranged(col_jones, tile, half, k, 1)
            row_sum = [None, None]
            col_sum = [None, None]
            for x in range(4):
                a, b = x // 2, x % 2
                y_re = sums[3 * x][i] - sums[3 * x + 2][i]
                y_im = sums[3 * x + 1][i] - sums[3 * x][i]
                y_re = y_re + turn(y_re, 4)
                y_im = y_im + turn(y_im, 4)
                one, two = jnp.where(real, y_re, y_im), jnp.where(real, -y_im, y_re)
                (row_sum[a],) = add_all(row_sum[a : a + 1], [q_re[b] * one + q_im[b] * two])
                (col_sum[b],) = add_all(col_sum[b : b + 1], [p_re[a] * one - p_im[a] * two])
            rows = pl.ds(pl.multiple_of(8 * k, 8), 8)
            g, h = row_sum
            g = jnp.where(equal, g, h) + flip(jnp.where(equal, h, g), 1)
            terms[0, rows, lanes] = g
            g, h = col_sum
            g = jnp.where(equal, g, h) + flip(jnp.where(equal, h, g), 2)
            terms[1, rows, lanes] = g
        return 0

    lax.fori_loop(0, 2 * directions // CHUNK, add_directions, 0, unroll=4)
    return sent


def first_gradient_kernel(
    meta_in_vmem, curvature_terms, masks, observed, mine, other, row_jones, col_jones, paired,
    residual_out, near, far, terms, residual, turned, semaphore, meta, meta_semaphore,
):
    meta_copy = pltpu.make_async_copy(meta_in_vmem, meta, meta_semaphore)
    meta_copy.start()
    sent = add_gradient_terms(
        0, meta_in_vmem, masks, observed, mine, other, row_jones, col_jones, paired,
        residual_out, terms, residual, turned, semaphore,
    )
    near[...] = jnp.zeros_like(near)
    far[...] = jnp.zeros_like(far)
    meta_copy.wait()
    tiles, directions = curvature_terms.shape[1], paired.shape[0]
    rows, few = 8 * directions, 2 * directions
    for side, blocks in enumerate(sides(meta, tiles)):
        stack = [terms[side], *(curvature_terms[side, tile] for tile in range(tiles))]
        sums = station_sums(jnp.concatenate(stack, axis=0), side == 0)
        part = gradient_block(sums[:rows], blocks[0] % 2, side)
        add_to_owner(meta, near, far, blocks[0], slice(0, few), part)
        for tile, block in enumerate(blocks):
            start = rows + tile * few
            groups = jnp.split(sums[start : start + few], directions // 4, axis=0)
            chosen = [groups[n : n + 4] for n in range(0, len(groups), 4)]
            made = [to_lanes(parts, block % 2) for parts in chosen]
            part = jnp.concatenate(made, axis=0)
            add_to_owner(meta, near, far, block, slice(few, None), part)
    sent.wait()


def last_gradient_kernel(
    tiles, meta_in_vmem, near_before, far_before,
    masks, observed, mine, other, row_jones, col_jones, paired,
    residual_before, residual_out, near, far, terms, residual, turned, semaphore,
    meta, meta_semaphore,
):
    del residual_before
    meta_copy = pltpu.make_async_copy(meta_in_vmem, meta, meta_semaphore)
    meta_copy.start()
    near[...] = near_before[...]
    far[...] = far_before[...]
    sent = add_gradient_terms(
        tiles - 1, meta_in_vmem, masks, observed, mine, other, row_jones, col_jones, paired,
        residual_out, terms, residual, turned, semaphore,
    )
    meta_copy.wait()
    for side in range(2):
        block = block_of(meta, tiles - 1, side)
        part = gradient_block(station_sums(terms[side], side == 0), block % 2, side)
        add_to_owner(meta, near, far, block, slice(0, part.shape[0]), part)
    sent.wait()


def finish_kernel(normalizer, parts, gradient, curvature):
    total = sum((parts[x] for x in range(1, parts.shape[0])), parts[0]) * normalizer
    directions = gradient.shape[0]
    rows, each = 2 * directions, directions // 4
    grad = total[:rows].reshape(each, 8, LANES)
    for g in range(4):
        gradient[g * each : (g + 1) * each] = grad[:, :, 2 * SB * g : 2 * SB * (g + 1)]
    for k in range(directions):
        group, member = k // 4, k % 4
        start = rows + group // 4 * 8 + member // 2 * 4 + member % 2
        lane = group % 4 * 2 * SB
        for c in range(2):
            row = total[start + 2 * c : start + 2 * c + 1]
            curvature[k, c : c + 1] = row[:, lane : lane + 2 * SB]


def call(kernel, scalars, arrays, in_hbm, results, scratch=(), to_hbm=(), aliases=None, cost=None):
    place = lambda space: pl.BlockSpec(memory_space=space)
    spaces = [pltpu.SMEM] * len(scalars) + [pltpu.VMEM] * len(arrays) + [pltpu.HBM] * len(in_hbm)
    return pl.pallas_call(
        kernel,
        in_specs=[place(space) for space in spaces],
        out_specs=[place(pltpu.HBM)] * len(to_hbm) + [place(pltpu.VMEM)] * len(results),
        out_shape=[
            *(pltpu.HBM(shape, jnp.float32) for shape in to_hbm),
            *(pltpu.VMEM(getattr(v, "shape", v), getattr(v, "dtype", jnp.float32)) for v in results),
        ],
        scratch_shapes=list(scratch),
        input_output_aliases=aliases or {},
        cost_estimate=cost,
        compiler_params=pltpu.CompilerParams(vmem_limit_bytes=32 * 1024 * 1024),
    )(*scalars, *arrays, *(pltpu.with_memory_space_constraint(v, pltpu.HBM) for v in in_hbm))


def swap_with(value, axis, mask):
    size = lax.axis_size(axis)
    return lax.ppermute(value, axis, [(place, place ^ mask) for place in range(size)])


def trade(slots):
    size = lax.axis_size("tile")
    groups = [list(range(core, size, 2)) for core in range(2)]
    return lax.all_to_all(slots, "tile", 0, 0, axis_index_groups=groups, tiled=True)


def body_kernels(coherency, observed, flags, tile_map, jones):
    tiles, directions, samples = coherency.shape[:3]
    chips = lax.axis_size("tile") // 2
    rows = 2 * directions
    extra = -(-directions // 16) * 8
    place = [
        jnp.full((tiles, 1), lax.axis_index(axis), jnp.int32) for axis in ("tile", "dir")
    ]
    meta = jnp.concatenate([*place, tile_map, flags], axis=1)

    def memory(*shape, kind=jnp.float32):
        return pltpu.VMEM(shape, kind)

    (packed,) = call(
        pack_kernel,
        [],
        [],
        [jones],
        [(chips, rows, LANES)],
        [memory(*jones.shape), pltpu.SemaphoreType.DMA],
    )
    near = trade(packed)
    narrow = (tiles, directions, samples // 2, 16, BASELINES)
    moments, narrow = call(
        moment_kernel,
        [],
        [],
        [flags, coherency],
        [jax.ShapeDtypeStruct(narrow, coherency.dtype)],
        [
            pltpu.SMEM(flags.shape, flags.dtype),
            memory(*coherency.shape, kind=coherency.dtype),
            memory(tiles, 4, 4 * rows, BASELINES),
            pltpu.SemaphoreType.DMA((tiles, PIECES)),
            pltpu.SemaphoreType.DMA,
            pltpu.SemaphoreType.DMA((tiles, PIECES)),
        ],
        [(tiles, 4, 4 * rows, BASELINES)],
        cost=pl.CostEstimate(
            flops=10 * coherency.size, bytes_accessed=4 * coherency.size, transcendentals=0
        ),
    )
    far = swap_with(near, "tile", 1)

    expanded = (tiles, 2, 4 * rows + SPARE_ROWS, LANES)
    of_tile = [(samples, 8, BASELINES), (directions, samples // 2, 2, 8, BASELINES)]
    narrow = pltpu.with_memory_space_constraint(narrow, pltpu.VMEM)
    weight = memory(directions, 12, 8, BASELINES)
    model, row_jones, col_jones, paired = call(
        first_model_kernel,
        [],
        [meta, near, far, narrow],
        [],
        [
            of_tile[0],
            expanded,
            expanded,
            of_tile[1],
        ],
        [weight],
    )
    first = [model, swap_with(model, "dir", 1), row_jones, col_jones, paired]
    model, paired = call(
        functools.partial(next_model_kernel, 1),
        [],
        [narrow, row_jones, col_jones],
        [],
        of_tile,
        [weight],
    )
    last = [model, swap_with(model, "dir", 1), row_jones, col_jones, paired]

    residual_shape = (tiles, samples, 8, LANES)
    terms = (2, 4 * rows, BASELINES)
    scratch = [
        memory(samples, 8, LANES),
        memory(samples // 2, 12, 8, BASELINES),
        pltpu.SemaphoreType.DMA,
    ]
    curvature_terms, masks = call(
        curvature_kernel,
        [],
        [meta, near, far, moments],
        [],
        [(2, tiles, 2 * directions, BASELINES), (tiles, 1 + flags.shape[1], 8, BASELINES)],
        [memory(tiles, 2, 2, 4 * directions + SPARE_ROWS, LANES)],
        cost=pl.CostEstimate(
            flops=coherency.size, bytes_accessed=coherency.size, transcendentals=0
        ),
    )
    scratch = [
        memory(*terms),
        *scratch,
        pltpu.SMEM(meta.shape, meta.dtype),
        pltpu.SemaphoreType.DMA,
    ]
    slots = (chips, rows + extra, LANES)
    residual, near, far = call(
        first_gradient_kernel,
        [],
        [meta, curvature_terms, masks, observed, *first],
        [],
        [slots, slots],
        scratch,
        [residual_shape],
    )
    residual, near, far = call(
        functools.partial(last_gradient_kernel, tiles),
        [],
        [meta, near, far, masks, observed, *last],
        [residual],
        [slots, slots],
        scratch,
        [residual_shape],
        {10: 0},
    )
    parts = trade(near + swap_with(far, "tile", 1))
    directions, _, owned = jones.shape
    in_vmem = pl.BlockSpec(memory_space=pltpu.VMEM)
    gradient, curvature = pl.pallas_call(
        functools.partial(finish_kernel, 1.0 / (samples * SB)),
        in_specs=[in_vmem],
        out_specs=[in_vmem] * 2,
        out_shape=[
            jax.ShapeDtypeStruct(jones.shape, jnp.float32),
            jax.ShapeDtypeStruct((directions, 2, owned), jnp.float32),
        ],
        compiler_params=pltpu.CompilerParams(vmem_limit_bytes=32 * 1024 * 1024),
    )(parts)
    return residual, gradient, curvature


def body(coherency, observed, flags, tile_map, jones):
    jones_all = lax.all_gather(jones, "tile", axis=2, tiled=True)
    how_many = coherency.shape[0]
    predictions = []
    products_list = []
    weight_list = []
    for number in range(how_many):
        predicted, products = tile_terms(
            coherency[number].astype(jnp.float32), jones_all, tile_map[number]
        )
        predictions.append(predicted)
        products_list.append(products)
        weight_list.append(weights(flags[number], tile_map[number]))
    partial_value = jnp.stack(predictions)
    weight = jnp.stack(weight_list)
    columns = observed.shape[3]
    portion = columns // lax.axis_size("dir")
    offset = lax.axis_index("dir") * portion
    summed = lax.psum(partial_value, "dir")
    residual = weight * (observed.astype(jnp.float32) - summed)
    residual_mine = lax.dynamic_slice_in_dim(residual, offset, portion, 3)
    grad_total = jnp.zeros((jones_all.shape[0], 8, jones_all.shape[2]), jnp.float32)
    curv_total = jnp.zeros((jones_all.shape[0], 2, jones_all.shape[2]), jnp.float32)
    for number in range(how_many):
        grad_row, grad_col, curv_row, curv_col = station_terms(
            residual[number], weight[number], products_list[number]
        )
        block_pair = tile_map[number]
        grad_total = add_block(
            add_block(grad_total, grad_row, block_pair[0]), grad_col, block_pair[1]
        )
        curv_total = add_block(
            add_block(curv_total, curv_row, block_pair[0]), curv_col, block_pair[1]
        )
    grad_owned, curv_owned = (
        lax.psum_scatter(grad_total, "tile", scatter_dimension=2, tiled=True),
        lax.psum_scatter(curv_total, "tile", scatter_dimension=2, tiled=True),
    )
    normalizer = 1.0 / (observed.shape[1] * SB)
    return (residual_mine, grad_owned * normalizer, curv_owned * normalizer)


def solution(mesh):
    specs = dict(
        mesh=mesh,
        in_specs=(
            P("tile", "dir", None, None, None),
            P("tile", None, None, None),
            P("tile", None),
            P("tile", None),
            P("dir", None, "tile"),
        ),
        out_specs=(P("tile", None, None, "dir"), P("dir", None, "tile"), P("dir", None, "tile")),
        check_vma=False,
    )

    def run(coherency, observed, flags, tile_map, jones):
        owned = jones.shape[2] // mesh.shape["tile"]
        directions = jones.shape[0] // mesh.shape["dir"]
        fits = owned == 2 * SB and directions == 24
        paired = mesh.shape["dir"] == 2 and mesh.shape["tile"] == 16
        paired = paired and coherency.shape[0] == 2 * mesh.shape["tile"]
        chosen = body_kernels if fits and paired else body
        return jax.shard_map(chosen, **specs)(coherency, observed, flags, tile_map, jones)

    return run
```

```python
import functools

import jax
import jax.numpy as jnp
from jax import lax
from jax.experimental import pallas as pl
from jax.experimental.pallas import tpu as pltpu
from jax.sharding import PartitionSpec as P

SB = 16
FREQ_CHANNELS = 4
LANES = 128
BASELINES = SB * SB
CHUNK = 3


def split_parts(values):
    shape = values.shape[:-2] + (2, 2, values.shape[-1])
    return (values[..., 0:4, :].reshape(shape), values[..., 4:8, :].reshape(shape))


def join_parts(re_part, im_part):
    shape = re_part.shape[:-3] + (4, re_part.shape[-1])
    return jnp.concatenate([re_part.reshape(shape), im_part.reshape(shape)], axis=-2)


def complex_product(left_re, left_im, right_re, right_im):
    lre = left_re[..., :, :, None, :]
    lim = left_im[..., :, :, None, :]
    rre = right_re[..., None, :, :, :]
    rim = right_im[..., None, :, :, :]
    return (jnp.sum(lre * rre - lim * rim, axis=-3), jnp.sum(lre * rim + lim * rre, axis=-3))


def adjoint(re_part, im_part):
    return (jnp.swapaxes(re_part, -3, -2), -jnp.swapaxes(im_part, -3, -2))


def weights(row_flag_mask, block_pair):
    valid_samples = jnp.repeat((1 - row_flag_mask).astype(jnp.float32), FREQ_CHANNELS)
    baseline = jnp.arange(SB * SB, dtype=jnp.int32)
    inner_row = baseline // SB
    inner_col = baseline % SB
    upper_triangle_pairs = jnp.where(
        (block_pair[0] < block_pair[1]) | (inner_row < inner_col), 1.0, 0.0
    ).astype(jnp.float32)
    return valid_samples[:, None, None] * upper_triangle_pairs[None, None, :]


def tile_terms(coher, jones_all, block_pair):
    row_gain_matrix = lax.dynamic_slice_in_dim(jones_all, block_pair[0] * SB, SB, 2)
    col_jones = lax.dynamic_slice_in_dim(jones_all, block_pair[1] * SB, SB, 2)
    first_antenna = jnp.repeat(row_gain_matrix, SB, axis=2)[:, None]
    station_q = jnp.tile(col_jones, (1, 1, SB))[:, None]
    coh_re, coh_im = split_parts(coher)
    p_re, p_im = split_parts(first_antenna)
    q_re, q_im = split_parts(station_q)
    qh_re, qh_im = adjoint(q_re, q_im)
    m_re, m_im = complex_product(coh_re, coh_im, qh_re, qh_im)
    n_re, n_im = complex_product(p_re, p_im, coh_re, coh_im)
    v_re, v_im = complex_product(p_re, p_im, m_re, m_im)
    predicted = jnp.sum(join_parts(v_re, v_im), axis=0)
    return (predicted, (m_re, m_im, n_re, n_im))


def station_terms(residual, weight, products):
    m_re, m_im, n_re, n_im = products
    r_re, r_im = split_parts(residual)
    mh_re, mh_im = adjoint(m_re, m_im)
    g_re, g_im = complex_product(r_re, r_im, mh_re, mh_im)
    row_side = jnp.sum(join_parts(g_re, g_im), axis=1)
    rh_re, rh_im = adjoint(r_re, r_im)
    f_re, f_im = complex_product(rh_re, rh_im, n_re, n_im)
    col_side = jnp.sum(join_parts(f_re, f_im), axis=1)
    row_curv = jnp.sum(jnp.sum(m_re * m_re + m_im * m_im, axis=-2) * weight[None], axis=1)
    column_curvature = jnp.sum(jnp.sum(n_re * n_re + n_im * n_im, axis=-3) * weight[None], axis=1)
    lead = row_side.shape[0]
    grad_row = jnp.sum(row_side.reshape(lead, 8, SB, SB), axis=3)
    grad_col = jnp.sum(col_side.reshape(lead, 8, SB, SB), axis=2)
    curv_row = jnp.sum(row_curv.reshape(lead, 2, SB, SB), axis=3)
    curv_col = jnp.sum(column_curvature.reshape(lead, 2, SB, SB), axis=2)
    return (grad_row, grad_col, curv_row, curv_col)


def add_block(total, piece, block):
    offset = block * SB
    current = lax.dynamic_slice_in_dim(total, offset, SB, 2)
    return lax.dynamic_update_slice_in_dim(total, current + piece, offset, 2)


def component(value):
    return lax.broadcasted_iota(jnp.int32, value.shape, value.ndim - 2)


def turn(value, ahead):
    return pltpu.roll(value, (8 - ahead) % 8, value.ndim - 2)


def flip(value, mask):
    if mask == 4:
        return turn(value, 4)
    return jnp.where(component(value) & mask == 0, turn(value, mask), turn(value, 8 - mask))


def transpose_matrix(value):
    place = component(value) & 3
    return jnp.where(place == 1, turn(value, 1), jnp.where(place == 2, turn(value, 7), value))


def fold(values):
    values = [values[x] + flip(values[x + 1], 1) for x in range(0, 4, 2)]
    return values[0] + flip(values[1], 2)


def pair_parts(first, second):
    low = component(first) < 4
    return jnp.where(low, first, turn(second, 4)), jnp.where(low, turn(first, 4), second)


def add_all(sums, values):
    if sums is None:
        return values
    return [v if total is None else total + v for total, v in zip(sums, values)]


def halves(value):
    high = value.astype(jnp.bfloat16)
    return high, (value - high.astype(jnp.float32)).astype(jnp.bfloat16)


def station_of(baseline, row_side):
    return baseline // SB if row_side else baseline % SB


def one_hot(row_side, transposed):
    shape = (BASELINES, LANES) if transposed else (LANES, BASELINES)
    lane = lax.broadcasted_iota(jnp.int32, shape, 1 if transposed else 0)
    baseline = lax.broadcasted_iota(jnp.int32, shape, 0 if transposed else 1)
    return (lane == station_of(baseline, row_side)).astype(jnp.bfloat16)


def expand(blocks, row_side):
    made = []
    for packed in blocks:
        made.extend([packed] + [pltpu.roll(packed, LANES - 2 * SB * g, 1) for g in range(1, 4)])
    high, low = halves(jnp.concatenate(made, axis=0))
    both = jnp.concatenate([high, low], axis=1)
    chosen = jnp.concatenate([one_hot(row_side, False)] * 2, axis=0)
    wide = jnp.dot(both, chosen, preferred_element_type=jnp.float32)
    ends = [0]
    for packed in blocks:
        ends.append(ends[-1] + 4 * packed.shape[0])
    return [wide[start:end] for start, end in zip(ends, ends[1:])]


def station_sums(values, row_side):
    high, low = halves(values)
    both = jnp.concatenate([high, low], axis=0)
    total = jnp.dot(both, one_hot(row_side, True), preferred_element_type=jnp.float32)
    count = high.shape[0]
    return total[:count] + total[count:]


def to_lanes(parts, half):
    moved = [pltpu.roll(part, 2 * SB * g + SB * half, 1) for g, part in enumerate(parts)]
    return sum(moved[1:], moved[0])


def arranged(ref, tile, half, k, mask):
    row = lambda c: ref[tile, half, pl.ds(8 * k + c, 8, stride=0), :]
    first = lax.broadcasted_iota(jnp.int32, (8, LANES), 0) & mask == 0
    pick = lambda c, d: jnp.where(first, row(c), row(d))
    return (pick(0, 3), pick(2, 1)), (pick(4, 7), pick(6, 5))


def half_lanes(index):
    return pl.ds(pl.multiple_of(index * LANES, LANES), LANES)


def upper_mask(meta, tile):
    shape = (8, BASELINES)
    baseline = lax.broadcasted_iota(jnp.int32, shape, 1)
    above = entry(meta, tile, 2, shape) < entry(meta, tile, 3, shape)
    return jnp.where((baseline // SB < baseline % SB) | above, 1.0, 0.0).astype(jnp.float32)


def pack_kernel(jones_in_hbm, packed, jones, semaphore):
    copy = pltpu.make_async_copy(jones_in_hbm, jones, semaphore)
    copy.start()
    copy.wait()
    each = jones.shape[0] // 4
    rows = packed.shape[1]
    made = jnp.concatenate(
        [jones[g * each : (g + 1) * each].reshape(rows, 2 * SB) for g in range(4)], axis=1
    )
    for copy in range(packed.shape[0]):
        packed[copy] = made


def entry(meta, row, column, shape=(8, LANES)):
    return jnp.broadcast_to(meta[row : row + 1, column : column + 1], shape)


def station_block(meta, near, far, tile, side):
    block = entry(meta, tile, 2 + side)
    owner = block >> 1
    own_core = (owner ^ entry(meta, 0, 0)) & 1 == 0
    chips, rows = near.shape[:2]
    found = None
    for chip in range(chips):
        packed = jnp.where(own_core, near[chip].reshape(-1, 8, LANES), far[chip].reshape(-1, 8, LANES))
        found = packed if found is None else jnp.where(owner >> 1 == chip, packed, found)
    shifted = pltpu.roll(found.reshape(rows, LANES), LANES - SB, 1).reshape(found.shape)
    return jnp.where(block & 1 == 0, found, shifted).reshape(rows, LANES)


PIECES = 6
SPARE_ROWS = 8


def block_of(meta, tile, side):
    return meta[tile, 2 + side]


def valid_of(flags, tile, sample):
    return (1 - flags[tile, sample // FREQ_CHANNELS]).astype(jnp.float32)


def sides(meta, tiles):
    return [[block_of(meta, tile, side) for tile in range(tiles)] for side in range(2)]


def pieces(source, target, semaphores):
    each = source.shape[0] // PIECES
    parts = [pl.ds(n * each, each) for n in range(PIECES)]
    return [
        pltpu.make_async_copy(source.at[part], target.at[part], semaphores.at[n])
        for n, part in enumerate(parts)
    ]


def moment_kernel(
    flags_in_hbm, source, moments_out, pairs,
    flags, coherency, moments, semaphores, flag_semaphore, out_semaphores,
):
    tiles, directions, samples = source.shape[:3]
    each = directions // PIECES
    flag_copy = pltpu.make_async_copy(flags_in_hbm, flags, flag_semaphore)
    flag_copy.start()
    copies = [pieces(source.at[t], coherency.at[t], semaphores.at[t]) for t in range(tiles)]
    for copy in sum(copies, []):
        copy.start()
    flag_copy.wait()
    sent = []
    for tile in range(tiles):

        def add_direction(k, _):
            rows = pl.ds(pl.multiple_of(8 * k, 8), 8)
            for half in range(2):
                lanes = slice(half * LANES, (half + 1) * LANES)
                sums = [jnp.zeros((8, LANES), jnp.float32)] * 4
                for s in range(samples):
                    c = coherency[tile, k, s, :, lanes].astype(jnp.float32)
                    weighted = valid_of(flags, tile, s) * c
                    sums = [v + weighted * (turn(c, n) if n else c) for n, v in enumerate(sums)]
                    if s % 2 == 1:
                        both = jnp.concatenate(pair_parts(before, c), axis=0)
                        pairs[tile, k, s // 2, :, lanes] = both.astype(pairs.dtype)
                    before = c
                for n in range(4):
                    moments[tile, n, rows, lanes] = sums[n]
            return 0

        for n, copy in enumerate(copies[tile]):
            copy.wait()
            lax.fori_loop(n * each, (n + 1) * each, add_direction, 0, unroll=2)
            rows = pl.ds(8 * n * each, 8 * each)
            sent.append(
                pltpu.make_async_copy(
                    moments.at[tile, :, rows],
                    moments_out.at[tile, :, rows],
                    out_semaphores.at[tile, n],
                )
            )
            sent[-1].start()
    for copy in sent:
        copy.wait()


def station_products(packed):
    e = packed.reshape(-1, 8, LANES)
    bits = component(e)
    part = bits >= 4
    second = bits & 1 != 0
    spread = lambda v: (lambda u: u + flip(u, 2))(v + flip(v, 4))
    across = flip(e, 1)
    squares = spread(e * e)
    cross_re = 2.0 * spread(e * across)
    sign = jnp.where(part == second, 1.0, -1.0)
    cross_im = 2.0 * spread(sign * (e * flip(across, 4)))
    made = jnp.where(bits & 2 == 0, squares, jnp.where(second, cross_im, cross_re))
    low = component(made[0]) < 4
    joined = [jnp.where(low, made[n], made[n + 1]) for n in range(0, made.shape[0], 2)]
    return jnp.concatenate(joined, axis=0)


def first_model_kernel(meta, near, far, narrow, model, row_jones, col_jones, paired, weight):
    tiles = narrow.shape[0]
    for side, jones in enumerate((row_jones, col_jones)):
        found = [station_block(meta, near, far, tile, side) for tile in range(tiles)]
        for tile, made in enumerate(expand(found, side == 0)):
            for half in range(2):
                lanes = slice(half * LANES, (half + 1) * LANES)
                jones[tile, half, : made.shape[0]] = made[:, lanes]
    models(0, narrow, row_jones, col_jones, model, paired, weight)


def next_model_kernel(tile, narrow, row_jones, col_jones, model, paired, weight):
    models(tile, narrow, row_jones, col_jones, model, paired, weight)


def models(tile, narrow, row_jones, col_jones, model, paired, weight):
    directions, pairs = paired.shape[:2]

    def weigh(k, _):
        for half in range(2):
            lanes = slice(half * LANES, (half + 1) * LANES)
            p_re, p_im = arranged(row_jones, tile, half, k, 2)
            q_re, q_im = arranged(col_jones, tile, half, k, 1)
            for x in range(4):
                a, b = x // 2, x % 2
                z_re = p_re[a] * q_re[b] + p_im[a] * q_im[b]
                z_im = p_im[a] * q_re[b] - p_re[a] * q_im[b]
                weight[k, 3 * x, :, lanes] = z_re
                weight[k, 3 * x + 1, :, lanes] = z_im - z_re
                weight[k, 3 * x + 2, :, lanes] = z_re + z_im
        return 0

    lax.fori_loop(0, directions, weigh, 0, unroll=8)

    def add_samples(step, _):
        lanes = half_lanes(step % 2)
        first = step // 2 * CHUNK
        zero = jnp.zeros((8, LANES), jnp.float32)
        low = component(zero) < 4
        sums = [None] * 12
        for k in range(directions):
            parts = []
            for i in range(CHUNK):
                both = narrow[tile, k, first + i, :, lanes].astype(jnp.float32)
                real, imag = both[:8], both[8:]
                paired[k, first + i, 0, :, lanes] = real
                paired[k, first + i, 1, :, lanes] = imag
                parts.append((real + imag, real, imag))
            for n in range(12):
                w = weight[k, n, :, lanes]
                sums[n] = add_all(sums[n], [w * parts[i][n % 3] for i in range(CHUNK)])
        for i in range(CHUNK):
            one, two, three = ([sums[3 * x + m][i] for x in range(4)] for m in range(3))
            real = fold([one[x] - three[x] for x in range(4)])
            imag = fold([one[x] + two[x] for x in range(4)])
            place = 2 * (first + i)
            model[place, :, lanes] = jnp.where(low, real, turn(imag, 4))
            model[place + 1, :, lanes] = jnp.where(low, turn(real, 4), imag)
        return 0

    lax.fori_loop(0, 2 * pairs // CHUNK, add_samples, 0, unroll=4)


def curvature_kernel(meta, near, far, moments, terms, masks, products):
    tiles = moments.shape[0]
    directions = moments.shape[2] // 8
    for tile in range(tiles):
        masks[tile, 0] = upper_mask(meta, tile)
        for time in range(masks.shape[1] - 1):
            valid = (1 - entry(meta, tile, 4 + time, (8, BASELINES))).astype(jnp.float32)
            masks[tile, 1 + time] = valid * masks[tile, 0]
    for side in range(2):
        found = [station_block(meta, near, far, tile, side) for tile in range(tiles)]
        made = expand([station_products(packed) for packed in found], side == 0)
        for tile in range(tiles):
            for half in range(2):
                lanes = slice(half * LANES, (half + 1) * LANES)
                products[tile, side, half, : made[tile].shape[0]] = made[tile][:, lanes]

    def combine(step, _):
        tile, group = step // (directions // 4), step % (directions // 4)
        mask = masks[tile, 0]
        bits = component(mask[:, :LANES])
        odd = bits & 1 != 0
        upper = bits & 2 != 0
        sign = jnp.where(bits < 4, -1.0, 1.0)
        member = (bits >> 2) * 2 + (bits & 1)
        for half in range(2):
            lanes = slice(half * LANES, (half + 1) * LANES)
            found = [None, None]
            for i in range(4):
                k = 4 * group + i
                rows = pl.ds(pl.multiple_of(8 * k, 8), 8)
                m = [moments[tile, n, rows, lanes] for n in range(4)]
                row = lambda side, n: products[tile, side, half, pl.ds(4 * k + n, 8, stride=0), :]
                h = [row(1, n) for n in range(4)]
                row_sum = m[0] * jnp.where(odd, h[1], h[0])
                row_sum = row_sum + jnp.where(odd, sign * (m[3] * h[3]), m[1] * h[2])
                h = [row(0, n) for n in range(4)]
                col_sum = m[0] * jnp.where(upper, h[1], h[0])
                col_sum = col_sum + m[2] * jnp.where(upper, -sign * h[3], h[2])
                row_sum = row_sum + turn(row_sum, 4)
                row_sum = row_sum + flip(row_sum, 1)
                col_sum = transpose_matrix(col_sum)
                col_sum = col_sum + turn(col_sum, 4)
                col_sum = col_sum + flip(col_sum, 1)
                for side, v in enumerate((row_sum, col_sum)):
                    found[side] = v if i == 0 else jnp.where(member == i, v, found[side])
            for side in range(2):
                place = pl.ds(pl.multiple_of(8 * group, 8), 8)
                terms[side, tile, place, lanes] = mask[:, lanes] * found[side]
        return 0

    lax.fori_loop(0, tiles * directions // 4, combine, 0, unroll=3)


def add_to_owner(meta, near, far, block, rows, part):
    owner = block // 2
    own_core = jnp.where(owner % 2 == meta[0, 0] % 2, 1.0, 0.0)
    near[owner // 2, rows] = near[owner // 2, rows] + own_core * part
    far[owner // 2, rows] = far[owner // 2, rows] + (1.0 - own_core) * part


def gradient_block(sums, half, side):
    part = to_lanes(jnp.split(sums, 4, axis=0), half).reshape(-1, 8, LANES)
    if side == 0:
        part = transpose_matrix(part)
    else:
        part = jnp.where(component(part) < 4, part, -part)
    return part.reshape(-1, LANES)


def add_gradient_terms(
    tile, meta, masks, observed, mine, other, row_jones, col_jones, paired,
    residual_out, terms, residual, turned, semaphore,
):
    directions, pairs = paired.shape[:2]
    first_half = entry(meta, 0, 1) == 0
    for i in range(pairs):
        both = []
        for s in (2 * i, 2 * i + 1):
            summed = mine[s] + other[s]
            weight = masks[tile, 1 + s // FREQ_CHANNELS]
            r = weight * (observed[tile, s].astype(jnp.float32) - summed)
            residual[s] = jnp.where(first_half, r[:, :LANES], r[:, LANES:])
            both.append(r)
        made = [pair_parts(*both)]
        for x in range(1, 4):
            bit = x & -x
            made.append(tuple(flip(v, bit) for v in made[x - bit]))
        for x, (real, imag) in enumerate(made):
            turned[i, 3 * x] = real
            turned[i, 3 * x + 1] = real + imag
            turned[i, 3 * x + 2] = real - imag
    sent = pltpu.make_async_copy(residual, residual_out.at[tile], semaphore)
    sent.start()

    def add_directions(step, _):
        half, lanes = step % 2, half_lanes(step % 2)
        first = step // 2 * CHUNK
        zero = jnp.zeros((8, LANES), jnp.float32)
        sums = [None] * 12
        for p in range(pairs):
            parts = []
            for i in range(CHUNK):
                real = paired[first + i, p, 0, :, lanes]
                imag = paired[first + i, p, 1, :, lanes]
                parts.append((real + imag, real, imag))
            for n in range(12):
                r = turned[p, n, :, lanes]
                sums[n] = add_all(sums[n], [r * parts[i][n % 3] for i in range(CHUNK)])
        bits = component(zero)
        real = bits < 4
        equal = (bits >> 1) & 1 == bits & 1
        for i in range(CHUNK):
            k = first + i
            p_re, p_im = arranged(row_jones, tile, half, k, 2)
            q_re, q_im = arranged(col_jones, tile, half, k, 1)
            row_sum = [None, None]
            col_sum = [None, None]
            for x in range(4):
                a, b = x // 2, x % 2
                y_re = sums[3 * x][i] - sums[3 * x + 2][i]
                y_im = sums[3 * x + 1][i] - sums[3 * x][i]
                y_re = y_re + turn(y_re, 4)
                y_im = y_im + turn(y_im, 4)
                one, two = jnp.where(real, y_re, y_im), jnp.where(real, -y_im, y_re)
                (row_sum[a],) = add_all(row_sum[a : a + 1], [q_re[b] * one + q_im[b] * two])
                (col_sum[b],) = add_all(col_sum[b : b + 1], [p_re[a] * one - p_im[a] * two])
            rows = pl.ds(pl.multiple_of(8 * k, 8), 8)
            g, h = row_sum
            g = jnp.where(equal, g, h) + flip(jnp.where(equal, h, g), 1)
            terms[0, rows, lanes] = g
            g, h = col_sum
            g = jnp.where(equal, g, h) + flip(jnp.where(equal, h, g), 2)
            terms[1, rows, lanes] = g
        return 0

    lax.fori_loop(0, 2 * directions // CHUNK, add_directions, 0, unroll=4)
    return sent


def first_gradient_kernel(
    meta_in_vmem, curvature_terms, masks, observed, mine, other, row_jones, col_jones, paired,
    residual_out, near, far, terms, residual, turned, semaphore, meta, meta_semaphore,
):
    meta_copy = pltpu.make_async_copy(meta_in_vmem, meta, meta_semaphore)
    meta_copy.start()
    sent = add_gradient_terms(
        0, meta_in_vmem, masks, observed, mine, other, row_jones, col_jones, paired,
        residual_out, terms, residual, turned, semaphore,
    )
    near[...] = jnp.zeros_like(near)
    far[...] = jnp.zeros_like(far)
    meta_copy.wait()
    tiles, directions = curvature_terms.shape[1], paired.shape[0]
    rows, few = 8 * directions, 2 * directions
    for side, blocks in enumerate(sides(meta, tiles)):
        stack = [terms[side], *(curvature_terms[side, tile] for tile in range(tiles))]
        sums = station_sums(jnp.concatenate(stack, axis=0), side == 0)
        part = gradient_block(sums[:rows], blocks[0] % 2, side)
        add_to_owner(meta, near, far, blocks[0], slice(0, few), part)
        for tile, block in enumerate(blocks):
            start = rows + tile * few
            groups = jnp.split(sums[start : start + few], directions // 4, axis=0)
            chosen = [groups[n : n + 4] for n in range(0, len(groups), 4)]
            made = [to_lanes(parts, block % 2) for parts in chosen]
            part = jnp.concatenate(made, axis=0)
            add_to_owner(meta, near, far, block, slice(few, None), part)
    sent.wait()


def last_gradient_kernel(
    tiles, meta_in_vmem, near_before, far_before,
    masks, observed, mine, other, row_jones, col_jones, paired,
    residual_before, residual_out, near, far, terms, residual, turned, semaphore,
    meta, meta_semaphore,
):
    del residual_before
    meta_copy = pltpu.make_async_copy(meta_in_vmem, meta, meta_semaphore)
    meta_copy.start()
    near[...] = near_before[...]
    far[...] = far_before[...]
    sent = add_gradient_terms(
        tiles - 1, meta_in_vmem, masks, observed, mine, other, row_jones, col_jones, paired,
        residual_out, terms, residual, turned, semaphore,
    )
    meta_copy.wait()
    for side in range(2):
        block = block_of(meta, tiles - 1, side)
        part = gradient_block(station_sums(terms[side], side == 0), block % 2, side)
        add_to_owner(meta, near, far, block, slice(0, part.shape[0]), part)
    sent.wait()


def finish_kernel(normalizer, parts, gradient, curvature):
    total = sum((parts[x] for x in range(1, parts.shape[0])), parts[0]) * normalizer
    directions = gradient.shape[0]
    rows, each = 2 * directions, directions // 4
    grad = total[:rows].reshape(each, 8, LANES)
    for g in range(4):
        gradient[g * each : (g + 1) * each] = grad[:, :, 2 * SB * g : 2 * SB * (g + 1)]
    for k in range(directions):
        group, member = k // 4, k % 4
        start = rows + group // 4 * 8 + member // 2 * 4 + member % 2
        lane = group % 4 * 2 * SB
        for c in range(2):
            row = total[start + 2 * c : start + 2 * c + 1]
            curvature[k, c : c + 1] = row[:, lane : lane + 2 * SB]


def call(kernel, scalars, arrays, in_hbm, results, scratch=(), to_hbm=(), aliases=None, cost=None):
    place = lambda space: pl.BlockSpec(memory_space=space)
    spaces = [pltpu.SMEM] * len(scalars) + [pltpu.VMEM] * len(arrays) + [pltpu.HBM] * len(in_hbm)
    return pl.pallas_call(
        kernel,
        in_specs=[place(space) for space in spaces],
        out_specs=[place(pltpu.HBM)] * len(to_hbm) + [place(pltpu.VMEM)] * len(results),
        out_shape=[
            *(pltpu.HBM(shape, jnp.float32) for shape in to_hbm),
            *(pltpu.VMEM(getattr(v, "shape", v), getattr(v, "dtype", jnp.float32)) for v in results),
        ],
        scratch_shapes=list(scratch),
        input_output_aliases=aliases or {},
        cost_estimate=cost,
        compiler_params=pltpu.CompilerParams(vmem_limit_bytes=32 * 1024 * 1024),
    )(*scalars, *arrays, *(pltpu.with_memory_space_constraint(v, pltpu.HBM) for v in in_hbm))


def swap_with(value, axis, mask):
    size = lax.axis_size(axis)
    return lax.ppermute(value, axis, [(place, place ^ mask) for place in range(size)])


def trade(slots):
    size = lax.axis_size("tile")
    groups = [list(range(core, size, 2)) for core in range(2)]
    return lax.all_to_all(slots, "tile", 0, 0, axis_index_groups=groups, tiled=True)


def body_kernels(coherency, observed, flags, tile_map, jones):
    tiles, directions, samples = coherency.shape[:3]
    chips = lax.axis_size("tile") // 2
    rows = 2 * directions
    extra = -(-directions // 16) * 8
    place = [
        jnp.full((tiles, 1), lax.axis_index(axis), jnp.int32) for axis in ("tile", "dir")
    ]
    meta = jnp.concatenate([*place, tile_map, flags], axis=1)

    def memory(*shape, kind=jnp.float32):
        return pltpu.VMEM(shape, kind)

    (packed,) = call(
        pack_kernel,
        [],
        [],
        [jones],
        [(chips, rows, LANES)],
        [memory(*jones.shape), pltpu.SemaphoreType.DMA],
    )
    near = trade(packed)
    narrow = (tiles, directions, samples // 2, 16, BASELINES)
    moments, narrow = call(
        moment_kernel,
        [],
        [],
        [flags, coherency],
        [jax.ShapeDtypeStruct(narrow, coherency.dtype)],
        [
            pltpu.SMEM(flags.shape, flags.dtype),
            memory(*coherency.shape, kind=coherency.dtype),
            memory(tiles, 4, 4 * rows, BASELINES),
            pltpu.SemaphoreType.DMA((tiles, PIECES)),
            pltpu.SemaphoreType.DMA,
            pltpu.SemaphoreType.DMA((tiles, PIECES)),
        ],
        [(tiles, 4, 4 * rows, BASELINES)],
        cost=pl.CostEstimate(
            flops=10 * coherency.size, bytes_accessed=4 * coherency.size, transcendentals=0
        ),
    )
    far = swap_with(near, "tile", 1)

    expanded = (tiles, 2, 4 * rows + SPARE_ROWS, LANES)
    of_tile = [(samples, 8, BASELINES), (directions, samples // 2, 2, 8, BASELINES)]
    narrow = pltpu.with_memory_space_constraint(narrow, pltpu.VMEM)
    weight = memory(directions, 12, 8, BASELINES)
    model, row_jones, col_jones, paired = call(
        first_model_kernel,
        [],
        [meta, near, far, narrow],
        [],
        [
            of_tile[0],
            expanded,
            expanded,
            of_tile[1],
        ],
        [weight],
    )
    first = [model, swap_with(model, "dir", 1), row_jones, col_jones, paired]
    model, paired = call(
        functools.partial(next_model_kernel, 1),
        [],
        [narrow, row_jones, col_jones],
        [],
        of_tile,
        [weight],
    )
    last = [model, swap_with(model, "dir", 1), row_jones, col_jones, paired]

    residual_shape = (tiles, samples, 8, LANES)
    terms = (2, 4 * rows, BASELINES)
    scratch = [
        memory(samples, 8, LANES),
        memory(samples // 2, 12, 8, BASELINES),
        pltpu.SemaphoreType.DMA,
    ]
    curvature_terms, masks = call(
        curvature_kernel,
        [],
        [meta, near, far, moments],
        [],
        [(2, tiles, 2 * directions, BASELINES), (tiles, 1 + flags.shape[1], 8, BASELINES)],
        [memory(tiles, 2, 2, 4 * directions + SPARE_ROWS, LANES)],
        cost=pl.CostEstimate(
            flops=coherency.size, bytes_accessed=coherency.size, transcendentals=0
        ),
    )
    scratch = [
        memory(*terms),
        *scratch,
        pltpu.SMEM(meta.shape, meta.dtype),
        pltpu.SemaphoreType.DMA,
    ]
    slots = (chips, rows + extra, LANES)
    residual, near, far = call(
        first_gradient_kernel,
        [],
        [meta, curvature_terms, masks, observed, *first],
        [],
        [slots, slots],
        scratch,
        [residual_shape],
    )
    residual, near, far = call(
        functools.partial(last_gradient_kernel, tiles),
        [],
        [meta, near, far, masks, observed, *last],
        [residual],
        [slots, slots],
        scratch,
        [residual_shape],
        {10: 0},
    )
    parts = trade(near + swap_with(far, "tile", 1))
    directions, _, owned = jones.shape
    in_vmem = pl.BlockSpec(memory_space=pltpu.VMEM)
    gradient, curvature = pl.pallas_call(
        functools.partial(finish_kernel, 1.0 / (samples * SB)),
        in_specs=[in_vmem],
        out_specs=[in_vmem] * 2,
        out_shape=[
            jax.ShapeDtypeStruct(jones.shape, jnp.float32),
            jax.ShapeDtypeStruct((directions, 2, owned), jnp.float32),
        ],
        compiler_params=pltpu.CompilerParams(vmem_limit_bytes=32 * 1024 * 1024),
    )(parts)
    return residual, gradient, curvature


def body(coherency, observed, flags, tile_map, jones):
    jones_all = lax.all_gather(jones, "tile", axis=2, tiled=True)
    how_many = coherency.shape[0]
    predictions = []
    products_list = []
    weight_list = []
    for number in range(how_many):
        predicted, products = tile_terms(
            coherency[number].astype(jnp.float32), jones_all, tile_map[number]
        )
        predictions.append(predicted)
        products_list.append(products)
        weight_list.append(weights(flags[number], tile_map[number]))
    partial_value = jnp.stack(predictions)
    weight = jnp.stack(weight_list)
    columns = observed.shape[3]
    portion = columns // lax.axis_size("dir")
    offset = lax.axis_index("dir") * portion
    summed = lax.psum(partial_value, "dir")
    residual = weight * (observed.astype(jnp.float32) - summed)
    residual_mine = lax.dynamic_slice_in_dim(residual, offset, portion, 3)
    grad_total = jnp.zeros((jones_all.shape[0], 8, jones_all.shape[2]), jnp.float32)
    curv_total = jnp.zeros((jones_all.shape[0], 2, jones_all.shape[2]), jnp.float32)
    for number in range(how_many):
        grad_row, grad_col, curv_row, curv_col = station_terms(
            residual[number], weight[number], products_list[number]
        )
        block_pair = tile_map[number]
        grad_total = add_block(
            add_block(grad_total, grad_row, block_pair[0]), grad_col, block_pair[1]
        )
        curv_total = add_block(
            add_block(curv_total, curv_row, block_pair[0]), curv_col, block_pair[1]
        )
    grad_owned, curv_owned = (
        lax.psum_scatter(grad_total, "tile", scatter_dimension=2, tiled=True),
        lax.psum_scatter(curv_total, "tile", scatter_dimension=2, tiled=True),
    )
    normalizer = 1.0 / (observed.shape[1] * SB)
    return (residual_mine, grad_owned * normalizer, curv_owned * normalizer)


def solution(mesh):
    specs = dict(
        mesh=mesh,
        in_specs=(
            P("tile", "dir", None, None, None),
            P("tile", None, None, None),
            P("tile", None),
            P("tile", None),
            P("dir", None, "tile"),
        ),
        out_specs=(P("tile", None, None, "dir"), P("dir", None, "tile"), P("dir", None, "tile")),
        check_vma=False,
    )

    def run(coherency, observed, flags, tile_map, jones):
        owned = jones.shape[2] // mesh.shape["tile"]
        directions = jones.shape[0] // mesh.shape["dir"]
        fits = owned == 2 * SB and directions == 24
        paired = mesh.shape["dir"] == 2 and mesh.shape["tile"] == 16
        paired = paired and coherency.shape[0] == 2 * mesh.shape["tile"]
        chosen = body_kernels if fits and paired else body
        return jax.shard_map(chosen, **specs)(coherency, observed, flags, tile_map, jones)

    return run
```
